32 devices in a mesh: dp: 8 (over y, x, core), seq: 4 (over z).
Axes of the slice: x: 2, y: 2, z: 4, core: 2. Of those that a mesh axis runs over, the one named last changes fastest.
Arguments:
- tokens: bfloat16 [22528, 512], P(('dp', 'seq')), may hold values from -6 to 6
- cotangent: bfloat16 [22528, 512], P(('dp', 'seq')), may hold values from -6 to 6
- w_qkv: bfloat16 [512, 1536], P(('dp', 'seq')), may hold values from -0.25 to 0.25
- w_out: bfloat16 [512, 512], P(('dp', 'seq')), may hold values from -1 to 1
- w_up: bfloat16 [512, 2048], P('dp', 'seq'), may hold values from -0.25 to 0.25
- w_down: bfloat16 [2048, 512], P('seq', 'dp'), may hold values from -0.125 to 0.125
- norm1_gain: bfloat16 [512], P(('dp', 'seq')), may hold values from 0.5 to 1.5
- norm1_shift: bfloat16 [512], P(('dp', 'seq')), may hold values from -3 to 3
- norm2_gain: bfloat16 [512], P(('dp', 'seq')), may hold values from 0.5 to 1.5
- norm2_shift: bfloat16 [512], P(('dp', 'seq')), may hold values from -3 to 3
- clip_steps: int32 [8, 3], P('dp'), may hold values from 76 to 192, as said below
- window_shifts: int32 [8, 3, 2], P('dp'), may hold values from 1 to 3
Outputs:
- output: bfloat16 [22528, 512], P(('dp', 'seq'))
- tokens_grad: bfloat16 [22528, 512], P(('dp', 'seq'))
- w_qkv_grad: float32 [512, 1536], P(('dp', 'seq'))
- w_out_grad: float32 [512, 512], P(('dp', 'seq'))
- w_up_grad: float32 [512, 2048], P('dp', 'seq')
- w_down_grad: float32 [2048, 512], P('seq', 'dp')
- norm1_gain_grad: float32 [512], P(('dp', 'seq'))
- norm1_shift_grad: float32 [512], P(('dp', 'seq'))
- norm2_gain_grad: float32 [512], P(('dp', 'seq'))
- norm2_shift_grad: float32 [512], P(('dp', 'seq'))
The draws below stay inside these ranges and needn't reach their ends.
Inputs may be any that keep to these rules, and one draw needn't show every extreme that they name: `clip_steps`: A group's row is a leading clip, a clip of 192 time steps, and a trailing clip; the middle clip starts on the group's first device along seq and ends on its last; the leading and trailing lengths are multiples of 4, and every row sums to 352. `window_shifts`: shifts of empty slots are not used.
All inputs are finite; a program needn't handle non-finite values.
Results may differ from the reference program's by a relative error of at most 0.013.
Values may be sent and summed in bfloat16 or wider, within the bound.
No kernel may reach another device: no remote copies, remote signals or barrier semaphores. Data moves between devices by JAX's collectives and lax.ppermute only.
A program may use at most 128 MiB of HBM per device.

```python
import jax
import jax.numpy as jnp
from jax import lax

D = 512
HEADS = 16
FF = 2048
FREQ = 8
LONG = 192
SLOTS = 3
STEPS_DEV = 88
HEAD_DIM = 32
TOKENS = 22528
N_DP = 8
N_SEQ = 4


def draw_clip_steps(key, part):
    key = jax.random.fold_in(key, 11)
    group_steps = N_SEQ * STEPS_DEV
    lead_least = max(0, (N_SEQ - 1) * STEPS_DEV - LONG + 4)
    lead_most = min(STEPS_DEV - 4, group_steps - LONG)
    option_count = (lead_most - lead_least) // 4 + 1
    picks = jax.random.randint(key, (N_DP, 1), 0, option_count).astype(jnp.int32)
    picks = picks.at[0, 0].set(0).at[1, 0].set(option_count - 1)
    leading = lead_least + 4 * picks
    middle_clip = jnp.full((N_DP, 1), LONG, jnp.int32)
    trailing = group_steps - LONG - leading
    return jnp.concatenate((leading, middle_clip, trailing), axis=1).astype(jnp.int32)


def place_ends(result, own_key, smallest, high):
    longest = result.shape.index(max(result.shape))
    spots = []
    for shift in (0, 1):
        where = [jax.random.randint(jax.random.fold_in(own_key, axis), (), 0, length) for axis, length in enumerate(result.shape)]
        where[longest] = (where[longest] + shift) % result.shape[longest]
        spots.append(tuple(where))
    return result.at[spots[0]].set(smallest).at[spots[1]].set(high)


def raised(values, stream_key, source, target, blocks, factor):
    owner, partner = [(jnp.arange(values.shape[position]) // (values.shape[position] // blocks)).reshape([-1 if axis == position else 1 for axis in range(values.ndim)]) for position in (source, target)]
    chosen = jax.random.permutation(stream_key, blocks)[partner]
    strong = (owner == chosen) | (owner == (partner + blocks // 2) % blocks)
    return jnp.where(strong, factor * values, values)


def level_of(rng, dims, cuts, smallest, high):
    factor_of, own = 1.0, jax.random.fold_in(rng, 6)
    for axis_at, blocks in cuts:
        heights = jnp.exp(jax.random.uniform(jax.random.fold_in(own, axis_at), (blocks,), jnp.float32, smallest / len(cuts), high / len(cuts)))
        factor_of = factor_of * jnp.repeat(heights, dims[axis_at] // blocks).reshape([-1 if axis == axis_at else 1 for axis in range(len(dims))])
    return factor_of


def centred(own_key, shape, width, most, shards=(), kind=jnp.bfloat16):
    entries = width * jax.random.normal(own_key, shape, jnp.float32)
    if shards:
        entries = entries * level_of(own_key, shape, shards, -0.22, 0.18)
    return jnp.clip(entries, -most, most).astype(kind)


def gaussian_with(stream_key, shape, deviation, limit, shards, heavy, kind=jnp.bfloat16):
    values = deviation * jax.random.normal(stream_key, shape, jnp.float32)
    if shards:
        values = values * level_of(stream_key, shape, shards, -0.22, 0.18)
    return jnp.clip(raised(values, jax.random.fold_in(stream_key, 3), *heavy), -limit, limit).astype(kind)


def setup_inputs(seed: int = 0) -> dict:
    key_list = jax.random.split(jax.random.key(seed), 13)
    return {
        "tokens": gaussian_with(key_list[0], (TOKENS, D), 1.0, 6.0, ((0, 32),), (0, 1, 32, 2.75)),
        "cotangent": gaussian_with(key_list[1], (TOKENS, D), 1.0, 6.0, ((0, 32),), (0, 1, 32, 2.75)),
        "w_qkv": centred(key_list[2], (D, 3 * D), D ** -0.5, 0.25, ((0, 32),)),
        "w_out": centred(key_list[3], (D, D), (D // 16) ** -0.5, 1.0, ((0, 32),)),
        "w_up": centred(key_list[4], (D, FF), D ** -0.5, 0.25, ((0, 8), (1, 4))),
        "w_down": centred(key_list[5], (FF, D), FF ** -0.5, 0.125, ((0, 4), (1, 8))),
        "norm1_gain": jnp.clip(0.5 + 1.0 * jax.random.uniform(key_list[6], (D,), jnp.float32) ** level_of(key_list[6], (D,), ((0, 32),), -0.2, 0.2), 0.5, 1.5).astype(jnp.bfloat16),
        "norm1_shift": centred(key_list[7], (D,), 0.5, 3.0, ((0, 32),)),
        "norm2_gain": jnp.clip(0.5 + 1.0 * jax.random.uniform(key_list[8], (D,), jnp.float32) ** level_of(key_list[8], (D,), ((0, 32),), -0.2, 0.2), 0.5, 1.5).astype(jnp.bfloat16),
        "norm2_shift": centred(key_list[9], (D,), 0.5, 3.0, ((0, 32),)),
        "clip_steps": draw_clip_steps(jax.random.fold_in(key_list[12], 71), 0),
        "window_shifts": place_ends(jax.random.randint(key_list[11], (N_DP, SLOTS, 2), 1, 4), jax.random.fold_in(key_list[11], 1), 1, 3).astype(jnp.int32),
    }


epsilon = 1e-06

@jax.custom_vjp
def low(v):
    return lax.optimization_barrier(v.astype(jnp.bfloat16)).astype(jnp.float32)

@jax.custom_vjp
def low_back(v):
    return v

def low_keep(v):
    return (low(v), None)

def low_pass(kept, grad):
    return (grad,)

def back_keep(v):
    return (v, None)

def back_low(kept, grad):
    return (low(grad),)
low.defvjp(low_keep, low_pass)
low_back.defvjp(back_keep, back_low)

def layer_norm(rows_in, gain, shift):
    row_mean = lax.optimization_barrier(jnp.mean(rows_in, axis=-1, keepdims=True))
    centered = rows_in - row_mean
    variance = lax.optimization_barrier(jnp.mean(centered * centered, axis=-1, keepdims=True))
    return centered * lax.rsqrt(variance + epsilon) * gain + shift

def window_ids(step_index, freq_index, steps_row, shifts_row):
    clip_ends = jnp.cumsum(steps_row).astype(jnp.int32)
    clip_starts = (clip_ends - steps_row).astype(jnp.int32)
    inside = (step_index[:, None] >= clip_starts[None, :]) & (step_index[:, None] < clip_ends[None, :])
    member = inside.astype(jnp.int32)
    slot_index = jnp.arange(steps_row.shape[0], dtype=jnp.int32)
    clip_slot = lax.optimization_barrier(jnp.sum(member * slot_index[None, :], axis=1)).astype(jnp.int32)
    clip_start = lax.optimization_barrier(jnp.sum(member * clip_starts[None, :], axis=1)).astype(jnp.int32)
    shift_time = lax.optimization_barrier(jnp.sum(member * shifts_row[None, :, 0], axis=1)).astype(jnp.int32)
    shift_freq = lax.optimization_barrier(jnp.sum(member * shifts_row[None, :, 1], axis=1)).astype(jnp.int32)
    is_valid = lax.optimization_barrier(jnp.sum(member, axis=1)) > 0
    time_group = (step_index - clip_start + 4 - shift_time) // 4
    freq_group = (freq_index + 4 - shift_freq) // 4
    window_key = (clip_slot * 65536 + time_group * 4 + freq_group).astype(jnp.int32)
    return (jnp.where(is_valid, window_key, -1).astype(jnp.int32), is_valid)

def block_views(array, blocks, span, rows):
    parts = [array[view_index * span:view_index * span + rows].reshape((blocks, span) + array.shape[1:]) for view_index in range(3)]
    return jnp.concatenate(parts, axis=1)

def layer_group(rows_in, steps_row, shifts_row, w_qkv, w_out, w_up, w_down, gain_one, shift_one, gain_two, shift_two):
    highest = lax.Precision.HIGHEST
    rows = rows_in.shape[0]
    span = 4 * FREQ
    blocks = rows // span
    row_index = jnp.arange(rows, dtype=jnp.int32)
    query_key, unused = window_ids(row_index // FREQ, row_index % FREQ, steps_row, shifts_row)
    ext_index = jnp.arange(rows + 8 * FREQ, dtype=jnp.int32)
    ext_key, ext_valid = window_ids(ext_index // FREQ - 3, ext_index % FREQ, steps_row, shifts_row)
    query_blocks_key = query_key.reshape(blocks, span)
    key_blocks_key = block_views(ext_key, blocks, span, rows)
    key_blocks_valid = block_views(ext_valid, blocks, span, rows)
    allowed = (query_blocks_key[:, :, None] == key_blocks_key[:, None, :]) & key_blocks_valid[:, None, :]
    normed = low(layer_norm(rows_in, gain_one, shift_one))
    qkv = jnp.dot(normed, w_qkv, precision=highest)
    queries = low(low_back(qkv[:, :D]))
    key_rows = low(low_back(qkv[:, D:2 * D]))
    value_rows = low(low_back(qkv[:, 2 * D:]))
    key_ext = jnp.pad(key_rows, ((3 * FREQ, 5 * FREQ), (0, 0)))
    value_ext = jnp.pad(value_rows, ((3 * FREQ, 5 * FREQ), (0, 0)))
    query_blocks = queries.reshape(blocks, span, HEADS, HEAD_DIM)
    key_blocks = block_views(key_ext, blocks, span, rows).reshape(blocks, 3 * span, HEADS, HEAD_DIM)
    value_blocks = block_views(value_ext, blocks, span, rows).reshape(blocks, 3 * span, HEADS, HEAD_DIM)
    raw = jnp.einsum('bqhd,bkhd->bhqk', query_blocks, key_blocks, precision=highest)
    scores = jnp.where(allowed[:, None], low_back(raw) * HEAD_DIM ** (-0.5), -1e+30)
    probs = jax.nn.softmax(scores, axis=-1)
    mixed = jnp.einsum('bhqk,bkhd->bqhd', low(probs), value_blocks, precision=highest).reshape(rows, D)
    mixed = low(low_back(mixed))
    branch = low_back(jnp.dot(mixed, w_out, precision=highest))
    middle = rows_in + branch
    normed_two = low(layer_norm(middle, gain_two, shift_two))
    hidden_pre = low_back(jnp.dot(normed_two, w_up, precision=highest))
    hidden = low(jax.nn.gelu(hidden_pre, approximate=False))
    return middle + jnp.dot(hidden, w_down, precision=highest)

def reference(tokens, cotangent, w_qkv, w_out, w_up, w_down, norm1_gain, norm1_shift, norm2_gain, norm2_shift, clip_steps, window_shifts):
    group_step = jax.checkpoint(layer_group)

    def forward(tokens_f, w_qkv_f, w_out_f, w_up_f, w_down_f, gain_one, shift_one, gain_two, shift_two):
        grouped = tokens_f.reshape(N_DP, TOKENS // N_DP, D)

        def scan_step(carry, inputs):
            rows_in, steps_row, shifts_row = inputs
            return (carry, group_step(rows_in, steps_row, shifts_row, w_qkv_f, w_out_f, w_up_f, w_down_f, gain_one, shift_one, gain_two, shift_two))
        unused, outputs = lax.scan(scan_step, jnp.zeros((), jnp.float32), (grouped, clip_steps, window_shifts))
        return outputs.reshape(TOKENS, D)
    floats = tuple((array.astype(jnp.float32) for array in (tokens, w_qkv, w_out, w_up, w_down, norm1_gain, norm1_shift, norm2_gain, norm2_shift)))
    output, pullback = jax.vjp(forward, *floats)
    grads = pullback(cotangent.astype(jnp.float32))
    return (output.astype(jnp.bfloat16), grads[0].astype(jnp.bfloat16), grads[1], grads[2], grads[3], grads[4], grads[5], grads[6], grads[7], grads[8])
```

```python
import functools

import jax
import jax.numpy as jnp
from jax import lax
from jax.experimental import pallas as pl
from jax.experimental.pallas import tpu as pltpu
from jax.sharding import PartitionSpec as P

D = 512
HEADS = 16
HEAD_DIM = D // HEADS
FF = 2048
FREQ = 8
STEPS_DEV = 88
HALO = 4 * FREQ
ROWS = STEPS_DEV * FREQ
WIN = 4 * FREQ
WINDOWS = STEPS_DEV // 4 + 2
WROWS = WINDOWS * WIN
TILE = 256
QUAD = 128
NORMS = 128
CHUNK = 512
CHUNKS = FF // CHUNK
epsilon = 1e-06
F32 = jnp.float32
BF16 = jnp.bfloat16


def mm(left, right):
    return jnp.dot(left, right, preferred_element_type=F32)


def mm_right(left, right):
    return lax.dot_general(left, right, (((1,), (1,)), ((), ())), preferred_element_type=F32)


def mm_left(left, right):
    return lax.dot_general(left, right, (((0,), (0,)), ((), ())), preferred_element_type=F32)


def window_place(info, w):
    lead, mid, trail = info[0], info[1], info[2]
    seq = info[10]
    base = seq * STEPS_DEV
    n_lead = lead // 4 + 1
    n_mid = mid // 4 + 1
    index = jnp.where(seq == 0, 0, base // 4 + 1) + w
    in_mid = index >= n_lead
    in_trail = index >= n_lead + n_mid
    before = jnp.where(in_trail, n_lead + n_mid, jnp.where(in_mid, n_lead, 0))
    start = jnp.where(in_trail, lead + mid, jnp.where(in_mid, lead, 0))
    steps = jnp.where(in_trail, trail, jnp.where(in_mid, mid, lead))
    shift_time = jnp.where(in_trail, info[7], jnp.where(in_mid, info[5], info[3]))
    shift_freq = jnp.where(in_trail, info[8], jnp.where(in_mid, info[6], info[4]))
    first = start - 4 + shift_time + 4 * (index - before)
    here = first < base + STEPS_DEV
    low = jnp.clip(start - first, 0, 4)
    high = jnp.where(here, jnp.clip(start + steps - first, 0, 4), 0)
    own_low = jnp.clip(base - first, 0, 4)
    own_high = jnp.clip(base + STEPS_DEV - first, 0, 4)
    row = jnp.clip(first - base + 4, 0, STEPS_DEV + 4) * FREQ
    row = pl.multiple_of(row, FREQ)
    return (
        row,
        low * FREQ,
        high * FREQ,
        jnp.maximum(low, own_low) * FREQ,
        jnp.minimum(high, own_high) * FREQ,
        shift_freq,
    )


def row_mask(low, high):
    index = lax.broadcasted_iota(jnp.int32, (WIN, 1), 0)
    return (index >= low) & (index < high)


def pad_rows(ext, left, rows, right):
    ext[0:HALO] = left[...].astype(F32)
    ext[HALO : HALO + ROWS] = rows[...].astype(F32)
    ext[HALO + ROWS :] = right[...].astype(F32)


def normalized(values):
    mean = jnp.mean(values, axis=-1, keepdims=True)
    centered = values - mean
    variance = jnp.mean(centered * centered, axis=-1, keepdims=True)
    scale = lax.rsqrt(variance + epsilon)
    return centered * scale, scale


def norm_back(grad, unit, scale):
    mean_one = jnp.mean(grad, axis=-1, keepdims=True)
    mean_two = jnp.mean(grad * unit, axis=-1, keepdims=True)
    return scale * (grad - mean_one - unit * mean_two)


def head_masks():
    lane = lax.broadcasted_iota(jnp.int32, (1, QUAD), 1) // HEAD_DIM
    return [(lane == h).astype(BF16) for h in range(QUAD // HEAD_DIM)]


def spread(block, masks):
    return jnp.concatenate([block * mask for mask in masks], axis=0)


def gathered(product, lane):
    parts = [product[h * WIN : (h + 1) * WIN] for h in range(QUAD // HEAD_DIM)]
    return jnp.where(
        lane < 1, parts[0], jnp.where(lane < 2, parts[1], jnp.where(lane < 3, parts[2], parts[3]))
    )


def place_blocks(info, pieces, order, scratch, rows, first=0):
    for piece, partner in zip(pieces, order):
        for k in range(piece.shape[0]):
            owner = (info[9] ^ partner) * piece.shape[0] + (info[10] ^ k)
            at = pl.multiple_of(owner * rows, rows)
            scratch[pl.ds(at, rows), :] = piece[k, first : first + rows, :]


def attention_kernel(direct, info, left, rows, right, *refs):
    pieces, refs = (refs[:8], refs[8:]) if direct else (refs[:1], refs[1:])
    x_out, qkv_out, mixed_out, probs_out, w_out, norms_out, ext, normed = refs
    if direct:
        place_blocks(info, pieces, ORDER, w_out, pieces[0].shape[1])
    else:
        w_out[...] = pieces[0][...]
    norms_out[...] = jnp.transpose(w_out[:, 3 * D :].astype(F32))[:8]
    gain, shift = norms_out[0:1], norms_out[1:2]
    pad_rows(ext, left, rows, right)

    def place(w, carry):
        row, low, high, _, _, _ = window_place(info, w)
        values = jnp.where(row_mask(low, high), ext[pl.ds(row, WIN), :], 0.0)
        at = pl.ds(pl.multiple_of(w * WIN, WIN), WIN)
        x_out[at, :] = values
        unit, _ = normalized(values)
        normed[at, :] = (unit * gain + shift).astype(BF16)
        return carry

    lax.fori_loop(0, WINDOWS, place, 0)

    def project(i, carry):
        at = pl.ds(pl.multiple_of(i * TILE, TILE), TILE)
        for part in range(3):
            cols = slice(part * D, (part + 1) * D)
            qkv_out[at, cols] = mm(normed[at, :], w_out[:, cols]).astype(BF16)
        return carry

    lax.fori_loop(0, WROWS // TILE, project, 0)
    masks = head_masks()
    lane = lax.broadcasted_iota(jnp.int32, (1, QUAD), 1) // HEAD_DIM
    key_row = lax.broadcasted_iota(jnp.int32, (WIN, QUAD), 0)
    query_row = lax.broadcasted_iota(jnp.int32, (WIN, QUAD), 1) % WIN
    key_freq, query_freq = key_row % FREQ, query_row % FREQ

    def attend(w, carry):
        _, low, high, _, _, shift_freq = window_place(info, w)
        at = pl.ds(pl.multiple_of(w * WIN, WIN), WIN)
        key_group = (key_freq + 4 - shift_freq) >> 2
        query_group = (query_freq + 4 - shift_freq) >> 2
        allowed = (key_group == query_group) & (key_row >= low) & (key_row < high)
        for quad in range(D // QUAD):
            cols = slice(quad * QUAD, (quad + 1) * QUAD)
            query = qkv_out[at, cols]
            key = qkv_out[at, D + quad * QUAD : D + (quad + 1) * QUAD]
            value = qkv_out[at, 2 * D + quad * QUAD : 2 * D + (quad + 1) * QUAD]
            raw = mm_right(key, spread(query, masks))
            scores = jnp.where(allowed, raw * HEAD_DIM**-0.5, -1e30)
            weights = jnp.exp(scores - jnp.max(scores, axis=0, keepdims=True))
            probs = weights / jnp.sum(weights, axis=0, keepdims=True)
            probs_out[at, cols] = probs
            mixed = gathered(mm_left(probs.astype(BF16), value), lane)
            mixed_out[at, cols] = mixed.astype(BF16)
        return carry

    lax.fori_loop(0, WINDOWS, attend, 0)


def gelu_parts(values):
    half_exp = jnp.exp(-0.5 * values * values)
    t = 1.0 / (1.0 + (0.3275911 * 0.7071067811865476) * jnp.abs(values))
    poly = t * (
        0.5 * 0.254829592
        + t
        * (
            0.5 * -0.284496736
            + t * (0.5 * 1.421413741 + t * (0.5 * -1.453152027 + t * (0.5 * 1.061405429)))
        )
    )
    tail = poly * half_exp
    return jnp.where(values >= 0, 1.0 - tail, tail), half_exp * 0.3989422804014327


def feed_kernel(direct, info, left, rows, right, x_in, mixed_in, norms, *refs):
    pieces, refs = (refs[:8], refs[8:]) if direct else (refs[:3], refs[3:])
    out, grad_middle, grad_mixed, grad_norms = refs[:4]
    if direct:
        (keep, send), refs = refs[4:6], refs[6:]
    else:
        (grad_up_out, grad_down_out, grad_w_out), refs = refs[4:7], refs[7:]
    up, down, w_out, ext, cot, cot_own, own, middle, total, normed, normed_own, hidden, pre, grad = refs
    if direct:
        count = pieces[0].shape[0]
        block = D // 8
        for piece, partner in zip(pieces, ORDER):
            dp = info[9] ^ partner
            at = pl.multiple_of(dp * block, block)
            for k in range(count):
                up[k, pl.ds(at, block), :] = piece[k, 0:block, :]
                down[k, pl.ds(at, block), :] = piece[k, block : 2 * block, :]
                row = pl.multiple_of((dp * count + (info[10] ^ k)) * 16, 16)
                w_out[pl.ds(row, 16), :] = piece[k, 2 * block :, :]
    else:
        up[...] = pieces[0][...]
        down[...] = pieces[1][...]
        w_out[...] = pieces[2][...]
    pad_rows(ext, left, rows, right)

    def place(w, carry):
        row, low, high, own_low, own_high, _ = window_place(info, w)
        values = ext[pl.ds(row, WIN), :]
        at = pl.ds(pl.multiple_of(w * WIN, WIN), WIN)
        cot[at, :] = jnp.where(row_mask(low, high), values, 0.0).astype(BF16)
        cot_own[at, :] = jnp.where(row_mask(own_low, own_high), values, 0.0).astype(BF16)
        own[at, :] = jnp.where(row_mask(own_low, own_high), jnp.ones((WIN, QUAD), F32), 0.0)
        return carry

    lax.fori_loop(0, WINDOWS, place, 0)
    gain, shift = norms[2:3], norms[3:4]

    def tile_of(i):
        return pl.ds(pl.multiple_of(i * TILE, TILE), TILE)

    def before(i, carry):
        at = tile_of(i)
        values = x_in[at, :] + mm(mixed_in[at, :], w_out[...])
        middle[at, :] = values
        total[at, :] = values
        unit, _ = normalized(values)
        low = unit * gain + shift
        normed[at, :] = low.astype(BF16)
        normed_own[at, :] = (low * own[at, 0:1]).astype(BF16)
        grad[at, :] = jnp.zeros((TILE, D), F32)
        return carry

    lax.fori_loop(0, WROWS // TILE, before, 0)

    def chunk_step(c, carry):
        up_c, down_c = up[c], down[c]

        def row_step(i, inner):
            at = tile_of(i)
            values = mm(normed[at, :], up_c)
            grad_hidden = mm(cot[at, :], down_c)
            below, density = gelu_parts(values)
            hidden_low = (values * below).astype(BF16)
            grad_low = (grad_hidden * (below + values * density)).astype(BF16)
            hidden[at, :] = hidden_low
            pre[at, :] = grad_low
            total[at, :] += mm_right(hidden_low, down_c)
            grad[at, :] += mm_right(grad_low, up_c)
            return inner

        lax.fori_loop(0, WROWS // TILE, row_step, 0)
        return carry

    for c in range(CHUNKS):
        chunk_step(c, 0)
        grad_up = mm_left(normed_own[...], pre[...])
        grad_down = mm_left(cot_own[...], hidden[...])
        if direct:
            ext[0:D, :] = grad_up
            for partner in range(8):
                target = send if partner & 1 else keep
                row = pl.multiple_of((info[9] ^ partner) * block, block)
                target[partner >> 1, c, 0:block, :] = ext[pl.ds(row, block), :].astype(BF16)
            ext[0:D, :] = grad_down
            for partner in range(8):
                target = send if partner & 1 else keep
                row = pl.multiple_of((info[9] ^ partner) * block, block)
                target[partner >> 1, c, block : 2 * block, :] = ext[pl.ds(row, block), :].astype(
                    BF16
                )
        else:
            grad_up_out[c] = grad_up
            grad_down_out[c] = grad_down
    grad_norms[...] = jnp.zeros(grad_norms.shape, F32)

    def after(i, carry):
        at = tile_of(i)
        unit, scale = normalized(middle[at, :])
        part = grad[at, :]
        masked = part * own[at, 0:1]
        grad_norms[0:1] += jnp.sum(masked * unit, axis=0, keepdims=True)
        grad_norms[1:2] += jnp.sum(masked, axis=0, keepdims=True)
        result = cot[at, :].astype(F32) + norm_back(part * gain, unit, scale)
        grad_middle[at, :] = result
        low = result.astype(BF16)
        grad_mixed[at, :] = mm_right(low, w_out[...]).astype(BF16)
        normed_own[at, :] = (result * own[at, 0:1]).astype(BF16)
        return carry

    lax.fori_loop(0, WROWS // TILE, after, 0)
    grad_out = mm_left(mixed_in[...], normed_own[...])
    if direct:
        ext[0:D, :] = grad_out
        for partner in range(8):
            target = send if partner & 1 else keep
            for k in range(count):
                row = pl.multiple_of(((info[9] ^ partner) * count + (info[10] ^ k)) * 16, 16)
                target[partner >> 1, k, 2 * block :, :] = ext[pl.ds(row, 16), :].astype(BF16)
    else:
        grad_w_out[...] = grad_out
    unplace(info, total, ext, out)


def unplace(info, values, ext, out):
    def back(w, carry):
        row, low, high, _, _, _ = window_place(info, w)
        at = pl.ds(pl.multiple_of(w * WIN, WIN), WIN)
        place = pl.ds(row, WIN)
        ext[place, :] = jnp.where(row_mask(low, high), values[at, :], ext[place, :])
        return carry

    lax.fori_loop(0, WINDOWS, back, 0)
    out[...] = ext[HALO : HALO + ROWS].astype(BF16)


def back_kernel(
    direct, info, x_in, qkv, probs_in, grad_mixed, grad_middle, w_qkv, norms, grad_norms, *refs
):
    out, refs = refs[0], refs[1:]
    if direct:
        (keep, send), refs = refs[:2], refs[2:]
    else:
        w_grad, refs = refs[0], refs[1:]
    ext, normed, grad_qkv, result, gains, grad_w = refs
    masks = head_masks()
    lane = lax.broadcasted_iota(jnp.int32, (1, QUAD), 1) // HEAD_DIM

    def attend_back(w, carry):
        at = pl.ds(pl.multiple_of(w * WIN, WIN), WIN)
        for quad in range(D // QUAD):
            cols = slice(quad * QUAD, (quad + 1) * QUAD)
            cols_key = slice(D + quad * QUAD, D + (quad + 1) * QUAD)
            cols_value = slice(2 * D + quad * QUAD, 2 * D + (quad + 1) * QUAD)
            query = spread(qkv[at, cols], masks)
            key = qkv[at, cols_key]
            value = qkv[at, cols_value]
            grad_out = spread(grad_mixed[at, cols], masks)
            probs = probs_in[at, cols]
            grad_probs = mm_right(value, grad_out)
            delta = jnp.sum(probs * grad_probs, axis=0, keepdims=True)
            grad_scores = (probs * (grad_probs - delta) * HEAD_DIM**-0.5).astype(BF16)
            grad_qkv[at, cols] = gathered(mm_left(grad_scores, key), lane).astype(BF16)
            grad_qkv[at, cols_key] = mm(grad_scores, query).astype(BF16)
            grad_qkv[at, cols_value] = mm(probs.astype(BF16), grad_out).astype(BF16)
        return carry

    lax.fori_loop(0, WINDOWS, attend_back, 0)
    gain, shift = norms[0:1], norms[1:2]
    gains[...] = jnp.zeros(gains.shape, F32)
    index = lax.broadcasted_iota(jnp.int32, (WIN, 1), 0)

    def mask_step(w, carry):
        _, _, _, own_low, own_high, _ = window_place(info, w)
        at = pl.ds(pl.multiple_of(w * WIN, WIN), WIN)
        own = ((index >= own_low) & (index < own_high)).astype(F32)
        unit, scale = normalized(x_in[at, :])
        normed[at, :] = ((unit * gain + shift) * own).astype(BF16)
        part = mm_right(grad_qkv[at, :], w_qkv[:, : 3 * D])
        masked = part * own
        gains[0:1] += jnp.sum(masked * unit, axis=0, keepdims=True)
        gains[1:2] += jnp.sum(masked, axis=0, keepdims=True)
        result[at, :] = grad_middle[at, :] + norm_back(part * gain, unit, scale)
        return carry

    lax.fori_loop(0, WINDOWS, mask_step, 0)
    gains[2:4] = grad_norms[0:2]
    for part in range(3):
        cols = slice(part * D, (part + 1) * D)
        grad_w[:, cols] = mm_left(normed[...], grad_qkv[:, cols])
    grad_w[:, 3 * D :] = jnp.transpose(gains[...])
    if direct:
        count = keep.shape[1]
        for partner in range(8):
            target = send if partner & 1 else keep
            for k in range(count):
                row = pl.multiple_of(((info[9] ^ partner) * count + (info[10] ^ k)) * 16, 16)
                target[partner >> 1, k] = grad_w[pl.ds(row, 16), :].astype(BF16)
    else:
        w_grad[...] = grad_w[...]
    unplace(info, result, ext, out)


ORDER = (0, 2, 4, 6, 1, 3, 5, 7)
SMEM = pl.BlockSpec(memory_space=pltpu.SMEM)
VMEM = pl.BlockSpec(memory_space=pltpu.VMEM)


def run_kernel(body, out_shape, scratch, flops, *operands):
    moved = sum(a.size * a.dtype.itemsize for a in (*operands, *out_shape))
    return pl.pallas_call(
        body,
        out_shape=out_shape,
        in_specs=[SMEM] + [VMEM] * (len(operands) - 1),
        out_specs=[VMEM] * len(out_shape),
        scratch_shapes=scratch,
        cost_estimate=pl.CostEstimate(
            flops=flops, bytes_accessed=moved, transcendentals=flops // 1024
        ),
        compiler_params=pltpu.CompilerParams(vmem_limit_bytes=50 * 1024 * 1024),
    )(*operands)


def swap(array, axis, bit):
    return lax.ppermute(array, axis, [(i, i ^ bit) for i in range(lax.axis_size(axis))])


def spread_out(shard):
    column = jnp.stack([shard] + [swap(shard, "seq", k) for k in range(1, lax.axis_size("seq"))])
    plane = [column] + [swap(column, "dp", partner) for partner in (2, 4, 6)]
    return plane + [swap(piece, "dp", 1) for piece in plane]


def collect(keep, send):
    pair = keep.astype(F32) + swap(send, "dp", 1).astype(F32)
    low = pair.astype(BF16)
    parts = [swap(low[m], "dp", 2 * m) for m in (1, 2, 3)]
    column = pair[0] + sum(part.astype(F32) for part in parts)
    low = column.astype(BF16)
    parts = [swap(low[k], "seq", k) for k in range(1, column.shape[0])]
    return column[0] + sum(part.astype(F32) for part in parts)


def shape(dims, kind):
    return jax.ShapeDtypeStruct(dims, kind)


def per_device(
    tokens,
    cotangent,
    w_qkv,
    w_out,
    w_up,
    w_down,
    norm1_gain,
    norm1_shift,
    norm2_gain,
    norm2_shift,
    clip_steps,
    window_shifts,
):
    n_dp, n_seq = lax.axis_size("dp"), lax.axis_size("seq")
    share = w_qkv.shape[0]
    direct = n_dp == 8 and share % 16 == 0
    info = jnp.concatenate(
        [
            clip_steps.reshape(3),
            window_shifts.reshape(6),
            lax.axis_index("dp").reshape(1).astype(jnp.int32),
            lax.axis_index("seq").reshape(1).astype(jnp.int32),
        ]
    )
    norms = jnp.stack([norm1_gain, norm1_shift, norm2_gain, norm2_shift], axis=1)
    first = jnp.concatenate([w_qkv, jnp.pad(norms, ((0, 0), (0, NORMS - 4)))], axis=1)
    width = first.shape[1]
    if direct:
        second = jnp.concatenate([w_up, w_down.T, w_out], axis=0)
        first_all = spread_out(first)
        second_all = spread_out(second)
    else:
        first_all = [lax.all_gather(first, ("dp", "seq"), axis=0, tiled=True)]
        up_all = lax.all_gather(lax.all_gather(w_up, "dp", axis=0, tiled=True), "seq", axis=0)
        down_all = lax.all_gather(lax.all_gather(w_down.T, "dp", axis=0, tiled=True), "seq", axis=0)
        second_all = [up_all, down_all, lax.all_gather(w_out, ("dp", "seq"), axis=0, tiled=True)]
    both = jnp.stack([tokens, cotangent])
    right_way = [(i, i + 1) for i in range(n_seq - 1)]
    left_way = [(i + 1, i) for i in range(n_seq - 1)]
    left = lax.ppermute(both[:, ROWS - HALO :], "seq", right_way)
    right = lax.ppermute(both[:, :HALO], "seq", left_way)

    x, qkv, mixed, probs, w_qkv_all, norms_all = run_kernel(
        functools.partial(attention_kernel, direct),
        [
            shape((WROWS, D), F32),
            shape((WROWS, 3 * D), BF16),
            shape((WROWS, D), BF16),
            shape((WROWS, D), F32),
            shape((D, width), BF16),
            shape((8, D), F32),
        ],
        [pltpu.VMEM((ROWS + 2 * HALO, D), F32), pltpu.VMEM((WROWS, D), BF16)],
        2 * WROWS * D * 3 * D * 2,
        info,
        left[0],
        tokens,
        right[0],
        *first_all,
    )
    if direct:
        block = (4, n_seq, 2 * (D // 8) + 16, CHUNK)
        grads_shape = [shape(block, BF16)] * 2
    else:
        grads_shape = [shape((CHUNKS, D, CHUNK), F32)] * 2 + [shape((D, D), F32)]
    out, grad_middle, grad_mixed, grad_norms, *grads = run_kernel(
        functools.partial(feed_kernel, direct),
        [
            shape((ROWS, D), BF16),
            shape((WROWS, D), F32),
            shape((WROWS, D), BF16),
            shape((8, D), F32),
            *grads_shape,
        ],
        [
            pltpu.VMEM((CHUNKS, D, CHUNK), BF16),
            pltpu.VMEM((CHUNKS, D, CHUNK), BF16),
            pltpu.VMEM((D, D), BF16),
            pltpu.VMEM((ROWS + 2 * HALO, D), F32),
            pltpu.VMEM((WROWS, D), BF16),
            pltpu.VMEM((WROWS, D), BF16),
            pltpu.VMEM((WROWS, QUAD), F32),
            pltpu.VMEM((WROWS, D), F32),
            pltpu.VMEM((WROWS, D), F32),
            pltpu.VMEM((WROWS, D), BF16),
            pltpu.VMEM((WROWS, D), BF16),
            pltpu.VMEM((WROWS, CHUNK), BF16),
            pltpu.VMEM((WROWS, CHUNK), BF16),
            pltpu.VMEM((WROWS, D), F32),
        ],
        2 * WROWS * D * (6 * FF + 3 * D),
        info,
        left[1],
        cotangent,
        right[1],
        x,
        mixed,
        norms_all,
        *second_all,
    )
    if direct:
        second_sum = collect(*grads)
        grad_up = second_sum[: D // 8]
        grad_down = second_sum[D // 8 : D // 4].T
        grad_out = second_sum[D // 4 :]
        grads_shape = [shape((4, n_seq, share, width), BF16)] * 2
    else:
        grad_up = lax.psum_scatter(grads[0], "seq", scatter_dimension=0)
        grad_up = lax.psum_scatter(grad_up, "dp", scatter_dimension=0, tiled=True)
        grad_down = lax.psum_scatter(grads[1], "seq", scatter_dimension=0)
        grad_down = lax.psum_scatter(grad_down, "dp", scatter_dimension=0, tiled=True).T
        grad_out = lax.psum_scatter(grads[2], ("dp", "seq"), scatter_dimension=0, tiled=True)
        grads_shape = [shape((D, width), F32)]
    tokens_grad, *grads = run_kernel(
        functools.partial(back_kernel, direct),
        [shape((ROWS, D), BF16), *grads_shape],
        [
            pltpu.VMEM((ROWS + 2 * HALO, D), F32),
            pltpu.VMEM((WROWS, D), BF16),
            pltpu.VMEM((WROWS, 3 * D), BF16),
            pltpu.VMEM((WROWS, D), F32),
            pltpu.VMEM((NORMS, D), F32),
            pltpu.VMEM((D, width), F32),
        ],
        2 * WROWS * D * (6 * D + 3 * D),
        info,
        x,
        qkv,
        probs,
        grad_mixed,
        grad_middle,
        w_qkv_all,
        norms_all,
        grad_norms,
    )
    if direct:
        first_sum = collect(*grads)
    else:
        first_sum = lax.psum_scatter(grads[0], ("dp", "seq"), scatter_dimension=0, tiled=True)
    return (
        out,
        tokens_grad,
        first_sum[:, : 3 * D],
        grad_out,
        grad_up,
        grad_down,
        first_sum[:, 3 * D],
        first_sum[:, 3 * D + 1],
        first_sum[:, 3 * D + 2],
        first_sum[:, 3 * D + 3],
    )


def solution(mesh):
    rows = P(("dp", "seq"), None)
    vector = P(("dp", "seq"))
    return jax.shard_map(
        per_device,
        mesh=mesh,
        in_specs=(
            rows,
            rows,
            rows,
            rows,
            P("dp", "seq"),
            P("seq", "dp"),
            vector,
            vector,
            vector,
            vector,
            P("dp", None),
            P("dp", None, None),
        ),
        out_specs=(
            rows,
            rows,
            rows,
            rows,
            P("dp", "seq"),
            P("seq", "dp"),
            vector,
            vector,
            vector,
            vector,
        ),
        check_vma=False,
    )
```

```python
import functools

import jax
import jax.numpy as jnp
from jax import lax
from jax.experimental import pallas as pl
from jax.experimental.pallas import tpu as pltpu
from jax.sharding import PartitionSpec as P

D = 512
HEADS = 16
HEAD_DIM = D // HEADS
FF = 2048
FREQ = 8
STEPS_DEV = 88
HALO = 4 * FREQ
ROWS = STEPS_DEV * FREQ
WIN = 4 * FREQ
WINDOWS = STEPS_DEV // 4 + 2
WROWS = WINDOWS * WIN
TILE = 256
QUAD = 128
NORMS = 128
CHUNK = 512
CHUNKS = FF // CHUNK
epsilon = 1e-06
F32 = jnp.float32
BF16 = jnp.bfloat16


def mm(left, right):
    return jnp.dot(left, right, preferred_element_type=F32)


def mm_right(left, right):
    return lax.dot_general(left, right, (((1,), (1,)), ((), ())), preferred_element_type=F32)


def mm_left(left, right):
    return lax.dot_general(left, right, (((0,), (0,)), ((), ())), preferred_element_type=F32)


def window_place(info, w):
    lead, mid, trail = info[0], info[1], info[2]
    seq = info[10]
    base = seq * STEPS_DEV
    n_lead = lead // 4 + 1
    n_mid = mid // 4 + 1
    index = jnp.where(seq == 0, 0, base // 4 + 1) + w
    in_mid = index >= n_lead
    in_trail = index >= n_lead + n_mid
    before = jnp.where(in_trail, n_lead + n_mid, jnp.where(in_mid, n_lead, 0))
    start = jnp.where(in_trail, lead + mid, jnp.where(in_mid, lead, 0))
    steps = jnp.where(in_trail, trail, jnp.where(in_mid, mid, lead))
    shift_time = jnp.where(in_trail, info[7], jnp.where(in_mid, info[5], info[3]))
    shift_freq = jnp.where(in_trail, info[8], jnp.where(in_mid, info[6], info[4]))
    first = start - 4 + shift_time + 4 * (index - before)
    here = first < base + STEPS_DEV
    low = jnp.clip(start - first, 0, 4)
    high = jnp.where(here, jnp.clip(start + steps - first, 0, 4), 0)
    own_low = jnp.clip(base - first, 0, 4)
    own_high = jnp.clip(base + STEPS_DEV - first, 0, 4)
    row = jnp.clip(first - base + 4, 0, STEPS_DEV + 4) * FREQ
    row = pl.multiple_of(row, FREQ)
    return (
        row,
        low * FREQ,
        high * FREQ,
        jnp.maximum(low, own_low) * FREQ,
        jnp.minimum(high, own_high) * FREQ,
        shift_freq,
    )


def window_at(w):
    return pl.ds(pl.multiple_of(w * WIN, WIN), WIN)


def tile_at(i):
    return pl.ds(pl.multiple_of(i * TILE, TILE), TILE)


def row_mask(low, high):
    index = lax.broadcasted_iota(jnp.int32, (WIN, 1), 0)
    return (index >= low) & (index < high)


def copy_all(pairs, sems, first=0):
    copies = [
        pltpu.make_async_copy(source, target, sems.at[first + i])
        for i, (source, target) in enumerate(pairs)
    ]
    for copy in copies:
        copy.start()
    return copies


def wait_all(copies):
    for copy in copies:
        copy.wait()


def row_copies(rows, near, far, column, stage, halos):
    return [
        (rows, stage),
        (near.at[:, column : column + 2 * D], halos.at[0]),
        (far.at[:, column : column + 2 * D], halos.at[1]),
    ]


def pad_rows(info, ext, stage, halos):
    ext[HALO : HALO + ROWS] = stage[...].astype(F32)
    odd = info[10] % 2 == 1
    for i, is_left in enumerate((odd, jnp.logical_not(odd))):
        at = pl.multiple_of(jnp.where(is_left, 0, HALO + ROWS), HALO)
        ext[pl.ds(at, HALO // 2), :] = halos[i, :, 0:D].astype(F32)
        ext[pl.ds(at + HALO // 2, HALO // 2), :] = halos[i, :, D : 2 * D].astype(F32)


def normalized(values):
    mean = jnp.mean(values, axis=-1, keepdims=True)
    centered = values - mean
    variance = jnp.mean(centered * centered, axis=-1, keepdims=True)
    scale = lax.rsqrt(variance + epsilon)
    return centered * scale, scale


def norm_back(grad, unit, scale):
    mean_one = jnp.mean(grad, axis=-1, keepdims=True)
    mean_two = jnp.mean(grad * unit, axis=-1, keepdims=True)
    return scale * (grad - mean_one - unit * mean_two)


def head_masks():
    lane = lax.broadcasted_iota(jnp.int32, (1, QUAD), 1) // HEAD_DIM
    return [(lane == h).astype(BF16) for h in range(QUAD // HEAD_DIM)]


def spread(block, masks):
    return jnp.concatenate([block * mask for mask in masks], axis=0)


def gathered(product, lane):
    parts = [product[h * WIN : (h + 1) * WIN] for h in range(QUAD // HEAD_DIM)]
    return jnp.where(
        lane < 1, parts[0], jnp.where(lane < 2, parts[1], jnp.where(lane < 3, parts[2], parts[3]))
    )


def attention_kernel(direct, info, rows, near, far, *refs):
    pieces, refs = (refs[:8], refs[8:]) if direct else (refs[:1], refs[1:])
    x_out, qkv_out, mixed_out, probs_out, w_out, norms_out, ext, stage, halos, sems = refs
    column = w_out.shape[1] if direct else 0
    row_copy = copy_all(row_copies(rows, near, far, column, stage, halos), sems)
    if direct:
        share, pairs = pieces[0].shape[1], []
        for piece, partner in zip(pieces, ORDER):
            for k in range(piece.shape[0]):
                owner = (info[9] ^ partner) * piece.shape[0] + (info[10] ^ k)
                at = pl.multiple_of(owner * share, share)
                pairs.append((piece.at[k], w_out.at[pl.ds(at, share), :]))
    else:
        pairs = [(pieces[0], w_out)]
    w_copy = copy_all(pairs, sems, len(row_copy))
    wait_all(row_copy)
    pad_rows(info, ext, stage, halos)

    def place(w, carry):
        row, low, high, _, _, _ = window_place(info, w)
        values = jnp.where(row_mask(low, high), ext[pl.ds(row, WIN), :], 0.0)
        x_out[window_at(w), :] = values.astype(BF16)
        return carry

    lax.fori_loop(0, WINDOWS, place, 0, unroll=4)
    wait_all(w_copy)
    norms_out[...] = jnp.transpose(w_out[:, 3 * D :].astype(F32))[:8]
    gain, shift = norms_out[0:1], norms_out[1:2]

    def project(i, carry):
        at = tile_at(i)
        unit, _ = normalized(x_out[at, :].astype(F32))
        low = (unit * gain + shift).astype(BF16)
        for part in range(3):
            cols = slice(part * D, (part + 1) * D)
            qkv_out[at, cols] = mm(low, w_out[:, cols]).astype(BF16)
        return carry

    lax.fori_loop(0, WROWS // TILE, project, 0)
    masks = head_masks()
    lane = lax.broadcasted_iota(jnp.int32, (1, QUAD), 1) // HEAD_DIM
    key_row = lax.broadcasted_iota(jnp.int32, (WIN, QUAD), 0)
    query_row = lax.broadcasted_iota(jnp.int32, (WIN, QUAD), 1) % WIN
    key_freq, query_freq = key_row % FREQ, query_row % FREQ

    def attend(w, carry):
        _, low, high, _, _, shift_freq = window_place(info, w)
        at = pl.ds(pl.multiple_of(w * WIN, WIN), WIN)
        key_group = (key_freq + 4 - shift_freq) >> 2
        query_group = (query_freq + 4 - shift_freq) >> 2
        allowed = (key_group == query_group) & (key_row >= low) & (key_row < high)
        quads = range(D // QUAD)
        raw = []
        for quad in quads:
            query = qkv_out[at, quad * QUAD : (quad + 1) * QUAD]
            key = qkv_out[at, D + quad * QUAD : D + (quad + 1) * QUAD]
            raw.append(mm_right(key, spread(query, masks)))
        scores = [jnp.where(allowed, r * HEAD_DIM**-0.5, -1e30) for r in raw]
        weights = [jnp.exp(s - jnp.max(s, axis=0, keepdims=True)) for s in scores]
        probs = [(p / jnp.sum(p, axis=0, keepdims=True)).astype(BF16) for p in weights]
        products = []
        for quad in quads:
            probs_out[at, quad * QUAD : (quad + 1) * QUAD] = probs[quad]
            value = qkv_out[at, 2 * D + quad * QUAD : 2 * D + (quad + 1) * QUAD]
            products.append(mm_left(probs[quad], value))
        for quad in quads:
            mixed = gathered(products[quad], lane).astype(BF16)
            mixed_out[at, quad * QUAD : (quad + 1) * QUAD] = mixed
        return carry

    lax.fori_loop(0, WINDOWS, attend, 0, unroll=4)


def gelu_parts(values):
    half_exp = jnp.exp(-0.5 * values * values)
    t = 1.0 / (1.0 + (0.3275911 * 0.7071067811865476) * jnp.abs(values))
    poly = t * (
        0.5 * 0.254829592
        + t
        * (
            0.5 * -0.284496736
            + t * (0.5 * 1.421413741 + t * (0.5 * -1.453152027 + t * (0.5 * 1.061405429)))
        )
    )
    tail = poly * half_exp
    return jnp.where(values >= 0, 1.0 - tail, tail), half_exp * 0.3989422804014327


def feed_kernel(direct, info, rows, near, far, x_in, mixed_in, norms, *refs):
    pieces, refs = (refs[:16], refs[16:]) if direct else (refs[:3], refs[3:])
    out, grad_middle, grad_mixed, grad_norms = refs[:4]
    if direct:
        (keep, send), refs = refs[4:6], refs[6:]
    else:
        (grad_up_out, grad_down_out, grad_w_out), refs = refs[4:7], refs[7:]
    up, down, w_out, ext, cot, cot_own, own, middle, total, normed, normed_own, hidden, pre, grad = refs[:14]
    stage, halos, sems = refs[14:]
    column = near.shape[1] - 2 * D
    row_copy = copy_all(row_copies(rows, near, far, column, stage, halos), sems)
    if direct:
        count = CHUNKS
        block = D // 8
        out_pairs, pairs = [], [[], []]
        for piece, partner, base in zip(pieces, ORDER * 2, (0,) * 8 + (1,) * 8):
            dp = info[9] ^ partner
            at = pl.ds(pl.multiple_of(dp * block, block), block)
            ks = slice(base, base + piece.shape[0])
            pairs[base].append((piece.at[:, 0:block, :], up.at[ks, at, :]))
            pairs[base].append((piece.at[:, block : 2 * block, :], down.at[ks, at, :]))
            for k in range(base, base + piece.shape[0]):
                row = pl.multiple_of((dp * count + (info[10] ^ k)) * 16, 16)
                out_pairs.append(
                    (piece.at[k - base, 2 * block : 2 * block + 16, :], w_out.at[pl.ds(row, 16), :])
                )
    else:
        pairs = [[(pieces[0], up), (pieces[1], down)], []]
        out_pairs = [(pieces[2], w_out)]
    at = len(row_copy)
    out_copy = copy_all(out_pairs, sems, at)
    at += len(out_pairs)
    first_copy = copy_all(pairs[0], sems, at)
    rest_copy = copy_all(pairs[1], sems, at + len(pairs[0]))
    wait_all(row_copy)
    pad_rows(info, ext, stage, halos)

    def place(w, carry):
        row, low, high, own_low, own_high, _ = window_place(info, w)
        values = ext[pl.ds(row, WIN), :]
        at = pl.ds(pl.multiple_of(w * WIN, WIN), WIN)
        cot[at, :] = jnp.where(row_mask(low, high), values, 0.0).astype(BF16)
        cot_own[at, :] = jnp.where(row_mask(own_low, own_high), values, 0.0).astype(BF16)
        own[at, :] = jnp.where(row_mask(own_low, own_high), jnp.ones((WIN, QUAD), F32), 0.0)
        return carry

    lax.fori_loop(0, WINDOWS, place, 0, unroll=4)
    gain, shift = norms[2:3], norms[3:4]
    wait_all(out_copy)

    def before(i, carry):
        at = tile_at(i)
        values = x_in[at, :].astype(F32) + mm(mixed_in[at, :], w_out[...])
        middle[at, :] = values
        total[at, :] = values
        unit, _ = normalized(values)
        low = unit * gain + shift
        normed[at, :] = low.astype(BF16)
        normed_own[at, :] = (low * own[at, 0:1]).astype(BF16)
        grad[at, :] = jnp.zeros((TILE, D), F32)
        return carry

    lax.fori_loop(0, WROWS // TILE, before, 0)

    def row_step(c, i):
        at = tile_at(i)
        values = mm(normed[at, :], up[c])
        grad_hidden = mm(cot[at, :], down[c])
        below, density = gelu_parts(values)
        hidden_low = (values * below).astype(BF16)
        grad_low = (grad_hidden * (below + values * density)).astype(BF16)
        hidden[at, :] = hidden_low
        pre[at, :] = grad_low
        total[at, :] += mm_right(hidden_low, down[c])
        grad[at, :] += mm_right(grad_low, up[c])

    for c in range(CHUNKS):
        if c < 2:
            wait_all((first_copy, rest_copy)[c])
        for i in range(WROWS // TILE):
            row_step(c, i)
        grad_up = mm_left(normed_own[...], pre[...])
        grad_down = mm_left(cot_own[...], hidden[...])
        if direct:
            ext[0:D, :] = grad_up
            for partner in range(8):
                target = send if partner & 1 else keep
                row = pl.multiple_of((info[9] ^ partner) * block, block)
                target[partner >> 1, c, 0:block, :] = ext[pl.ds(row, block), :].astype(BF16)
            ext[0:D, :] = grad_down
            for partner in range(8):
                target = send if partner & 1 else keep
                row = pl.multiple_of((info[9] ^ partner) * block, block)
                target[partner >> 1, c, block : 2 * block, :] = ext[pl.ds(row, block), :].astype(
                    BF16
                )
        else:
            grad_up_out[c] = grad_up
            grad_down_out[c] = grad_down
    grad_norms[...] = jnp.zeros(grad_norms.shape, F32)

    def after(i, carry):
        at = tile_at(i)
        unit, scale = normalized(middle[at, :])
        part = grad[at, :]
        masked = part * own[at, 0:1]
        grad_norms[0:1] += jnp.sum(masked * unit, axis=0, keepdims=True)
        grad_norms[1:2] += jnp.sum(masked, axis=0, keepdims=True)
        result = cot[at, :].astype(F32) + norm_back(part * gain, unit, scale)
        grad_middle[at, :] = result
        low = result.astype(BF16)
        grad_mixed[at, :] = mm_right(low, w_out[...]).astype(BF16)
        normed_own[at, :] = (result * own[at, 0:1]).astype(BF16)
        return carry

    lax.fori_loop(0, WROWS // TILE, after, 0)
    grad_out = mm_left(mixed_in[...], normed_own[...])
    if direct:
        ext[0:D, :] = grad_out
        for partner in range(8):
            target = send if partner & 1 else keep
            for k in range(count):
                row = pl.multiple_of(((info[9] ^ partner) * count + (info[10] ^ k)) * 16, 16)
                target[partner >> 1, k, 2 * block :, :] = ext[pl.ds(row, 16), :].astype(BF16)
    else:
        grad_w_out[...] = grad_out
    unplace(info, total, ext, out)


def unplace(info, values, ext, out):
    def back(w, carry):
        row, low, high, _, _, _ = window_place(info, w)
        at = pl.ds(pl.multiple_of(w * WIN, WIN), WIN)
        place = pl.ds(row, WIN)
        ext[place, :] = jnp.where(row_mask(low, high), values[at, :], ext[place, :])
        return carry

    lax.fori_loop(0, WINDOWS, back, 0, unroll=4)
    out[...] = ext[HALO : HALO + ROWS].astype(BF16)


def back_kernel(
    direct, info, x_in, qkv, probs_in, grad_mixed, grad_middle, w_qkv, norms, grad_norms, *refs
):
    out, refs = refs[0], refs[1:]
    if direct:
        (keep, send), refs = refs[:2], refs[2:]
    else:
        w_grad, refs = refs[0], refs[1:]
    ext, normed, grad_qkv, result, gains, grad_w, own = refs
    masks = head_masks()
    lane = lax.broadcasted_iota(jnp.int32, (1, QUAD), 1) // HEAD_DIM

    def attend_back(w, carry):
        at = window_at(w)
        own[at, :] = jnp.where(
            row_mask(*window_place(info, w)[3:5]), jnp.ones((WIN, QUAD), F32), 0.0
        )
        quads = range(D // QUAD)
        cols = [slice(quad * QUAD, (quad + 1) * QUAD) for quad in quads]
        cols_key = [slice(D + quad * QUAD, D + (quad + 1) * QUAD) for quad in quads]
        cols_value = [slice(2 * D + quad * QUAD, 2 * D + (quad + 1) * QUAD) for quad in quads]
        grad_out = [spread(grad_mixed[at, c], masks) for c in cols]
        grad_probs = [mm_right(qkv[at, c], g) for c, g in zip(cols_value, grad_out)]
        low = [probs_in[at, c] for c in cols]
        probs = [p.astype(F32) for p in low]
        delta = [jnp.sum(p * g, axis=0, keepdims=True) for p, g in zip(probs, grad_probs)]
        grad_scores = [
            (p * (g - d) * HEAD_DIM**-0.5).astype(BF16)
            for p, g, d in zip(probs, grad_probs, delta)
        ]
        grad_value = [mm(p, g) for p, g in zip(low, grad_out)]
        grad_query = [mm_left(g, qkv[at, c]) for g, c in zip(grad_scores, cols_key)]
        grad_key = [mm(g, spread(qkv[at, c], masks)) for g, c in zip(grad_scores, cols)]
        for quad in quads:
            grad_qkv[at, cols_value[quad]] = grad_value[quad].astype(BF16)
            grad_qkv[at, cols_key[quad]] = grad_key[quad].astype(BF16)
            grad_qkv[at, cols[quad]] = gathered(grad_query[quad], lane).astype(BF16)
        return carry

    lax.fori_loop(0, WINDOWS, attend_back, 0, unroll=4)
    gain, shift = norms[0:1], norms[1:2]
    gains[...] = jnp.zeros(gains.shape, F32)

    def after(i, carry):
        at = tile_at(i)
        unit, scale = normalized(x_in[at, :].astype(F32))
        mask = own[at, 0:1]
        normed[at, :] = ((unit * gain + shift) * mask).astype(BF16)
        part = mm_right(grad_qkv[at, :], w_qkv[:, : 3 * D])
        masked = part * mask
        gains[0:1] += jnp.sum(masked * unit, axis=0, keepdims=True)
        gains[1:2] += jnp.sum(masked, axis=0, keepdims=True)
        result[at, :] = grad_middle[at, :] + norm_back(part * gain, unit, scale)
        return carry

    lax.fori_loop(0, WROWS // TILE, after, 0)
    gains[2:4] = grad_norms[0:2]
    for part in range(3):
        cols = slice(part * D, (part + 1) * D)
        grad_w[:, cols] = mm_left(normed[...], grad_qkv[:, cols])
    grad_w[:, 3 * D :] = jnp.transpose(gains[...])
    if direct:
        count = keep.shape[1]
        for partner in range(8):
            target = send if partner & 1 else keep
            for k in range(count):
                row = pl.multiple_of(((info[9] ^ partner) * count + (info[10] ^ k)) * 16, 16)
                target[partner >> 1, k] = grad_w[pl.ds(row, 16), :].astype(BF16)
    else:
        w_grad[...] = grad_w[...]
    unplace(info, result, ext, out)


ORDER = (0, 2, 4, 6, 1, 3, 5, 7)
LIMIT = 36 * 1024 * 1024
SMEM = pl.BlockSpec(memory_space=pltpu.SMEM)
VMEM = pl.BlockSpec(memory_space=pltpu.VMEM)
ANY = pl.BlockSpec(memory_space=pl.ANY)


def near_core(array):
    return pltpu.with_memory_space_constraint(array, pltpu.VMEM)


def far_core(array):
    return pltpu.with_memory_space_constraint(array, pltpu.HBM)


def run_kernel(body, out_shape, scratch, flops, info, vmem, hbm):
    operands = (*hbm[:3], *vmem, *hbm[3:])
    specs = [ANY] * len(hbm[:3]) + [VMEM] * len(vmem) + [ANY] * len(hbm[3:])
    placed = [near_core(a) if s is VMEM else far_core(a) for a, s in zip(operands, specs)]
    moved = sum(a.size * a.dtype.itemsize for a in operands)
    return pl.pallas_call(
        body,
        out_shape=out_shape,
        in_specs=[SMEM] + specs,
        out_specs=[VMEM] * len(out_shape),
        scratch_shapes=scratch,
        cost_estimate=pl.CostEstimate(
            flops=flops, bytes_accessed=moved, transcendentals=flops // 1024
        ),
        compiler_params=pltpu.CompilerParams(vmem_limit_bytes=LIMIT),
    )(info, *placed)


def swap(array, axis, bit):
    return lax.ppermute(array, axis, [(i, i ^ bit) for i in range(lax.axis_size(axis))])


def together(*values):
    return lax.optimization_barrier(values)


def along_seq(shard):
    return [swap(shard, "seq", k) for k in (1, 2, 3)]


def along_plane(column):
    return [swap(column, "dp", partner) for partner in (2, 4, 6)]


def along_core(pieces):
    return [swap(piece, "dp", 1) for piece in pieces]


def add_parts(own, parts):
    return own.astype(F32) + sum(part.astype(F32) for part in parts)


def shape(dims, kind):
    return pltpu.VMEM(dims, kind)


def per_device(
    tokens,
    cotangent,
    w_qkv,
    w_out,
    w_up,
    w_down,
    norm1_gain,
    norm1_shift,
    norm2_gain,
    norm2_shift,
    clip_steps,
    window_shifts,
):
    n_dp, n_seq = lax.axis_size("dp"), lax.axis_size("seq")
    share = w_qkv.shape[0]
    direct = n_dp == 8 and share % 16 == 0
    info = jnp.concatenate(
        [
            clip_steps.reshape(3),
            window_shifts.reshape(6),
            lax.axis_index("dp").reshape(1).astype(jnp.int32),
            lax.axis_index("seq").reshape(1).astype(jnp.int32),
        ]
    )
    norms = jnp.stack([norm1_gain, norm1_shift, norm2_gain, norm2_shift], axis=1)
    first = jnp.concatenate([w_qkv, jnp.pad(norms, ((0, 0), (0, NORMS - 4)))], axis=1)
    width = first.shape[1]
    head = [a[i : i + HALO // 2] for a in (tokens, cotangent) for i in (0, HALO // 2)]
    tail = [a[i : i + HALO // 2] for a in (tokens, cotangent) for i in (ROWS - HALO, ROWS - HALO // 2)]
    head, tail = jnp.concatenate(head, axis=1), jnp.concatenate(tail, axis=1)
    odd = lax.axis_index("seq") % 2 == 1
    to_near, to_far = jnp.where(odd, head, tail), jnp.where(odd, tail, head)
    if direct:
        second = jnp.concatenate([w_up, w_down.T, w_out], axis=0)
        with_near = jnp.concatenate([first, to_near], axis=1)
        with_far = jnp.concatenate([first, to_far], axis=1)
        near, middle, far, *second_own = together(
            swap(with_near, "seq", 1),
            swap(first, "seq", 2),
            swap(with_far, "seq", 3),
            *along_plane(second),
        )
        column = jnp.stack([first, near[:, :width], middle, far[:, :width]])
        second_own = [second] + second_own
        column, second = together(column, second)
        results = together(*along_plane(column), *along_seq(second), *along_core(second_own))
        first_plane, rest, second_own = [column, *results[:3]], results[3:6], second_own + [*results[6:]]
        rest = jnp.stack(rest)
        *first_plane, rest = together(*first_plane, rest)
        first_all = first_plane + along_core(first_plane)
        second_plane = along_plane(rest)
    else:
        first_all = [lax.all_gather(first, ("dp", "seq"), axis=0, tiled=True)]
        up_all = lax.all_gather(lax.all_gather(w_up, "dp", axis=0, tiled=True), "seq", axis=0)
        down_all = lax.all_gather(lax.all_gather(w_down.T, "dp", axis=0, tiled=True), "seq", axis=0)
        second_all = [up_all, down_all, lax.all_gather(w_out, ("dp", "seq"), axis=0, tiled=True)]
        from_left = lax.ppermute(tail, "seq", [(i, i + 1) for i in range(n_seq - 1)])
        from_right = lax.ppermute(head, "seq", [(i + 1, i) for i in range(n_seq - 1)])
        near, far = jnp.where(odd, from_left, from_right), jnp.where(odd, from_right, from_left)

    x, qkv, mixed, probs, w_qkv_all, norms_all = run_kernel(
        functools.partial(attention_kernel, direct),
        [
            shape((WROWS, D), BF16),
            shape((WROWS, 3 * D), BF16),
            shape((WROWS, D), BF16),
            shape((WROWS, D), BF16),
            shape((D, width), BF16),
            shape((8, D), F32),
        ],
        [
            pltpu.VMEM((ROWS + 2 * HALO, D), F32),
            pltpu.VMEM((ROWS, D), BF16),
            pltpu.VMEM((2, HALO // 2, 2 * D), BF16),
            pltpu.SemaphoreType.DMA((35,)),
        ],
        2 * WROWS * D * 3 * D * 2,
        info,
        (),
        (tokens, near, far, *first_all),
    )
    if direct:
        *second_plane, mixed = together(*second_plane, mixed)
        second_plane = [rest, *second_plane]
        second_all = second_own + second_plane + along_core(second_plane)
        second_all = [a.reshape(-1, *second.shape) for a in second_all]
        block = (4, n_seq, *second.shape)
        grads_shape = [shape(block, BF16)] * 2
    else:
        grads_shape = [shape((CHUNKS, D, CHUNK), F32)] * 2 + [shape((D, D), F32)]
    out, grad_middle, grad_mixed, grad_norms, *grads = run_kernel(
        functools.partial(feed_kernel, direct),
        [
            shape((ROWS, D), BF16),
            shape((WROWS, D), F32),
            shape((WROWS, D), BF16),
            shape((8, D), F32),
            *grads_shape,
        ],
        [
            pltpu.VMEM((CHUNKS, D, CHUNK), BF16),
            pltpu.VMEM((CHUNKS, D, CHUNK), BF16),
            pltpu.VMEM((D, D), BF16),
            pltpu.VMEM((ROWS + 2 * HALO, D), F32),
            pltpu.VMEM((WROWS, D), BF16),
            pltpu.VMEM((WROWS, D), BF16),
            pltpu.VMEM((WROWS, QUAD), F32),
            pltpu.VMEM((WROWS, D), F32),
            pltpu.VMEM((WROWS, D), F32),
            pltpu.VMEM((WROWS, D), BF16),
            pltpu.VMEM((WROWS, D), BF16),
            pltpu.VMEM((WROWS, CHUNK), BF16),
            pltpu.VMEM((WROWS, CHUNK), BF16),
            pltpu.VMEM((WROWS, D), F32),
            pltpu.VMEM((ROWS, D), BF16),
            pltpu.VMEM((2, HALO // 2, 2 * D), BF16),
            pltpu.SemaphoreType.DMA((67,)),
        ],
        2 * WROWS * D * (6 * FF + 3 * D),
        info,
        (x, mixed, norms_all),
        (cotangent, near, far, *second_all),
    )
    if direct:
        pair = add_parts(grads[0], along_core(grads[1:]))
        second_pair, low_own, low_rest, grad_mixed = together(
            pair[0], pair[1:, 0].astype(BF16), pair[1:, 1:].astype(BF16), grad_mixed
        )
        second_parts = [swap(low_rest[m], "dp", 2 * m + 2) for m in range(3)]
        grads_shape = [shape((4, n_seq, share, width), BF16)] * 2
    else:
        grad_up = lax.psum_scatter(grads[0], "seq", scatter_dimension=0)
        grad_up = lax.psum_scatter(grad_up, "dp", scatter_dimension=0, tiled=True)
        grad_down = lax.psum_scatter(grads[1], "seq", scatter_dimension=0)
        grad_down = lax.psum_scatter(grad_down, "dp", scatter_dimension=0, tiled=True).T
        grad_out = lax.psum_scatter(grads[2], ("dp", "seq"), scatter_dimension=0, tiled=True)
        grads_shape = [shape((D, width), F32)]
    tokens_grad, *grads = run_kernel(
        functools.partial(back_kernel, direct),
        [shape((ROWS, D), BF16), *grads_shape],
        [
            pltpu.VMEM((ROWS + 2 * HALO, D), F32),
            pltpu.VMEM((WROWS, D), BF16),
            pltpu.VMEM((WROWS, 3 * D), BF16),
            pltpu.VMEM((WROWS, D), F32),
            pltpu.VMEM((NORMS, D), F32),
            pltpu.VMEM((D, width), F32),
            pltpu.VMEM((WROWS, QUAD), F32),
        ],
        2 * WROWS * D * (6 * D + 3 * D),
        info,
        (x, qkv, probs, grad_mixed, grad_middle, w_qkv_all, norms_all, grad_norms),
        (),
    )
    if direct:
        keep, send, *second_parts = together(*grads, *second_parts)
        pair = add_parts(keep, along_core([send]))
        low, first_own, second_rest = together(
            pair[1:].astype(BF16), pair[0], add_parts(second_pair[1:], second_parts)
        )
        second_low = second_rest.astype(BF16)
        parts = together(
            *[swap(low[m], "dp", 2 * m + 2) for m in range(3)],
            *[swap(second_low[k], "seq", k + 1) for k in range(3)],
        )
        first_column = add_parts(first_own, parts[:3])
        low, low_own, first_own = together(
            first_column[1:].astype(BF16), low_own, first_column[0]
        )
        first_parts = [swap(low[k], "seq", k + 1) for k in range(3)]
        own_parts = [swap(low_own[m], "dp", 2 * m + 2) for m in range(3)]
        second_sum = add_parts(second_pair[0], [*parts[3:], *own_parts])
        first_sum = add_parts(first_own, first_parts)
        grad_up = second_sum[: D // 8]
        grad_down = second_sum[D // 8 : D // 4].T
        grad_out = second_sum[D // 4 :]
    else:
        first_sum = lax.psum_scatter(grads[0], ("dp", "seq"), scatter_dimension=0, tiled=True)
    return (
        out,
        tokens_grad,
        first_sum[:, : 3 * D],
        grad_out,
        grad_up,
        grad_down,
        first_sum[:, 3 * D],
        first_sum[:, 3 * D + 1],
        first_sum[:, 3 * D + 2],
        first_sum[:, 3 * D + 3],
    )


def solution(mesh):
    rows = P(("dp", "seq"), None)
    vector = P(("dp", "seq"))
    return jax.shard_map(
        per_device,
        mesh=mesh,
        in_specs=(
            rows,
            rows,
            rows,
            rows,
            P("dp", "seq"),
            P("seq", "dp"),
            vector,
            vector,
            vector,
            vector,
            P("dp", None),
            P("dp", None, None),
        ),
        out_specs=(
            rows,
            rows,
            rows,
            rows,
            P("dp", "seq"),
            P("seq", "dp"),
            vector,
            vector,
            vector,
            vector,
        ),
        check_vma=False,
    )
```

```python
import functools

import jax
import jax.numpy as jnp
from jax import lax
from jax.experimental import pallas as pl
from jax.experimental.pallas import tpu as pltpu
from jax.sharding import PartitionSpec as P

D = 512
HEADS = 16
HEAD_DIM = D // HEADS
FF = 2048
FREQ = 8
STEPS_DEV = 88
HALO = 4 * FREQ
ROWS = STEPS_DEV * FREQ
WIN = 4 * FREQ
WINDOWS = STEPS_DEV // 4 + 2
WROWS = WINDOWS * WIN
TILE = 256
QUAD = 128
NORMS = 128
CHUNK = 512
CHUNKS = FF // CHUNK
epsilon = 1e-06
F32 = jnp.float32
BF16 = jnp.bfloat16


def mm(left, right):
    return jnp.dot(left, right, preferred_element_type=F32)


def mm_right(left, right):
    return lax.dot_general(left, right, (((1,), (1,)), ((), ())), preferred_element_type=F32)


def mm_left(left, right):
    return lax.dot_general(left, right, (((0,), (0,)), ((), ())), preferred_element_type=F32)


def window_place(info, w):
    lead, mid, trail = info[0], info[1], info[2]
    seq = info[10]
    base = seq * STEPS_DEV
    n_lead = lead // 4 + 1
    n_mid = mid // 4 + 1
    index = jnp.where(seq == 0, 0, base // 4 + 1) + w
    in_mid = index >= n_lead
    in_trail = index >= n_lead + n_mid
    before = jnp.where(in_trail, n_lead + n_mid, jnp.where(in_mid, n_lead, 0))
    start = jnp.where(in_trail, lead + mid, jnp.where(in_mid, lead, 0))
    steps = jnp.where(in_trail, trail, jnp.where(in_mid, mid, lead))
    shift_time = jnp.where(in_trail, info[7], jnp.where(in_mid, info[5], info[3]))
    shift_freq = jnp.where(in_trail, info[8], jnp.where(in_mid, info[6], info[4]))
    first = start - 4 + shift_time + 4 * (index - before)
    here = first < base + STEPS_DEV
    low = jnp.clip(start - first, 0, 4)
    high = jnp.where(here, jnp.clip(start + steps - first, 0, 4), 0)
    own_low = jnp.clip(base - first, 0, 4)
    own_high = jnp.clip(base + STEPS_DEV - first, 0, 4)
    row = jnp.clip(first - base + 4, 0, STEPS_DEV + 4) * FREQ
    row = pl.multiple_of(row, FREQ)
    return (
        row,
        low * FREQ,
        high * FREQ,
        jnp.maximum(low, own_low) * FREQ,
        jnp.minimum(high, own_high) * FREQ,
        shift_freq,
    )


def window_at(w):
    return pl.ds(pl.multiple_of(w * WIN, WIN), WIN)


def tile_at(i):
    return pl.ds(pl.multiple_of(i * TILE, TILE), TILE)


def row_mask(low, high):
    index = lax.broadcasted_iota(jnp.int32, (WIN, 1), 0)
    return (index >= low) & (index < high)


def copy_all(pairs, sems, first=0):
    copies = [
        pltpu.make_async_copy(source, target, sems.at[first + i])
        for i, (source, target) in enumerate(pairs)
    ]
    for copy in copies:
        copy.start()
    return copies


def wait_all(copies):
    for copy in copies:
        copy.wait()


def row_copies(rows, near, far, stage, halos):
    pairs = [(rows, stage)]
    for i, parts in enumerate((near, far)):
        size = HALO // len(parts)
        pairs += [
            (part, halos.at[i, j * size : (j + 1) * size, :]) for j, part in enumerate(parts)
        ]
    return pairs


def pad_rows(info, ext, stage, halos):
    ext[HALO : HALO + ROWS] = stage[...].astype(F32)
    odd = info[10] % 2 == 1
    for i, is_left in enumerate((odd, jnp.logical_not(odd))):
        at = pl.multiple_of(jnp.where(is_left, 0, HALO + ROWS), HALO)
        ext[pl.ds(at, HALO), :] = halos[i].astype(F32)


def normalized(values):
    mean = jnp.mean(values, axis=-1, keepdims=True)
    centered = values - mean
    variance = jnp.mean(centered * centered, axis=-1, keepdims=True)
    scale = lax.rsqrt(variance + epsilon)
    return centered * scale, scale


def norm_back(grad, unit, scale):
    mean_one = jnp.mean(grad, axis=-1, keepdims=True)
    mean_two = jnp.mean(grad * unit, axis=-1, keepdims=True)
    return scale * (grad - mean_one - unit * mean_two)


def head_masks():
    lane = lax.broadcasted_iota(jnp.int32, (1, QUAD), 1) // HEAD_DIM
    return [(lane == h).astype(BF16) for h in range(QUAD // HEAD_DIM)]


def spread(block, masks):
    return jnp.concatenate([block * mask for mask in masks], axis=0)


def gathered(product, lane):
    parts = [product[h * WIN : (h + 1) * WIN] for h in range(QUAD // HEAD_DIM)]
    return jnp.where(
        lane < 1, parts[0], jnp.where(lane < 2, parts[1], jnp.where(lane < 3, parts[2], parts[3]))
    )


def sum_kernel(plan, *refs):
    ins, outs = refs[: -len(plan)], refs[-len(plan) :]
    for out, pieces in zip(outs, plan):
        for target, source in pieces:
            value = ins[0][source].astype(F32)
            for part in ins[1:]:
                value = value + part[source].astype(F32)
            out[target] = value.astype(out.dtype)


def add(plan, shapes, *operands):
    return pl.pallas_call(
        functools.partial(sum_kernel, plan),
        out_shape=[jax.ShapeDtypeStruct(*s) for s in shapes],
        in_specs=[VMEM] * len(operands),
        out_specs=[VMEM] * len(shapes),
        compiler_params=pltpu.CompilerParams(vmem_limit_bytes=SMALL),
    )(*[near_core(a) for a in operands])


def tail_kernel(row, own, *refs):
    parts, out = refs[:-1], refs[-1]
    total = own[...]
    for part in parts:
        total = total + part[row : row + out.shape[0], :].astype(F32)
    out[...] = total


def add_tail(own, parts, row):
    return pl.pallas_call(
        functools.partial(tail_kernel, row),
        out_shape=[jax.ShapeDtypeStruct(own.shape, F32)],
        in_specs=[VMEM] * (1 + len(parts)),
        out_specs=[VMEM],
        compiler_params=pltpu.CompilerParams(vmem_limit_bytes=SMALL),
    )(*[near_core(a) for a in (own, *parts)])


def pair_kernel(keep, *refs):
    for m, (part, out) in enumerate(zip(refs[:4], refs[4:])):
        out[...] = (keep[m].astype(F32) + part[...].astype(F32)).astype(out.dtype)


def add_pairs(keep, parts):
    slot = keep.shape[1:]
    return pl.pallas_call(
        pair_kernel,
        out_shape=[jax.ShapeDtypeStruct(slot, kind) for kind in (F32, BF16, BF16, BF16)],
        in_specs=[VMEM] * 5,
        out_specs=[VMEM] * 4,
        compiler_params=pltpu.CompilerParams(vmem_limit_bytes=SMALL),
    )(*[near_core(a) for a in (keep, *parts)])


def finish_kernel(own, one, two, three, grad, *norm_grads):
    total = own[...] + (one[...].astype(F32) + two[...].astype(F32) + three[...].astype(F32))
    grad[...] = total[:, : 3 * D]
    rows = jnp.transpose(total[:, 3 * D :])
    for i, norm_grad in enumerate(norm_grads):
        norm_grad[...] = rows[i : i + 1]


def finish_first(own, parts):
    share = own.shape[0]
    shapes = [(share, 3 * D)] + [(1, share)] * 4
    return pl.pallas_call(
        finish_kernel,
        out_shape=[jax.ShapeDtypeStruct(dims, F32) for dims in shapes],
        in_specs=[VMEM] * (1 + len(parts)),
        out_specs=[VMEM] * len(shapes),
        compiler_params=pltpu.CompilerParams(vmem_limit_bytes=SMALL),
    )(*[near_core(a) for a in (own, *parts)])


def add_slots(*operands):
    slot = operands[0].shape[1:]
    plan = [[(slice(None), i)] for i in range(4)]
    return add(plan, [(slot, F32)] + [(slot, BF16)] * 3, *operands)


def prepare_kernel(tokens, cotangent, w_qkv, w_out, w_up, w_down, *refs):
    norms, (with_near, first, with_far, second, up_near, up_far, vectors, sems) = refs[:4], refs[4:]
    share, width = first.shape
    block = w_up.shape[0]
    odd = lax.axis_index("seq") % 2
    pairs = [(norm, vectors.at[i]) for i, norm in enumerate(norms)]
    for target in (with_near, first, with_far):
        pairs += [(w_qkv, target.at[:, : 3 * D]), (w_out, target.at[:, 3 * D : 4 * D])]
    for target, up_target, is_head in ((with_near, up_near, odd), (with_far, up_far, 1 - odd)):
        start = pl.multiple_of((1 - is_head) * (ROWS - HALO), HALO)
        for j in range(2):
            at = width + j * D
            rows = pl.ds(start + j * (HALO // 2), HALO // 2)
            pairs.append((tokens.at[rows, :], target.at[:, at : at + D]))
        pairs.append((cotangent.at[pl.ds(start, HALO), :], up_target.at[2 * block :, :]))
    for target in (second, up_near, up_far):
        pairs += [(w_up, target.at[0:block]), (w_down, target.at[block : 2 * block])]
    first_row = 2 * block
    for i, source in enumerate([w_qkv.at[:, j * D : (j + 1) * D] for j in range(3)] + [w_out]):
        pairs.append((source, second.at[first_row + share * i : first_row + share * (i + 1), :]))
    copies = copy_all(pairs, sems)
    wait_all(copies[: len(norms)])
    columns = jnp.concatenate(
        [vectors[i].astype(F32) for i in range(4)] + [jnp.zeros((NORMS - 4, share), F32)], axis=0
    )
    columns = jnp.transpose(columns).astype(BF16)
    for target in (with_near, first, with_far):
        target[:, 4 * D : width] = columns
    second[first_row + 4 * share :, :] = jnp.concatenate([columns] * (D // NORMS), axis=1)
    wait_all(copies[len(norms) :])


def attention_kernel(direct, info, rows, near, far, *refs):
    pieces, refs = (refs[:4], refs[4:]) if direct else (refs[:1], refs[1:])
    x_out, qkv_out, mixed_out, probs_out, w_out, norms_out, ext, stage, halos, sems = refs
    width = w_out.shape[1]
    near, far = [
        [a.at[:, width + j * D : width + (j + 1) * D] for j in range(2)] if direct else [a]
        for a in (near, far)
    ]
    row_copy = copy_all(row_copies(rows, near, far, stage, halos), sems)
    if direct:
        count, share, pairs = pieces[0].shape[1] + 1, pieces[0].shape[2], []
        for core, piece in enumerate(pieces[:2]):
            for chip in range(4):
                for k in range(1, count):
                    owner = (2 * chip + (info[9] % 2 ^ core)) * count + (info[10] ^ k)
                    at = pl.multiple_of(owner * share, share)
                    pairs.append((piece.at[chip, k - 1], w_out.at[pl.ds(at, share), :]))
        own = [piece.at[m] for piece in pieces[2:] for m in range(4)]
        for piece, partner in zip(own, ORDER):
            owner = (info[9] ^ partner) * count + info[10]
            at = pl.ds(pl.multiple_of(owner * share, share), share)
            for i in range(5):
                cols = min(D, w_out.shape[1] - i * D)
                row = D // 4 + i * share
                source = piece.at[row : row + share, 0:cols]
                pairs.append((source, w_out.at[at, i * D : i * D + cols]))
    else:
        pairs = [(pieces[0], w_out)]
    w_copy = copy_all(pairs, sems, len(row_copy))
    wait_all(row_copy)
    pad_rows(info, ext, stage, halos)

    def place(w, carry):
        row, low, high, _, _, _ = window_place(info, w)
        values = jnp.where(row_mask(low, high), ext[pl.ds(row, WIN), :], 0.0)
        x_out[window_at(w), :] = values.astype(BF16)
        return carry

    lax.fori_loop(0, WINDOWS, place, 0, unroll=4)
    wait_all(w_copy)
    norms_out[...] = jnp.transpose(w_out[:, 4 * D :].astype(F32))[:8]
    gain, shift = norms_out[0:1], norms_out[1:2]

    def project(i, carry):
        at = tile_at(i)
        unit, _ = normalized(x_out[at, :].astype(F32))
        low = (unit * gain + shift).astype(BF16)
        for part in range(3):
            cols = slice(part * D, (part + 1) * D)
            qkv_out[at, cols] = mm(low, w_out[:, cols]).astype(BF16)
        return carry

    lax.fori_loop(0, WROWS // TILE, project, 0)
    masks = head_masks()
    lane = lax.broadcasted_iota(jnp.int32, (1, QUAD), 1) // HEAD_DIM
    key_row = lax.broadcasted_iota(jnp.int32, (WIN, QUAD), 0)
    query_row = lax.broadcasted_iota(jnp.int32, (WIN, QUAD), 1) % WIN
    key_freq, query_freq = key_row % FREQ, query_row % FREQ

    def attend(w, carry):
        _, low, high, _, _, shift_freq = window_place(info, w)
        at = pl.ds(pl.multiple_of(w * WIN, WIN), WIN)
        key_group = (key_freq + 4 - shift_freq) >> 2
        query_group = (query_freq + 4 - shift_freq) >> 2
        allowed = (key_group == query_group) & (key_row >= low) & (key_row < high)
        quads = range(D // QUAD)
        raw = []
        for quad in quads:
            query = qkv_out[at, quad * QUAD : (quad + 1) * QUAD]
            key = qkv_out[at, D + quad * QUAD : D + (quad + 1) * QUAD]
            raw.append(mm_right(key, spread(query, masks)))
        scores = [jnp.where(allowed, r * HEAD_DIM**-0.5, -1e30) for r in raw]
        weights = [jnp.exp(s - jnp.max(s, axis=0, keepdims=True)) for s in scores]
        probs = [(p / jnp.sum(p, axis=0, keepdims=True)).astype(BF16) for p in weights]
        products = []
        for quad in quads:
            probs_out[at, quad * QUAD : (quad + 1) * QUAD] = probs[quad]
            value = qkv_out[at, 2 * D + quad * QUAD : 2 * D + (quad + 1) * QUAD]
            products.append(mm_left(probs[quad], value))
        for quad in quads:
            mixed = gathered(products[quad], lane).astype(BF16)
            mixed_out[at, quad * QUAD : (quad + 1) * QUAD] = mixed
        return carry

    lax.fori_loop(0, WINDOWS, attend, 0, unroll=4)


def gelu_parts(values):
    half_exp = jnp.exp(-0.5 * values * values)
    t = 1.0 / (1.0 + (0.3275911 * 0.7071067811865476) * jnp.abs(values))
    poly = t * (
        0.5 * 0.254829592
        + t
        * (
            0.5 * -0.284496736
            + t * (0.5 * 1.421413741 + t * (0.5 * -1.453152027 + t * (0.5 * 1.061405429)))
        )
    )
    tail = poly * half_exp
    return jnp.where(values >= 0, 1.0 - tail, tail), half_exp * 0.3989422804014327


def feed_pieces(info, pieces, up, down):
    block, pairs = D // 8, []
    for piece, partner in zip(pieces, ORDER):
        at = pl.ds(pl.multiple_of((info[9] ^ partner) * block, block), block)
        pairs.append((piece.at[:, 0:block, :], up.at[:, at, :]))
        pairs.append((piece.at[:, block : 2 * block, :], down.at[:, at, :]))
    return pairs


def feed_rows(at, up, down, normed, cot, hidden, pre):
    values = mm(normed[at, :], up)
    grad_hidden = mm(cot[at, :], down)
    below, density = gelu_parts(values)
    hidden_low = (values * below).astype(BF16)
    grad_low = (grad_hidden * (below + values * density)).astype(BF16)
    hidden[at, :] = hidden_low
    pre[at, :] = grad_low
    return mm_right(hidden_low, down), mm_right(grad_low, up)


def feed_grads(direct, info, row, normed_own, cot_own, hidden, pre, space, refs):
    block = D // 8
    for i, product in enumerate(((normed_own, pre), (cot_own, hidden))):
        grad = mm_left(product[0][...], product[1][...])
        if not direct:
            refs[i][row // (2 * block)] = grad
            continue
        space[0:D, :] = grad
        for partner in range(8):
            at = pl.multiple_of((info[9] ^ partner) * block, block)
            first = row + i * block
            refs[partner & 1][partner >> 1, first : first + block, :] = space[
                pl.ds(at, block), :
            ].astype(BF16)


def feed_first_kernel(direct, info, rows, near, far, x_in, mixed_in, norms, w_all, *refs):
    pieces, refs = refs[:2], refs[2:]
    middle, total, grad, normed, normed_own, cot, cot_own, own = refs[:8]
    grads, (up, down, ext, hidden, pre, stage, halos, sems) = refs[8:10], refs[10:]
    near, far = [[a.at[a.shape[0] - HALO :, :]] for a in (near, far)]
    row_copy = copy_all(row_copies(rows, near, far, stage, halos), sems)
    if direct:
        own_pieces = [piece.at[m : m + 1] for piece in pieces for m in range(4)]
        pairs = feed_pieces(info, own_pieces, up, down)
    else:
        pairs = [(pieces[0].at[0:1], up), (pieces[1].at[0:1], down)]
    first_copy = copy_all(pairs, sems, len(row_copy))
    wait_all(row_copy)
    pad_rows(info, ext, stage, halos)

    def place(w, carry):
        row, low, high, own_low, own_high, _ = window_place(info, w)
        values = ext[pl.ds(row, WIN), :]
        at = window_at(w)
        cot[at, :] = jnp.where(row_mask(low, high), values, 0.0).astype(BF16)
        cot_own[at, :] = jnp.where(row_mask(own_low, own_high), values, 0.0).astype(BF16)
        own[at, :] = jnp.where(row_mask(own_low, own_high), jnp.ones((WIN, QUAD), F32), 0.0)
        return carry

    lax.fori_loop(0, WINDOWS, place, 0, unroll=4)
    gain, shift = norms[2:3], norms[3:4]

    def before(i, carry):
        at = tile_at(i)
        values = x_in[at, :].astype(F32) + mm(mixed_in[at, :], w_all[:, 3 * D : 4 * D])
        middle[at, :] = values
        unit, _ = normalized(values)
        low = unit * gain + shift
        normed[at, :] = low.astype(BF16)
        normed_own[at, :] = (low * own[at, 0:1]).astype(BF16)
        return carry

    lax.fori_loop(0, WROWS // TILE, before, 0)
    wait_all(first_copy)
    for i in range(WROWS // TILE):
        at = slice(i * TILE, (i + 1) * TILE)
        branch, back = feed_rows(at, up[0], down[0], normed, cot, hidden, pre)
        total[at, :] = middle[at, :] + branch
        grad[at, :] = back
    feed_grads(direct, info, 0, normed_own, cot_own, hidden, pre, ext, grads)


def feed_rest_kernel(direct, info, *refs):
    middle, total_in, grad_in, normed, normed_own, cot, cot_own, own = refs[:8]
    mixed_in, norms, w_all = refs[8:11]
    pieces, refs = (refs[11:19], refs[19:]) if direct else (refs[11:13], refs[13:])
    out, grad_middle, grad_mixed, grad_norms = refs[:4]
    grads, refs = (refs[4:6], refs[6:]) if direct else (refs[4:7], refs[7:])
    up, down, ext, total, grad, grad_own, hidden, pre, sems = refs
    if direct:
        pairs = feed_pieces(info, pieces, up, down)
    else:
        pairs = [(pieces[0].at[1:CHUNKS], up), (pieces[1].at[1:CHUNKS], down)]
    wait_all(copy_all(pairs, sems))
    block = D // 8
    gain = norms[2:3]
    for c in range(CHUNKS - 1):
        for i in range(WROWS // TILE):
            at = slice(i * TILE, (i + 1) * TILE)
            branch, back = feed_rows(at, up[c], down[c], normed, cot, hidden, pre)
            total[at, :] = (total if c else total_in)[at, :] + branch
            grad[at, :] = (grad if c else grad_in)[at, :] + back
        feed_grads(direct, info, c * 2 * block, normed_own, cot_own, hidden, pre, ext, grads)
    grad_norms[...] = jnp.zeros(grad_norms.shape, F32)

    def after(i, carry):
        at = tile_at(i)
        unit, scale = normalized(middle[at, :])
        part = grad[at, :]
        masked = part * own[at, 0:1]
        grad_norms[0:1] += jnp.sum(masked * unit, axis=0, keepdims=True)
        grad_norms[1:2] += jnp.sum(masked, axis=0, keepdims=True)
        result = cot[at, :].astype(F32) + norm_back(part * gain, unit, scale)
        grad_middle[at, :] = result
        low = result.astype(BF16)
        grad_mixed[at, :] = mm_right(low, w_all[:, 3 * D : 4 * D]).astype(BF16)
        grad_own[at, :] = (result * own[at, 0:1]).astype(BF16)
        return carry

    lax.fori_loop(0, WROWS // TILE, after, 0)
    grad_out = mm_left(mixed_in[...], grad_own[...])
    if direct:
        ext[0:D, :] = grad_out
        first = (CHUNKS - 1) * 2 * block
        for partner in range(8):
            for k in range(CHUNKS):
                row = pl.multiple_of(((info[9] ^ partner) * CHUNKS + (info[10] ^ k)) * 16, 16)
                grads[partner & 1][partner >> 1, first + 16 * k : first + 16 * (k + 1), :] = ext[
                    pl.ds(row, 16), :
                ].astype(BF16)
    else:
        grads[2][...] = grad_out
    unplace(info, total, ext, out)


def unplace(info, values, ext, out):
    def back(w, carry):
        row, low, high, _, _, _ = window_place(info, w)
        at = pl.ds(pl.multiple_of(w * WIN, WIN), WIN)
        place = pl.ds(row, WIN)
        ext[place, :] = jnp.where(row_mask(low, high), values[at, :], ext[place, :])
        return carry

    lax.fori_loop(0, WINDOWS, back, 0, unroll=4)
    out[...] = ext[HALO : HALO + ROWS].astype(BF16)


def back_kernel(
    direct, info, x_in, qkv, probs_in, grad_mixed, grad_middle, w_qkv, norms, grad_norms, *refs
):
    out, refs = refs[0], refs[1:]
    if direct:
        (keep, send), refs = refs[:2], refs[2:]
    else:
        w_grad, refs = refs[0], refs[1:]
    ext, normed, grad_qkv, result, gains, grad_w, own = refs
    masks = head_masks()
    lane = lax.broadcasted_iota(jnp.int32, (1, QUAD), 1) // HEAD_DIM

    def attend_back(w, carry):
        at = window_at(w)
        own[at, :] = jnp.where(
            row_mask(*window_place(info, w)[3:5]), jnp.ones((WIN, QUAD), F32), 0.0
        )
        quads = range(D // QUAD)
        cols = [slice(quad * QUAD, (quad + 1) * QUAD) for quad in quads]
        cols_key = [slice(D + quad * QUAD, D + (quad + 1) * QUAD) for quad in quads]
        cols_value = [slice(2 * D + quad * QUAD, 2 * D + (quad + 1) * QUAD) for quad in quads]
        grad_out = [spread(grad_mixed[at, c], masks) for c in cols]
        grad_probs = [mm_right(qkv[at, c], g) for c, g in zip(cols_value, grad_out)]
        low = [probs_in[at, c] for c in cols]
        probs = [p.astype(F32) for p in low]
        delta = [jnp.sum(p * g, axis=0, keepdims=True) for p, g in zip(probs, grad_probs)]
        grad_scores = [
            (p * (g - d) * HEAD_DIM**-0.5).astype(BF16)
            for p, g, d in zip(probs, grad_probs, delta)
        ]
        grad_value = [mm(p, g) for p, g in zip(low, grad_out)]
        grad_query = [mm_left(g, qkv[at, c]) for g, c in zip(grad_scores, cols_key)]
        grad_key = [mm(g, spread(qkv[at, c], masks)) for g, c in zip(grad_scores, cols)]
        for quad in quads:
            grad_qkv[at, cols_value[quad]] = grad_value[quad].astype(BF16)
            grad_qkv[at, cols_key[quad]] = grad_key[quad].astype(BF16)
            grad_qkv[at, cols[quad]] = gathered(grad_query[quad], lane).astype(BF16)
        return carry

    lax.fori_loop(0, WINDOWS, attend_back, 0, unroll=4)
    gain, shift = norms[0:1], norms[1:2]
    gains[...] = jnp.zeros(gains.shape, F32)

    def after(i, carry):
        at = tile_at(i)
        unit, scale = normalized(x_in[at, :].astype(F32))
        mask = own[at, 0:1]
        normed[at, :] = ((unit * gain + shift) * mask).astype(BF16)
        part = mm_right(grad_qkv[at, :], w_qkv[:, : 3 * D])
        masked = part * mask
        gains[0:1] += jnp.sum(masked * unit, axis=0, keepdims=True)
        gains[1:2] += jnp.sum(masked, axis=0, keepdims=True)
        result[at, :] = grad_middle[at, :] + norm_back(part * gain, unit, scale)
        return carry

    lax.fori_loop(0, WROWS // TILE, after, 0)
    gains[2:4] = grad_norms[0:2]
    for part in range(3):
        cols = slice(part * D, (part + 1) * D)
        grad_w[:, cols] = mm_left(normed[...], grad_qkv[:, cols])
    grad_w[:, 3 * D :] = jnp.transpose(gains[...])
    if direct:
        count = keep.shape[1]
        for partner in range(8):
            target = send if partner & 1 else keep
            for k in range(count):
                row = pl.multiple_of(((info[9] ^ partner) * count + (info[10] ^ k)) * 16, 16)
                target[partner >> 1, k] = grad_w[pl.ds(row, 16), :].astype(BF16)
    else:
        w_grad[...] = grad_w[...]
    unplace(info, result, ext, out)


ORDER = (0, 2, 4, 6, 1, 3, 5, 7)
CHIPS = [[0, 2, 4, 6], [1, 3, 5, 7]]
LIMIT = 20 * 1024 * 1024
SMALL = 8 * 1024 * 1024
SMEM = pl.BlockSpec(memory_space=pltpu.SMEM)
VMEM = pl.BlockSpec(memory_space=pltpu.VMEM)
ANY = pl.BlockSpec(memory_space=pl.ANY)


def near_core(array):
    return pltpu.with_memory_space_constraint(array, pltpu.VMEM)


def far_core(array):
    return pltpu.with_memory_space_constraint(array, pltpu.HBM)


def run_kernel(body, out_shape, scratch, flops, info, *operands):
    specs = [ANY if isinstance(a, list) else VMEM for a in operands]
    operands = [a[0] if isinstance(a, list) else near_core(a) for a in operands]
    moved = sum(a.size * a.dtype.itemsize for a in operands)
    return pl.pallas_call(
        body,
        out_shape=out_shape,
        in_specs=[SMEM] + specs,
        out_specs=[VMEM] * len(out_shape),
        scratch_shapes=scratch,
        cost_estimate=pl.CostEstimate(
            flops=flops, bytes_accessed=moved, transcendentals=flops // 1024
        ),
        compiler_params=pltpu.CompilerParams(vmem_limit_bytes=LIMIT),
    )(info, *operands)


def swap(array, axis, bit):
    return lax.ppermute(array, axis, [(i, i ^ bit) for i in range(lax.axis_size(axis))])


def together(*values):
    return lax.optimization_barrier(values)


def along_seq(shard):
    return [swap(shard, "seq", k) for k in (1, 2, 3)]


def along_plane(column):
    return [swap(column, "dp", partner) for partner in (2, 4, 6)]


def along_core(pieces):
    return [swap(piece, "dp", 1) for piece in pieces]


def add_parts(own, parts):
    return own.astype(F32) + sum(part.astype(F32) for part in parts)


def shape(dims, kind):
    return pltpu.VMEM(dims, kind)


def per_device(
    tokens,
    cotangent,
    w_qkv,
    w_out,
    w_up,
    w_down,
    norm1_gain,
    norm1_shift,
    norm2_gain,
    norm2_shift,
    clip_steps,
    window_shifts,
):
    n_dp, n_seq = lax.axis_size("dp"), lax.axis_size("seq")
    share = w_qkv.shape[0]
    direct = n_dp == 8 and share % 16 == 0
    info = jnp.concatenate(
        [
            clip_steps.reshape(3),
            window_shifts.reshape(6),
            lax.axis_index("dp").reshape(1).astype(jnp.int32),
            lax.axis_index("seq").reshape(1).astype(jnp.int32),
        ]
    )
    width = 4 * D + NORMS
    vectors = (norm1_gain, norm1_shift, norm2_gain, norm2_shift)
    if direct:
        with_near, first, with_far, second, up_near, up_far = pl.pallas_call(
            prepare_kernel,
            out_shape=[
                jax.ShapeDtypeStruct((share, width + 2 * D), BF16),
                jax.ShapeDtypeStruct((share, width), BF16),
                jax.ShapeDtypeStruct((share, width + 2 * D), BF16),
                jax.ShapeDtypeStruct((2 * w_up.shape[0] + 5 * share, D), BF16),
                jax.ShapeDtypeStruct((2 * w_up.shape[0] + HALO, D), BF16),
                jax.ShapeDtypeStruct((2 * w_up.shape[0] + HALO, D), BF16),
            ],
            in_specs=[ANY] * 10,
            out_specs=[VMEM] * 6,
            scratch_shapes=[
                pltpu.VMEM((4, 1, share), BF16),
                pltpu.SemaphoreType.DMA((26,)),
            ],
            compiler_params=pltpu.CompilerParams(vmem_limit_bytes=LIMIT),
        )(
            *[
                far_core(a)
                for a in (tokens, cotangent, w_qkv, w_out, w_up, w_down.T)
                + tuple(v.reshape(1, -1) for v in vectors)
            ]
        )
        block = w_up.shape[0]
        own_x, own_y, near, middle, far = together(
            swap(second, "dp", 2),
            swap(second, "dp", 4),
            swap(with_near, "seq", 1),
            swap(first, "seq", 2),
            swap(with_far, "seq", 3),
        )
        column = jnp.stack([near[:, :width], middle, far[:, :width]])
        column, second = together(column, second)
        first_half = lax.all_gather(column, "dp", axis_index_groups=CHIPS)
        first_half, own_d, *rest = together(
            first_half,
            swap(second, "dp", 6),
            swap(up_near, "seq", 1),
            swap(second[: 2 * block], "seq", 2),
            swap(up_far, "seq", 3),
        )
        second_own = jnp.stack([second, own_x, own_y, own_d])
        near_cot, far_cot = rest[0], rest[2]
        rest = [rest[0][: 2 * block], rest[1], rest[2][: 2 * block]]
        rest = jnp.stack(rest)
        first_half, rest, second_own = together(first_half, rest, second_own)
        second_own = [second_own, *along_core([second_own])]
        first_all = [first_half, *along_core([first_half]), *second_own]
        second_plane = along_plane(rest)
    else:
        norms = jnp.pad(jnp.stack(vectors, axis=1), ((0, 0), (0, NORMS - 4)))
        first = jnp.concatenate([w_qkv, w_out, norms], axis=1)
        both = jnp.stack([tokens, cotangent])
        head, tail = both[:, :HALO], both[:, ROWS - HALO :]
        odd = lax.axis_index("seq") % 2 == 1
        first_all = [lax.all_gather(first, ("dp", "seq"), axis=0, tiled=True)]
        up_all = lax.all_gather(lax.all_gather(w_up, "dp", axis=0, tiled=True), "seq", axis=0)
        down_all = lax.all_gather(lax.all_gather(w_down.T, "dp", axis=0, tiled=True), "seq", axis=0)
        second_own = second_all = [up_all, down_all]
        from_left = lax.ppermute(tail, "seq", [(i, i + 1) for i in range(n_seq - 1)])
        from_right = lax.ppermute(head, "seq", [(i + 1, i) for i in range(n_seq - 1)])
        near, near_cot = jnp.where(odd, from_left, from_right)
        far, far_cot = jnp.where(odd, from_right, from_left)

    def in_hbm(arrays):
        return [[a] for a in arrays]

    x, qkv, mixed, probs, w_all, norms_all = run_kernel(
        functools.partial(attention_kernel, direct),
        [
            shape((WROWS, D), BF16),
            shape((WROWS, 3 * D), BF16),
            shape((WROWS, D), BF16),
            shape((WROWS, D), BF16),
            shape((D, width), BF16),
            shape((8, D), F32),
        ],
        [
            pltpu.VMEM((ROWS + 2 * HALO, D), F32),
            pltpu.VMEM((ROWS, D), BF16),
            pltpu.VMEM((2, HALO, D), BF16),
            pltpu.SemaphoreType.DMA((69,)),
        ],
        2 * WROWS * D * 3 * D * 2,
        info,
        *in_hbm((tokens, near, far, *first_all)),
    )
    if direct:
        grads_shape = [shape((4, 2 * block, D), BF16)] * 2
    else:
        grads_shape = [shape((1, D, CHUNK), F32)] * 2
    *state, keep, send = run_kernel(
        functools.partial(feed_first_kernel, direct),
        [shape((WROWS, D), F32)] * 3
        + [shape((WROWS, D), BF16)] * 4
        + [shape((WROWS, QUAD), F32), *grads_shape],
        [
            pltpu.VMEM((1, D, CHUNK), BF16),
            pltpu.VMEM((1, D, CHUNK), BF16),
            pltpu.VMEM((ROWS + 2 * HALO, D), F32),
            pltpu.VMEM((WROWS, CHUNK), BF16),
            pltpu.VMEM((WROWS, CHUNK), BF16),
            pltpu.VMEM((ROWS, D), BF16),
            pltpu.VMEM((2, HALO, D), BF16),
            pltpu.SemaphoreType.DMA((19,)),
        ],
        2 * WROWS * D * (6 * CHUNK + D),
        info,
        *in_hbm((cotangent, near_cot, far_cot)),
        x,
        mixed,
        norms_all,
        w_all,
        *in_hbm(second_own),
    )
    if direct:
        *second_plane, total = together(*second_plane, state[1])
        state[1] = total
        second_plane = [rest, *second_plane]
        second_all = second_plane + along_core(second_plane)
        own_pair, *low = add_slots(keep, *along_core([send]))
        *low, state[1] = together(*low, state[1])
        own_parts = [swap(part, "dp", 2 * m + 2) for m, part in enumerate(low)]
        extra = (CHUNKS - 1) * 2 * block
        grads_shape = [shape((4, extra + n_seq * share, D), BF16)] * 2
    else:
        first_grads = [keep, send]
        grads_shape = [shape((CHUNKS - 1, D, CHUNK), F32)] * 2 + [shape((D, D), F32)]
    out, grad_middle, grad_mixed, grad_norms, *grads = run_kernel(
        functools.partial(feed_rest_kernel, direct),
        [
            jax.ShapeDtypeStruct((ROWS, D), BF16),
            shape((WROWS, D), F32),
            shape((WROWS, D), BF16),
            shape((8, D), F32),
            *grads_shape,
        ],
        [
            pltpu.VMEM((CHUNKS - 1, D, CHUNK), BF16),
            pltpu.VMEM((CHUNKS - 1, D, CHUNK), BF16),
            pltpu.VMEM((ROWS + 2 * HALO, D), F32),
            pltpu.VMEM((WROWS, D), F32),
            pltpu.VMEM((WROWS, D), F32),
            pltpu.VMEM((WROWS, D), BF16),
            pltpu.VMEM((WROWS, CHUNK), BF16),
            pltpu.VMEM((WROWS, CHUNK), BF16),
            pltpu.SemaphoreType.DMA((16,)),
        ],
        2 * WROWS * D * (18 * CHUNK + 2 * D),
        info,
        *state,
        mixed,
        norms_all,
        w_all,
        *in_hbm(second_all),
    )
    if direct:
        keep, send, *own_parts = together(*grads, *own_parts)
        pair, *low = add_slots(keep, *along_core([send]))
        *low, grad_mixed = together(*low, grad_mixed)
        parts = [swap(part, "dp", 2 * m + 2) for m, part in enumerate(low)]
        grads_shape = [shape((4, n_seq, share, 3 * D + NORMS), BF16)] * 2
    else:
        grads_up, grads_down = [
            jnp.concatenate([a, b], axis=0) for a, b in zip(first_grads, grads[:2])
        ]
        grad_up = lax.psum_scatter(grads_up, "seq", scatter_dimension=0)
        grad_up = lax.psum_scatter(grad_up, "dp", scatter_dimension=0, tiled=True)
        grad_down = lax.psum_scatter(grads_down, "seq", scatter_dimension=0)
        grad_down = lax.psum_scatter(grad_down, "dp", scatter_dimension=0, tiled=True).T
        grad_out = lax.psum_scatter(grads[2], ("dp", "seq"), scatter_dimension=0, tiled=True)
        grads_shape = [shape((D, 3 * D + NORMS), F32)]
    tokens_grad, *grads = run_kernel(
        functools.partial(back_kernel, direct),
        [jax.ShapeDtypeStruct((ROWS, D), BF16), *grads_shape],
        [
            pltpu.VMEM((ROWS + 2 * HALO, D), F32),
            pltpu.VMEM((WROWS, D), BF16),
            pltpu.VMEM((WROWS, 3 * D), BF16),
            pltpu.VMEM((WROWS, D), F32),
            pltpu.VMEM((NORMS, D), F32),
            pltpu.VMEM((D, 3 * D + NORMS), F32),
            pltpu.VMEM((WROWS, QUAD), F32),
        ],
        2 * WROWS * D * (6 * D + 3 * D),
        info,
        x,
        qkv,
        probs,
        grad_mixed,
        grad_middle,
        w_all,
        norms_all,
        grad_norms,
    )
    if direct:
        sends = [grads[1][m] for m in range(4)]
        from_core = along_core(sends)
        keep, *parts = together(grads[0], *from_core, *parts)
        from_core, parts = parts[:4], parts[4:]
        first_pair, *first_low = add_pairs(keep, from_core)
        rows = [(slice(2 * block * k, 2 * block * (k + 1)),) for k in range(CHUNKS - 1)]
        out_rows = [(slice(extra + share * k, extra + share * (k + 1)),) for k in range(n_seq)]
        top, bottom = (slice(0, 2 * block),), (slice(2 * block, 2 * block + share),)
        plan = [[(slice(None), out_rows[0])]]
        plan += [[(top, r), (bottom, o)] for r, o in zip(rows, out_rows[1:])]
        sizes = [((share, D), F32)] + [((2 * block + share, D), BF16)] * (n_seq - 1)
        out_own, *low = add(plan, sizes, pair, *parts)
        first = [swap(part, "dp", 2 * m + 2) for m, part in enumerate(first_low)]
        second = [swap(low[1], "seq", 2), swap(low[2], "seq", 3)]
        near_low, x0, x1, x2 = together(low[0], *first)
        first_own, *first_low = add_slots(first_pair, x0, x1, x2)
        first_parts = [swap(part, "seq", k + 1) for k, part in enumerate(first_low)]
        second.append(swap(near_low, "seq", 1))
        top, bottom = (slice(0, block),), (slice(block, 2 * block),)
        everything = slice(None)
        grad_up, grad_down = add(
            [[(everything, top)], [(everything, bottom)]],
            [((block, D), F32)] * 2,
            own_pair,
            *own_parts,
            *second,
        )
        grad_down = grad_down.T
        (grad_out,) = add_tail(out_own, second, 2 * block)
        w_qkv_grad, *norm_grads = finish_first(first_own, first_parts)
        norm_grads = [grad.reshape(share) for grad in norm_grads]
    else:
        first_sum = lax.psum_scatter(grads[0], ("dp", "seq"), scatter_dimension=0, tiled=True)
        w_qkv_grad = first_sum[:, : 3 * D]
        norm_grads = [first_sum[:, 3 * D + i] for i in range(4)]
    return (
        out,
        tokens_grad,
        w_qkv_grad,
        grad_out,
        grad_up,
        grad_down,
        *norm_grads,
    )


def solution(mesh):
    rows = P(("dp", "seq"), None)
    vector = P(("dp", "seq"))
    return jax.shard_map(
        per_device,
        mesh=mesh,
        in_specs=(
            rows,
            rows,
            rows,
            rows,
            P("dp", "seq"),
            P("seq", "dp"),
            vector,
            vector,
            vector,
            vector,
            P("dp", None),
            P("dp", None, None),
        ),
        out_specs=(
            rows,
            rows,
            rows,
            rows,
            P("dp", "seq"),
            P("seq", "dp"),
            vector,
            vector,
            vector,
            vector,
        ),
        check_vma=False,
    )
```

```python
import functools

import jax
import jax.numpy as jnp
from jax import lax
from jax.experimental import pallas as pl
from jax.experimental.pallas import tpu as pltpu
from jax.sharding import PartitionSpec as P

D = 512
HEADS = 16
HEAD_DIM = D // HEADS
FF = 2048
FREQ = 8
STEPS_DEV = 88
HALO = 4 * FREQ
ROWS = STEPS_DEV * FREQ
WIN = 4 * FREQ
WINDOWS = STEPS_DEV // 4 + 2
WROWS = WINDOWS * WIN
TILE = 768
QUAD = 128
NORMS = 128
CHUNK = 512
CHUNKS = FF // CHUNK
epsilon = 1e-06
F32 = jnp.float32
BF16 = jnp.bfloat16


def mm(left, right):
    return jnp.dot(left, right, preferred_element_type=F32)


def mm_right(left, right):
    return lax.dot_general(left, right, (((1,), (1,)), ((), ())), preferred_element_type=F32)


def mm_left(left, right):
    return lax.dot_general(left, right, (((0,), (0,)), ((), ())), preferred_element_type=F32)


def window_place(info, w):
    lead, mid, trail = info[0], info[1], info[2]
    seq = info[10]
    base = seq * STEPS_DEV
    n_lead = lead // 4 + 1
    n_mid = mid // 4 + 1
    index = jnp.where(seq == 0, 0, base // 4 + 1) + w
    in_mid = index >= n_lead
    in_trail = index >= n_lead + n_mid
    before = jnp.where(in_trail, n_lead + n_mid, jnp.where(in_mid, n_lead, 0))
    start = jnp.where(in_trail, lead + mid, jnp.where(in_mid, lead, 0))
    steps = jnp.where(in_trail, trail, jnp.where(in_mid, mid, lead))
    shift_time = jnp.where(in_trail, info[7], jnp.where(in_mid, info[5], info[3]))
    shift_freq = jnp.where(in_trail, info[8], jnp.where(in_mid, info[6], info[4]))
    first = start - 4 + shift_time + 4 * (index - before)
    here = first < base + STEPS_DEV
    low = jnp.clip(start - first, 0, 4)
    high = jnp.where(here, jnp.clip(start + steps - first, 0, 4), 0)
    own_low = jnp.clip(base - first, 0, 4)
    own_high = jnp.clip(base + STEPS_DEV - first, 0, 4)
    row = jnp.clip(first - base + 4, 0, STEPS_DEV + 4) * FREQ
    row = pl.multiple_of(row, FREQ)
    return (
        row,
        low * FREQ,
        high * FREQ,
        jnp.maximum(low, own_low) * FREQ,
        jnp.minimum(high, own_high) * FREQ,
        shift_freq,
    )


def window_at(w):
    return pl.ds(pl.multiple_of(w * WIN, WIN), WIN)


def tile_at(i):
    return pl.ds(pl.multiple_of(i * TILE, TILE), TILE)


def row_mask(low, high):
    index = lax.broadcasted_iota(jnp.int32, (WIN, 1), 0)
    return (index >= low) & (index < high)


def copy_all(pairs, sems, first=0):
    copies = [
        pltpu.make_async_copy(source, target, sems.at[first + i])
        for i, (source, target) in enumerate(pairs)
    ]
    for copy in copies:
        copy.start()
    return copies


def wait_all(copies):
    for copy in copies:
        copy.wait()


def edge_copies(rows, near, far, ext_low, halos):
    pairs = [
        (rows.at[0:HALO, :], ext_low.at[0:HALO, :]),
        (rows.at[ROWS - 2 * HALO :, :], ext_low.at[HALO:, :]),
    ]
    for i, parts in enumerate((near, far)):
        size = HALO // len(parts)
        pairs += [
            (part, halos.at[i, j * size : (j + 1) * size, :]) for j, part in enumerate(parts)
        ]
    return pairs


def pad_edges(info, ext, ext_low, halos):
    ext[HALO : 2 * HALO] = ext_low[0:HALO].astype(F32)
    ext[ROWS - HALO : ROWS + HALO] = ext_low[HALO:].astype(F32)
    odd = info[10] % 2 == 1
    for i, is_left in enumerate((odd, jnp.logical_not(odd))):
        at = pl.multiple_of(jnp.where(is_left, 0, HALO + ROWS), HALO)
        ext[pl.ds(at, HALO), :] = halos[i].astype(F32)


EDGES = (0, WINDOWS - 2, WINDOWS - 1)


def place_rows(info, w, ext, out):
    row, low, high, _, _, _ = window_place(info, w)
    values = jnp.where(row_mask(low, high), ext[pl.ds(row, WIN), :], 0.0)
    out[window_at(w), :] = values.astype(BF16)


def place_cotangent(info, w, ext, cot, cot_own):
    row, low, high, own_low, own_high, _ = window_place(info, w)
    values = ext[pl.ds(row, WIN), :]
    cot[window_at(w), :] = jnp.where(row_mask(low, high), values, 0.0).astype(BF16)
    cot_own[window_at(w), :] = jnp.where(row_mask(own_low, own_high), values, 0.0).astype(BF16)


def layout_kernel(info, tokens, cotangent, x_out, cot, cot_own, own, ext, stage, sems):
    copies = copy_all([(tokens, stage.at[0]), (cotangent, stage.at[1])], sems)
    for edge in (slice(0, HALO), slice(HALO + ROWS, 2 * HALO + ROWS)):
        ext[edge, :] = jnp.zeros((HALO, D), F32)
    copies[0].wait()
    ext[HALO : HALO + ROWS] = stage[0].astype(F32)

    def tokens_step(w, carry):
        place_rows(info, w, ext, x_out)
        return carry

    lax.fori_loop(0, WINDOWS, tokens_step, 0, unroll=4)
    copies[1].wait()
    ext[HALO : HALO + ROWS] = stage[1].astype(F32)

    def cotangent_step(w, carry):
        place_cotangent(info, w, ext, cot, cot_own)
        mask = row_mask(*window_place(info, w)[3:5])
        own[window_at(w), :] = jnp.where(mask, jnp.ones((WIN, QUAD), F32), 0.0)
        return carry

    lax.fori_loop(0, WINDOWS, cotangent_step, 0, unroll=4)


def normalized(values):
    mean = jnp.mean(values, axis=-1, keepdims=True)
    centered = values - mean
    variance = jnp.mean(centered * centered, axis=-1, keepdims=True)
    scale = lax.rsqrt(variance + epsilon)
    return centered * scale, scale


def norm_back(grad, unit, scale):
    mean_one = jnp.mean(grad, axis=-1, keepdims=True)
    mean_two = jnp.mean(grad * unit, axis=-1, keepdims=True)
    return scale * (grad - mean_one - unit * mean_two)


def head_masks():
    lane = lax.broadcasted_iota(jnp.int32, (1, QUAD), 1) // HEAD_DIM
    return [(lane == h).astype(BF16) for h in range(QUAD // HEAD_DIM)]


def spread(block, masks):
    return jnp.concatenate([block * mask for mask in masks], axis=0)


def gathered(product, lane):
    parts = [product[h * WIN : (h + 1) * WIN] for h in range(QUAD // HEAD_DIM)]
    return jnp.where(
        lane < 1, parts[0], jnp.where(lane < 2, parts[1], jnp.where(lane < 3, parts[2], parts[3]))
    )


def sum_kernel(plan, *refs):
    ins, outs = refs[: -len(plan)], refs[-len(plan) :]
    for out, pieces in zip(outs, plan):
        for target, source in pieces:
            value = ins[0][source].astype(F32)
            for part in ins[1:]:
                value = value + part[source].astype(F32)
            out[target] = value.astype(out.dtype)


def add(plan, shapes, *operands):
    return pl.pallas_call(
        functools.partial(sum_kernel, plan),
        out_shape=[jax.ShapeDtypeStruct(*s) for s in shapes],
        in_specs=[VMEM] * len(operands),
        out_specs=[VMEM] * len(shapes),
        compiler_params=pltpu.CompilerParams(vmem_limit_bytes=SMALL),
    )(*[near_core(a) for a in operands])


def pair_kernel(keep, *refs):
    for m, (part, out) in enumerate(zip(refs[:4], refs[4:])):
        out[...] = (keep[m].astype(F32) + part[...].astype(F32)).astype(out.dtype)


def add_pairs(keep, parts):
    slot = keep.shape[1:]
    return pl.pallas_call(
        pair_kernel,
        out_shape=[jax.ShapeDtypeStruct(slot, kind) for kind in (F32, BF16, BF16, BF16)],
        in_specs=[VMEM] * 5,
        out_specs=[VMEM] * 4,
        compiler_params=pltpu.CompilerParams(vmem_limit_bytes=SMALL),
    )(*[near_core(a) for a in (keep, *parts)])


def chunks_kernel(keep_first, keep_rest, keep_out, first, rest, out, *refs):
    own, near, pair, *low = refs
    block, share = keep_first.shape[1], keep_out.shape[1] // CHUNKS

    def sums(slot, k):
        a, b, row = (keep_first, first, 0) if k == 0 else (keep_rest, rest, (k - 1) * block)
        rows, out_rows = slice(row, row + block), slice(share * k, share * (k + 1))
        return (
            a[slot, rows].astype(F32) + b[slot, rows].astype(F32),
            keep_out[slot, out_rows].astype(F32) + out[slot, out_rows].astype(F32),
        )

    for slot in range(4):
        for k in range(CHUNKS):
            if k < 2:
                target, row = (own, near)[k].at[slot], 0
            else:
                target, row = ([pair] + low)[slot], (k - 2) * (block + share)
            one, two = sums(slot, k)
            target[row : row + block, :] = one.astype(target.dtype)
            target[row + block : row + block + share, :] = two.astype(target.dtype)


def add_chunks(keeps, parts):
    rows = keeps[0].shape[1] + keeps[2].shape[1] // CHUNKS
    shapes = [((4, rows, D), F32), ((4, rows, D), BF16), ((2 * rows, D), F32)]
    shapes += [((2 * rows, D), BF16)] * 3
    return pl.pallas_call(
        chunks_kernel,
        out_shape=[jax.ShapeDtypeStruct(*s) for s in shapes],
        in_specs=[VMEM] * 6,
        out_specs=[VMEM] * 6,
        compiler_params=pltpu.CompilerParams(vmem_limit_bytes=SMALL),
    )(*[near_core(a) for a in (*keeps, *parts)])


def finish_kernel(own, one, two, three, grad, *norm_grads):
    total = own[...] + (one[...].astype(F32) + two[...].astype(F32) + three[...].astype(F32))
    grad[...] = total[:, : 3 * D]
    rows = jnp.transpose(total[:, 3 * D :])
    for i, norm_grad in enumerate(norm_grads):
        norm_grad[...] = rows[i : i + 1]


def finish_first(own, parts):
    share = own.shape[0]
    shapes = [(share, 3 * D)] + [(1, share)] * 4
    return pl.pallas_call(
        finish_kernel,
        out_shape=[jax.ShapeDtypeStruct(dims, F32) for dims in shapes],
        in_specs=[VMEM] * (1 + len(parts)),
        out_specs=[VMEM] * len(shapes),
        compiler_params=pltpu.CompilerParams(vmem_limit_bytes=SMALL),
    )(*[near_core(a) for a in (own, *parts)])


def add_slots(*operands):
    slot = operands[0].shape[1:]
    plan = [[(slice(None), i)] for i in range(4)]
    return add(plan, [(slot, F32)] + [(slot, BF16)] * 3, *operands)


def prepare_kernel(tokens, cotangent, w_qkv, w_out, w_up, w_down, *refs):
    norms, (with_near, first, with_far, second, up_near, up_far, vectors, sems) = refs[:4], refs[4:]
    share, width = first.shape
    block = w_up.shape[0]
    odd = lax.axis_index("seq") % 2
    pairs = [(norm, vectors.at[i]) for i, norm in enumerate(norms)]
    for target in (with_near, first, with_far):
        pairs += [(w_qkv, target.at[:, : 3 * D]), (w_out, target.at[:, 3 * D : 4 * D])]
    for target, up_target, is_head in ((with_near, up_near, odd), (with_far, up_far, 1 - odd)):
        start = pl.multiple_of((1 - is_head) * (ROWS - HALO), HALO)
        for j in range(2):
            at = width + j * D
            rows = pl.ds(start + j * (HALO // 2), HALO // 2)
            pairs.append((tokens.at[rows, :], target.at[:, at : at + D]))
        pairs.append((cotangent.at[pl.ds(start, HALO), :], up_target.at[2 * block :, :]))
    for target in (second, up_near, up_far):
        pairs += [(w_up, target.at[0:block]), (w_down, target.at[block : 2 * block])]
    first_row = 2 * block
    for i, source in enumerate([w_qkv.at[:, j * D : (j + 1) * D] for j in range(3)] + [w_out]):
        pairs.append((source, second.at[first_row + share * i : first_row + share * (i + 1), :]))
    copies = copy_all(pairs, sems)
    wait_all(copies[: len(norms)])
    columns = jnp.concatenate(
        [vectors[i].astype(F32) for i in range(4)] + [jnp.zeros((NORMS - 4, share), F32)], axis=0
    )
    columns = jnp.transpose(columns).astype(BF16)
    for target in (with_near, first, with_far):
        target[:, 4 * D : width] = columns
    second[first_row + 4 * share :, :] = jnp.concatenate([columns] * (D // NORMS), axis=1)
    wait_all(copies[len(norms) :])


def attention_kernel(direct, info, rows, near, far, x_in, *refs):
    pieces, refs = (refs[:4], refs[4:]) if direct else (refs[:1], refs[1:])
    x_out, qkv_out, mixed_out, probs_out, w_out, norms_out, ext, edges, halos, sems = refs
    width = w_out.shape[1]
    near, far = [
        [a.at[:, width + j * D : width + (j + 1) * D] for j in range(2)] if direct else [a]
        for a in (near, far)
    ]
    edge_copy = copy_all(edge_copies(rows, near, far, edges, halos), sems)
    x_out[...] = x_in[...]
    if direct:
        count, share = pieces[0].shape[1] + 1, pieces[0].shape[2]
        for core, piece in enumerate(pieces[:2]):
            for chip in range(4):
                for k in range(1, count):
                    owner = (2 * chip + (info[9] % 2 ^ core)) * count + (info[10] ^ k)
                    at = pl.multiple_of(owner * share, share)
                    w_out[pl.ds(at, share), :] = piece[chip, k - 1]
        for i, partner in enumerate(ORDER):
            owner = (info[9] ^ partner) * count + info[10]
            at = pl.ds(pl.multiple_of(owner * share, share), share)
            for j in range(5):
                cols = min(D, width - j * D)
                row = D // 4 + j * share
                part = pieces[2 + i // 4][i % 4, row : row + share, 0:cols]
                w_out[at, j * D : j * D + cols] = part
    else:
        w_out[...] = pieces[0][...]
    wait_all(edge_copy)
    pad_edges(info, ext, edges, halos)
    for w in EDGES:
        place_rows(info, w, ext, x_out)
    norms_out[...] = jnp.transpose(w_out[:, 4 * D :].astype(F32))[:8]
    gain, shift = norms_out[0:1], norms_out[1:2]

    def project(i, carry):
        at = tile_at(i)
        unit, _ = normalized(x_out[at, :].astype(F32))
        low = (unit * gain + shift).astype(BF16)
        for part in range(3):
            cols = slice(part * D, (part + 1) * D)
            qkv_out[at, cols] = mm(low, w_out[:, cols]).astype(BF16)
        return carry

    lax.fori_loop(0, WROWS // TILE, project, 0)
    masks = head_masks()
    lane = lax.broadcasted_iota(jnp.int32, (1, QUAD), 1) // HEAD_DIM
    key_row = lax.broadcasted_iota(jnp.int32, (WIN, QUAD), 0)
    query_row = lax.broadcasted_iota(jnp.int32, (WIN, QUAD), 1) % WIN
    key_freq, query_freq = key_row % FREQ, query_row % FREQ

    def attend(w, carry):
        _, low, high, _, _, shift_freq = window_place(info, w)
        at = pl.ds(pl.multiple_of(w * WIN, WIN), WIN)
        key_group = (key_freq + 4 - shift_freq) >> 2
        query_group = (query_freq + 4 - shift_freq) >> 2
        allowed = (key_group == query_group) & (key_row >= low) & (key_row < high)
        quads = range(D // QUAD)
        raw = []
        for quad in quads:
            query = qkv_out[at, quad * QUAD : (quad + 1) * QUAD]
            key = qkv_out[at, D + quad * QUAD : D + (quad + 1) * QUAD]
            raw.append(mm_right(key, spread(query, masks)))
        scores = [jnp.where(allowed, r * HEAD_DIM**-0.5, -1e30) for r in raw]
        weights = [jnp.exp(s - jnp.max(s, axis=0, keepdims=True)) for s in scores]
        probs = [(p / jnp.sum(p, axis=0, keepdims=True)).astype(BF16) for p in weights]
        products = []
        for quad in quads:
            probs_out[at, quad * QUAD : (quad + 1) * QUAD] = probs[quad]
            value = qkv_out[at, 2 * D + quad * QUAD : 2 * D + (quad + 1) * QUAD]
            products.append(mm_left(probs[quad], value))
        for quad in quads:
            mixed = gathered(products[quad], lane).astype(BF16)
            mixed_out[at, quad * QUAD : (quad + 1) * QUAD] = mixed
        return carry

    lax.fori_loop(0, WINDOWS, attend, 0, unroll=12)


def gelu_parts(values):
    half_exp = jnp.exp(-0.5 * values * values)
    t = 1.0 / (1.0 + (0.3275911 * 0.7071067811865476) * jnp.abs(values))
    poly = t * (
        0.5 * 0.254829592
        + t
        * (
            0.5 * -0.284496736
            + t * (0.5 * 1.421413741 + t * (0.5 * -1.453152027 + t * (0.5 * 1.061405429)))
        )
    )
    tail = poly * half_exp
    return jnp.where(values >= 0, 1.0 - tail, tail), half_exp * 0.3989422804014327


def place_feed(info, pieces, up, down):
    block = D // 8
    for piece, partner in zip(pieces, ORDER):
        at = pl.ds(pl.multiple_of((info[9] ^ partner) * block, block), block)
        for c in range(up.shape[0]):
            up[c, at, :] = piece[c, 0:block, :]
            down[c, at, :] = piece[c, block : 2 * block, :]


def feed_rows(at, up, down, normed, cot, hidden, pre):
    values = mm(normed[at, :], up)
    grad_hidden = mm(cot[at, :], down)
    below, density = gelu_parts(values)
    hidden_low = (values * below).astype(BF16)
    grad_low = (grad_hidden * (below + values * density)).astype(BF16)
    hidden[at, :] = hidden_low
    pre[at, :] = grad_low
    return mm_right(hidden_low, down), mm_right(grad_low, up)


def feed_grads(direct, info, row, normed_own, cot_own, hidden, pre, space, refs):
    block = D // 8
    for i, product in enumerate(((normed_own, pre), (cot_own, hidden))):
        grad = mm_left(product[0][...], product[1][...])
        if not direct:
            refs[i][row // (2 * block)] = grad
            continue
        space[0:D, :] = grad
        for partner in range(8):
            at = pl.multiple_of((info[9] ^ partner) * block, block)
            first = row + i * block
            refs[partner & 1][partner >> 1, first : first + block, :] = space[
                pl.ds(at, block), :
            ].astype(BF16)


def feed_first_kernel(
    direct, info, rows, near, far, cot_in, cot_own_in, own, x_in, mixed_in, norms, w_all, *refs
):
    pieces, refs = refs[:2], refs[2:]
    middle, total, grad, normed, normed_own, cot, cot_own = refs[:7]
    grads, (up, down, ext, hidden, pre, edges, halos, sems) = refs[7:9], refs[9:]
    near, far = [[a.at[a.shape[0] - HALO :, :]] for a in (near, far)]
    edge_copy = copy_all(edge_copies(rows, near, far, edges, halos), sems)
    cot[...], cot_own[...] = cot_in[...], cot_own_in[...]
    if direct:
        own_pieces = [piece.at[m : m + 1] for piece in pieces for m in range(4)]
        place_feed(info, own_pieces, up, down)
    else:
        up[...], down[...] = pieces[0][0:1], pieces[1][0:1]
    wait_all(edge_copy)
    pad_edges(info, ext, edges, halos)
    for w in EDGES:
        place_cotangent(info, w, ext, cot, cot_own)
    gain, shift = norms[2:3], norms[3:4]

    def before(i, carry):
        at = tile_at(i)
        values = x_in[at, :].astype(F32) + mm(mixed_in[at, :], w_all[:, 3 * D : 4 * D])
        middle[at, :] = values
        unit, _ = normalized(values)
        low = unit * gain + shift
        normed[at, :] = low.astype(BF16)
        normed_own[at, :] = (low * own[at, 0:1]).astype(BF16)
        return carry

    lax.fori_loop(0, WROWS // TILE, before, 0)
    for i in range(WROWS // TILE):
        at = slice(i * TILE, (i + 1) * TILE)
        branch, back = feed_rows(at, up[0], down[0], normed, cot, hidden, pre)
        total[at, :] = middle[at, :] + branch
        grad[at, :] = back
    feed_grads(direct, info, 0, normed_own, cot_own, hidden, pre, ext, grads)


def feed_rest_kernel(direct, info, total_in, grad_in, normed, normed_own, cot, cot_own, *refs):
    pieces, refs = (refs[:8], refs[8:]) if direct else (refs[:2], refs[2:])
    total, grad, *grads, up, down, ext, hidden, pre = refs
    if direct:
        place_feed(info, pieces, up, down)
    else:
        up[...], down[...] = pieces[0][1:CHUNKS], pieces[1][1:CHUNKS]
    for c in range(CHUNKS - 1):
        for i in range(WROWS // TILE):
            at = slice(i * TILE, (i + 1) * TILE)
            branch, back = feed_rows(at, up[c], down[c], normed, cot, hidden, pre)
            total[at, :] = (total if c else total_in)[at, :] + branch
            grad[at, :] = (grad if c else grad_in)[at, :] + back
        feed_grads(direct, info, c * (D // 4), normed_own, cot_own, hidden, pre, ext, grads)


def feed_last_kernel(direct, info, middle, grad, cot, own, mixed_in, norms, w_all, *refs):
    grad_middle, grad_mixed, grad_norms, *grads, ext, grad_own = refs
    gain = norms[2:3]
    grad_norms[...] = jnp.zeros(grad_norms.shape, F32)
    for i in range(WROWS // TILE):
        at = slice(i * TILE, (i + 1) * TILE)
        unit, scale = normalized(middle[at, :])
        part = grad[at, :]
        masked = part * own[at, 0:1]
        grad_norms[0:1] += jnp.sum(masked * unit, axis=0, keepdims=True)
        grad_norms[1:2] += jnp.sum(masked, axis=0, keepdims=True)
        result = cot[at, :].astype(F32) + norm_back(part * gain, unit, scale)
        grad_middle[at, :] = result
        grad_mixed[at, :] = mm_right(result.astype(BF16), w_all[:, 3 * D : 4 * D]).astype(BF16)
        grad_own[at, :] = (result * own[at, 0:1]).astype(BF16)
    grad_out = mm_left(mixed_in[...], grad_own[...])
    if direct:
        ext[0:D, :] = grad_out
        share = grads[0].shape[1] // CHUNKS
        for partner in range(8):
            for k in range(CHUNKS):
                owner = (info[9] ^ partner) * CHUNKS + (info[10] ^ k)
                row = pl.multiple_of(owner * share, share)
                grads[partner & 1][partner >> 1, share * k : share * (k + 1), :] = ext[
                    pl.ds(row, share), :
                ].astype(BF16)
    else:
        grads[0][...] = grad_out


def finish_rows_kernel(info, total, x_in, grad_normed, grad_middle, norms, out, tokens_grad, ext):
    unplace(info, total, ext, out)
    unit, scale = normalized(x_in[...].astype(F32))
    grad_normed[...] = grad_middle[...] + norm_back(grad_normed[...] * norms[0:1], unit, scale)
    unplace(info, grad_normed, ext, tokens_grad)


def unplace(info, values, ext, out):
    def back(w, carry):
        row, low, high, _, _, _ = window_place(info, w)
        at = pl.ds(pl.multiple_of(w * WIN, WIN), WIN)
        place = pl.ds(row, WIN)
        ext[place, :] = jnp.where(row_mask(low, high), values[at, :], ext[place, :])
        return carry

    lax.fori_loop(0, WINDOWS, back, 0, unroll=4)
    out[...] = ext[HALO : HALO + ROWS].astype(BF16)


def back_kernel(
    direct, info, x_in, own, qkv, probs_in, grad_mixed, w_qkv, norms, grad_norms, *refs
):
    grad_normed, refs = refs[0], refs[1:]
    if direct:
        (keep, send), refs = refs[:2], refs[2:]
    else:
        w_grad, refs = refs[0], refs[1:]
    normed, grad_qkv, gains, grad_w = refs
    masks = head_masks()
    lane = lax.broadcasted_iota(jnp.int32, (1, QUAD), 1) // HEAD_DIM

    def attend_back(w, carry):
        at = window_at(w)
        quads = range(D // QUAD)
        cols = [slice(quad * QUAD, (quad + 1) * QUAD) for quad in quads]
        cols_key = [slice(D + quad * QUAD, D + (quad + 1) * QUAD) for quad in quads]
        cols_value = [slice(2 * D + quad * QUAD, 2 * D + (quad + 1) * QUAD) for quad in quads]
        grad_out = [spread(grad_mixed[at, c], masks) for c in cols]
        grad_probs = [mm_right(qkv[at, c], g) for c, g in zip(cols_value, grad_out)]
        low = [probs_in[at, c] for c in cols]
        probs = [p.astype(F32) for p in low]
        delta = [jnp.sum(p * g, axis=0, keepdims=True) for p, g in zip(probs, grad_probs)]
        grad_scores = [
            (p * (g - d) * HEAD_DIM**-0.5).astype(BF16)
            for p, g, d in zip(probs, grad_probs, delta)
        ]
        grad_value = [mm(p, g) for p, g in zip(low, grad_out)]
        grad_query = [mm_left(g, qkv[at, c]) for g, c in zip(grad_scores, cols_key)]
        grad_key = [mm(g, spread(qkv[at, c], masks)) for g, c in zip(grad_scores, cols)]
        for quad in quads:
            grad_qkv[at, cols_value[quad]] = grad_value[quad].astype(BF16)
            grad_qkv[at, cols_key[quad]] = grad_key[quad].astype(BF16)
            grad_qkv[at, cols[quad]] = gathered(grad_query[quad], lane).astype(BF16)
        return carry

    lax.fori_loop(0, WINDOWS, attend_back, 0, unroll=12)
    gain, shift = norms[0:1], norms[1:2]
    gains[...] = jnp.zeros(gains.shape, F32)

    def after(i, carry):
        at = tile_at(i)
        unit, _ = normalized(x_in[at, :].astype(F32))
        mask = own[at, 0:1]
        normed[at, :] = ((unit * gain + shift) * mask).astype(BF16)
        part = mm_right(grad_qkv[at, :], w_qkv[:, : 3 * D])
        masked = part * mask
        gains[0:1] += jnp.sum(masked * unit, axis=0, keepdims=True)
        gains[1:2] += jnp.sum(masked, axis=0, keepdims=True)
        grad_normed[at, :] = part
        return carry

    lax.fori_loop(0, WROWS // TILE, after, 0)
    gains[2:4] = grad_norms[0:2]
    for part in range(3):
        cols = slice(part * D, (part + 1) * D)
        grad_w[:, cols] = mm_left(normed[...], grad_qkv[:, cols])
    grad_w[:, 3 * D :] = jnp.transpose(gains[...])
    if direct:
        count = keep.shape[1]
        for partner in range(8):
            target = send if partner & 1 else keep
            for k in range(count):
                row = pl.multiple_of(((info[9] ^ partner) * count + (info[10] ^ k)) * 16, 16)
                target[partner >> 1, k] = grad_w[pl.ds(row, 16), :].astype(BF16)
    else:
        w_grad[...] = grad_w[...]


ORDER = (0, 2, 4, 6, 1, 3, 5, 7)
CHIPS = [[0, 2, 4, 6], [1, 3, 5, 7]]
LIMIT = 20 * 1024 * 1024
SMALL = 8 * 1024 * 1024
SMEM = pl.BlockSpec(memory_space=pltpu.SMEM)
VMEM = pl.BlockSpec(memory_space=pltpu.VMEM)
ANY = pl.BlockSpec(memory_space=pl.ANY)


def near_core(array):
    return pltpu.with_memory_space_constraint(array, pltpu.VMEM)


def far_core(array):
    return pltpu.with_memory_space_constraint(array, pltpu.HBM)


def run_kernel(body, out_shape, scratch, flops, info, *operands):
    specs = [ANY if isinstance(a, list) else VMEM for a in operands]
    operands = [a[0] if isinstance(a, list) else near_core(a) for a in operands]
    moved = sum(a.size * a.dtype.itemsize for a in operands)
    return pl.pallas_call(
        body,
        out_shape=out_shape,
        in_specs=[SMEM] + specs,
        out_specs=[VMEM] * len(out_shape),
        scratch_shapes=scratch,
        cost_estimate=pl.CostEstimate(
            flops=flops, bytes_accessed=moved, transcendentals=flops // 1024
        ),
        compiler_params=pltpu.CompilerParams(vmem_limit_bytes=LIMIT),
    )(info, *operands)


def swap(array, axis, bit):
    return lax.ppermute(array, axis, [(i, i ^ bit) for i in range(lax.axis_size(axis))])


def together(*values):
    return lax.optimization_barrier(values)


def along_seq(shard):
    return [swap(shard, "seq", k) for k in (1, 2, 3)]


def along_plane(column):
    return [swap(column, "dp", partner) for partner in (2, 4, 6)]


def along_core(pieces):
    return [swap(piece, "dp", 1) for piece in pieces]


def add_parts(own, parts):
    return own.astype(F32) + sum(part.astype(F32) for part in parts)


def shape(dims, kind):
    return pltpu.VMEM(dims, kind)


def per_device(
    tokens,
    cotangent,
    w_qkv,
    w_out,
    w_up,
    w_down,
    norm1_gain,
    norm1_shift,
    norm2_gain,
    norm2_shift,
    clip_steps,
    window_shifts,
):
    n_dp, n_seq = lax.axis_size("dp"), lax.axis_size("seq")
    share = w_qkv.shape[0]
    direct = n_dp == 8 and share % 16 == 0
    info = jnp.concatenate(
        [
            clip_steps.reshape(3),
            window_shifts.reshape(6),
            lax.axis_index("dp").reshape(1).astype(jnp.int32),
            lax.axis_index("seq").reshape(1).astype(jnp.int32),
        ]
    )
    width = 4 * D + NORMS
    vectors = (norm1_gain, norm1_shift, norm2_gain, norm2_shift)

    def in_hbm(arrays):
        return [[a] for a in arrays]

    x, cot, cot_own, own = run_kernel(
        layout_kernel,
        [shape((WROWS, D), BF16)] * 3 + [shape((WROWS, QUAD), F32)],
        [
            pltpu.VMEM((ROWS + 2 * HALO, D), F32),
            pltpu.VMEM((2, ROWS, D), BF16),
            pltpu.SemaphoreType.DMA((2,)),
        ],
        2 * WROWS * D * D,
        info,
        *in_hbm((tokens, cotangent)),
    )
    if direct:
        with_near, first, with_far, second, up_near, up_far = pl.pallas_call(
            prepare_kernel,
            out_shape=[
                jax.ShapeDtypeStruct((share, width + 2 * D), BF16),
                jax.ShapeDtypeStruct((share, width), BF16),
                jax.ShapeDtypeStruct((share, width + 2 * D), BF16),
                jax.ShapeDtypeStruct((2 * w_up.shape[0] + 5 * share, D), BF16),
                jax.ShapeDtypeStruct((2 * w_up.shape[0] + HALO, D), BF16),
                jax.ShapeDtypeStruct((2 * w_up.shape[0] + HALO, D), BF16),
            ],
            in_specs=[ANY] * 10,
            out_specs=[VMEM] * 6,
            scratch_shapes=[
                pltpu.VMEM((4, 1, share), BF16),
                pltpu.SemaphoreType.DMA((26,)),
            ],
            compiler_params=pltpu.CompilerParams(vmem_limit_bytes=LIMIT),
        )(
            *[
                far_core(a)
                for a in (tokens, cotangent, w_qkv, w_out, w_up, w_down.T)
                + tuple(v.reshape(1, -1) for v in vectors)
            ]
        )
        block = w_up.shape[0]
        own_x, own_y, near, middle, far, x, cot, cot_own, own = together(
            swap(second, "dp", 2),
            swap(second, "dp", 4),
            swap(with_near, "seq", 1),
            swap(first, "seq", 2),
            swap(with_far, "seq", 3),
            x,
            cot,
            cot_own,
            own,
        )
        column = jnp.stack([near[:, :width], middle, far[:, :width]])
        column, second = together(column, second)
        first_half = lax.all_gather(column, "dp", axis_index_groups=CHIPS)
        first_half, own_d, *rest = together(
            first_half,
            swap(second, "dp", 6),
            swap(up_near, "seq", 1),
            swap(second[: 2 * block], "seq", 2),
            swap(up_far, "seq", 3),
        )
        second_own = jnp.stack([second, own_x, own_y, own_d])
        near_cot, far_cot = rest[0], rest[2]
        rest = [rest[0][: 2 * block], rest[1], rest[2][: 2 * block]]
        rest = jnp.stack(rest)
        first_half, rest, second_own = together(first_half, rest, second_own)
        second_own = [second_own, *along_core([second_own])]
        first_all = [first_half, *along_core([first_half]), *second_own]
        second_plane = along_plane(rest)
    else:
        norms = jnp.pad(jnp.stack(vectors, axis=1), ((0, 0), (0, NORMS - 4)))
        first = jnp.concatenate([w_qkv, w_out, norms], axis=1)
        both = jnp.stack([tokens, cotangent])
        head, tail = both[:, :HALO], both[:, ROWS - HALO :]
        odd = lax.axis_index("seq") % 2 == 1
        first_all = [lax.all_gather(first, ("dp", "seq"), axis=0, tiled=True)]
        up_all = lax.all_gather(lax.all_gather(w_up, "dp", axis=0, tiled=True), "seq", axis=0)
        down_all = lax.all_gather(lax.all_gather(w_down.T, "dp", axis=0, tiled=True), "seq", axis=0)
        second_own = second_all = [up_all, down_all]
        from_left = lax.ppermute(tail, "seq", [(i, i + 1) for i in range(n_seq - 1)])
        from_right = lax.ppermute(head, "seq", [(i + 1, i) for i in range(n_seq - 1)])
        near, near_cot = jnp.where(odd, from_left, from_right)
        far, far_cot = jnp.where(odd, from_right, from_left)

    x, qkv, mixed, probs, w_all, norms_all = run_kernel(
        functools.partial(attention_kernel, direct),
        [
            shape((WROWS, D), BF16),
            shape((WROWS, 3 * D), BF16),
            shape((WROWS, D), BF16),
            shape((WROWS, D), BF16),
            shape((D, width), BF16),
            shape((8, D), F32),
        ],
        [
            pltpu.VMEM((ROWS + 2 * HALO, D), F32),
            pltpu.VMEM((3 * HALO, D), BF16),
            pltpu.VMEM((2, HALO, D), BF16),
            pltpu.SemaphoreType.DMA((6,)),
        ],
        2 * WROWS * D * 3 * D * 2,
        info,
        *in_hbm((tokens, near, far)),
        x,
        *first_all,
    )
    if direct:
        grads_shape = [shape((4, 2 * block, D), BF16)] * 2
    else:
        grads_shape = [shape((1, D, CHUNK), F32)] * 2
    *state, keep, send = run_kernel(
        functools.partial(feed_first_kernel, direct),
        [shape((WROWS, D), F32)] * 3
        + [shape((WROWS, D), BF16)] * 4
        + grads_shape,
        [
            pltpu.VMEM((1, D, CHUNK), BF16),
            pltpu.VMEM((1, D, CHUNK), BF16),
            pltpu.VMEM((ROWS + 2 * HALO, D), F32),
            pltpu.VMEM((WROWS, CHUNK), BF16),
            pltpu.VMEM((WROWS, CHUNK), BF16),
            pltpu.VMEM((3 * HALO, D), BF16),
            pltpu.VMEM((2, HALO, D), BF16),
            pltpu.SemaphoreType.DMA((4,)),
        ],
        2 * WROWS * D * (6 * CHUNK + D),
        info,
        *in_hbm((cotangent, near_cot, far_cot)),
        cot,
        cot_own,
        own,
        x,
        mixed,
        norms_all,
        w_all,
        *second_own,
    )
    if direct:
        *second_plane, total = together(*second_plane, state[1])
        state[1] = total
        second_plane = [rest, *second_plane]
        second_all = second_plane + along_core(second_plane)
        first_grads = [keep, send]
        extra = (CHUNKS - 1) * 2 * block
        grads_shape = [shape((4, extra, D), BF16)] * 2
        out_shape = [shape((4, n_seq * share, D), BF16)] * 2
    else:
        first_grads = [keep, send]
        grads_shape = [shape((CHUNKS - 1, D, CHUNK), F32)] * 2
        out_shape = [shape((D, D), F32)]
    middle, total, grad, normed, normed_own, cot, cot_own = state
    total, grad, *grads = run_kernel(
        functools.partial(feed_rest_kernel, direct),
        [shape((WROWS, D), F32)] * 2 + grads_shape,
        [
            pltpu.VMEM((CHUNKS - 1, D, CHUNK), BF16),
            pltpu.VMEM((CHUNKS - 1, D, CHUNK), BF16),
            pltpu.VMEM((D, D), F32),
            pltpu.VMEM((WROWS, CHUNK), BF16),
            pltpu.VMEM((WROWS, CHUNK), BF16),
        ],
        2 * WROWS * D * 18 * CHUNK,
        info,
        total,
        grad,
        normed,
        normed_own,
        cot,
        cot_own,
        *second_all,
    )
    if direct:
        from_core = along_core([first_grads[1], grads[1]])
    grad_middle, grad_mixed, grad_norms, *out_grads = run_kernel(
        functools.partial(feed_last_kernel, direct),
        [
            shape((WROWS, D), F32),
            shape((WROWS, D), BF16),
            shape((8, D), F32),
            *out_shape,
        ],
        [pltpu.VMEM((D, D), F32), pltpu.VMEM((WROWS, D), BF16)],
        2 * WROWS * D * 2 * D,
        info,
        middle,
        grad,
        cot,
        own,
        mixed,
        norms_all,
        w_all,
    )
    if direct:
        from_core = [*from_core, *along_core(out_grads[1:])]
        keeps, from_core = [first_grads[0], grads[0], out_grads[0]], together(*from_core)
        own_pair, to_near, pair, *low = add_chunks(keeps, from_core)
        to_near, *low, grad_mixed = together(to_near, *low, grad_mixed)
        parts = [swap(part, "dp", 2 * m + 2) for m, part in enumerate(low)]
        parts.append(swap(to_near, "seq", 1))
        grads_shape = [shape((4, n_seq, share, 3 * D + NORMS), BF16)] * 2
    else:
        grads_up, grads_down = [
            jnp.concatenate([a, b], axis=0) for a, b in zip(first_grads, grads)
        ]
        grad_up = lax.psum_scatter(grads_up, "seq", scatter_dimension=0)
        grad_up = lax.psum_scatter(grad_up, "dp", scatter_dimension=0, tiled=True)
        grad_down = lax.psum_scatter(grads_down, "seq", scatter_dimension=0)
        grad_down = lax.psum_scatter(grad_down, "dp", scatter_dimension=0, tiled=True).T
        grad_out = lax.psum_scatter(out_grads[0], ("dp", "seq"), scatter_dimension=0, tiled=True)
        grads_shape = [shape((D, 3 * D + NORMS), F32)]
    grad_normed, *grads = run_kernel(
        functools.partial(back_kernel, direct),
        [shape((WROWS, D), F32), *grads_shape],
        [
            pltpu.VMEM((WROWS, D), BF16),
            pltpu.VMEM((WROWS, 3 * D), BF16),
            pltpu.VMEM((NORMS, D), F32),
            pltpu.VMEM((D, 3 * D + NORMS), F32),
        ],
        2 * WROWS * D * (6 * D + 3 * D),
        info,
        x,
        own,
        qkv,
        probs,
        grad_mixed,
        w_all,
        norms_all,
        grad_norms,
    )
    if direct:
        grad_normed, *grads = together(grad_normed, *grads)
    out, tokens_grad = run_kernel(
        finish_rows_kernel,
        [jax.ShapeDtypeStruct((ROWS, D), BF16)] * 2,
        [pltpu.VMEM((ROWS + 2 * HALO, D), F32)],
        2 * WROWS * D * D,
        info,
        total,
        x,
        grad_normed,
        grad_middle,
        norms_all,
    )
    if direct:
        keep, send, *parts, from_near = together(*grads, *parts)
        rows = 2 * block + share
        plan = [[(slice(None), (slice(k * rows, (k + 1) * rows),))] for k in range(2)]
        low = add(plan, [((rows, D), BF16)] * 2, pair, *parts)
        second = [swap(low[0], "seq", 2), swap(low[1], "seq", 3)]
        first_pair, *first_low = add_slots(keep, *along_core([send]))
        first = [swap(part, "dp", 2 * m + 2) for m, part in enumerate(first_low)]
        own_pair, *own_low = add_slots(own_pair, from_near)
        *first, own0, own1, own2 = together(*first, *own_low)
        first_own, *first_low = add_slots(first_pair, *first)
        first_parts = [swap(part, "seq", k + 1) for k, part in enumerate(first_low)]
        own_parts = [swap(part, "dp", 2 * m + 2) for m, part in enumerate((own0, own1, own2))]
        everything, bounds = slice(None), (0, block, 2 * block, rows)
        grad_up, grad_down, grad_out = add(
            [[(everything, (slice(a, b),))] for a, b in zip(bounds, bounds[1:])],
            [((b - a, D), F32) for a, b in zip(bounds, bounds[1:])],
            own_pair,
            *own_parts,
            *second,
        )
        first_own, grad_up, grad_down, grad_out = together(
            first_own, grad_up, grad_down, grad_out
        )
        grad_down = grad_down.T
        w_qkv_grad, *norm_grads = finish_first(first_own, first_parts)
        norm_grads = [grad.reshape(share) for grad in norm_grads]
    else:
        first_sum = lax.psum_scatter(grads[0], ("dp", "seq"), scatter_dimension=0, tiled=True)
        w_qkv_grad = first_sum[:, : 3 * D]
        norm_grads = [first_sum[:, 3 * D + i] for i in range(4)]
    return (
        out,
        tokens_grad,
        w_qkv_grad,
        grad_out,
        grad_up,
        grad_down,
        *norm_grads,
    )


def solution(mesh):
    rows = P(("dp", "seq"), None)
    vector = P(("dp", "seq"))
    return jax.shard_map(
        per_device,
        mesh=mesh,
        in_specs=(
            rows,
            rows,
            rows,
            rows,
            P("dp", "seq"),
            P("seq", "dp"),
            vector,
            vector,
            vector,
            vector,
            P("dp", None),
            P("dp", None, None),
        ),
        out_specs=(
            rows,
            rows,
            rows,
            rows,
            P("dp", "seq"),
            P("seq", "dp"),
            vector,
            vector,
            vector,
            vector,
        ),
        check_vma=False,
    )
```

```python
import functools

import jax
import jax.numpy as jnp
from jax import lax
from jax.experimental import pallas as pl
from jax.experimental.pallas import tpu as pltpu
from jax.sharding import PartitionSpec as P

D = 512
HEADS = 16
HEAD_DIM = D // HEADS
FF = 2048
FREQ = 8
STEPS_DEV = 88
HALO = 4 * FREQ
ROWS = STEPS_DEV * FREQ
WIN = 4 * FREQ
WINDOWS = STEPS_DEV // 4 + 2
WROWS = WINDOWS * WIN
TILE = 768
QUAD = 128
NORMS = 128
CHUNK = 512
CHUNKS = FF // CHUNK
epsilon = 1e-06
F32 = jnp.float32
BF16 = jnp.bfloat16


def mm(left, right):
    return jnp.dot(left, right, preferred_element_type=F32)


def mm_right(left, right):
    return lax.dot_general(left, right, (((1,), (1,)), ((), ())), preferred_element_type=F32)


def mm_left(left, right):
    return lax.dot_general(left, right, (((0,), (0,)), ((), ())), preferred_element_type=F32)


def window_place(info, w):
    lead, mid, trail = info[0], info[1], info[2]
    seq = info[10]
    base = seq * STEPS_DEV
    n_lead = lead // 4 + 1
    n_mid = mid // 4 + 1
    index = jnp.where(seq == 0, 0, base // 4 + 1) + w
    in_mid = index >= n_lead
    in_trail = index >= n_lead + n_mid
    before = jnp.where(in_trail, n_lead + n_mid, jnp.where(in_mid, n_lead, 0))
    start = jnp.where(in_trail, lead + mid, jnp.where(in_mid, lead, 0))
    steps = jnp.where(in_trail, trail, jnp.where(in_mid, mid, lead))
    shift_time = jnp.where(in_trail, info[7], jnp.where(in_mid, info[5], info[3]))
    shift_freq = jnp.where(in_trail, info[8], jnp.where(in_mid, info[6], info[4]))
    first = start - 4 + shift_time + 4 * (index - before)
    here = first < base + STEPS_DEV
    low = jnp.clip(start - first, 0, 4)
    high = jnp.where(here, jnp.clip(start + steps - first, 0, 4), 0)
    own_low = jnp.clip(base - first, 0, 4)
    own_high = jnp.clip(base + STEPS_DEV - first, 0, 4)
    row = jnp.clip(first - base + 4, 0, STEPS_DEV + 4) * FREQ
    row = pl.multiple_of(row, FREQ)
    return (
        row,
        low * FREQ,
        high * FREQ,
        jnp.maximum(low, own_low) * FREQ,
        jnp.minimum(high, own_high) * FREQ,
        shift_freq,
    )


def window_at(w):
    return pl.ds(pl.multiple_of(w * WIN, WIN), WIN)


def tile_at(i):
    return pl.ds(pl.multiple_of(i * TILE, TILE), TILE)


def row_mask(low, high):
    index = lax.broadcasted_iota(jnp.int32, (WIN, 1), 0)
    return (index >= low) & (index < high)


def copy_all(pairs, sems, first=0):
    copies = [
        pltpu.make_async_copy(source, target, sems.at[first + i])
        for i, (source, target) in enumerate(pairs)
    ]
    for copy in copies:
        copy.start()
    return copies


def wait_all(copies):
    for copy in copies:
        copy.wait()


def edge_copies(rows, near, far, ext_low, halos):
    pairs = [
        (rows.at[0:HALO, :], ext_low.at[0:HALO, :]),
        (rows.at[ROWS - 2 * HALO :, :], ext_low.at[HALO:, :]),
    ]
    for i, parts in enumerate((near, far)):
        size = HALO // len(parts)
        pairs += [
            (part, halos.at[i, j * size : (j + 1) * size, :]) for j, part in enumerate(parts)
        ]
    return pairs


def pad_edges(info, ext, ext_low, halos):
    ext[HALO : 2 * HALO] = ext_low[0:HALO].astype(F32)
    ext[ROWS - HALO : ROWS + HALO] = ext_low[HALO:].astype(F32)
    odd = info[10] % 2 == 1
    for i, is_left in enumerate((odd, jnp.logical_not(odd))):
        at = pl.multiple_of(jnp.where(is_left, 0, HALO + ROWS), HALO)
        ext[pl.ds(at, HALO), :] = halos[i].astype(F32)


EDGES = (0, WINDOWS - 2, WINDOWS - 1)


def place_rows(info, w, ext, out):
    row, low, high, _, _, _ = window_place(info, w)
    values = jnp.where(row_mask(low, high), ext[pl.ds(row, WIN), :], 0.0)
    out[window_at(w), :] = values.astype(BF16)


def place_cotangent(info, w, ext, cot, cot_own):
    row, low, high, own_low, own_high, _ = window_place(info, w)
    values = ext[pl.ds(row, WIN), :]
    cot[window_at(w), :] = jnp.where(row_mask(low, high), values, 0.0).astype(BF16)
    cot_own[window_at(w), :] = jnp.where(row_mask(own_low, own_high), values, 0.0).astype(BF16)


def layout_kernel(info, tokens, cotangent, x_out, cot, cot_own, own, ext, stage, sems):
    copies = copy_all([(tokens, stage.at[0]), (cotangent, stage.at[1])], sems)
    for edge in (slice(0, HALO), slice(HALO + ROWS, 2 * HALO + ROWS)):
        ext[edge, :] = jnp.zeros((HALO, D), F32)
    copies[0].wait()
    ext[HALO : HALO + ROWS] = stage[0].astype(F32)

    def tokens_step(w, carry):
        place_rows(info, w, ext, x_out)
        return carry

    lax.fori_loop(0, WINDOWS, tokens_step, 0, unroll=4)
    copies[1].wait()
    ext[HALO : HALO + ROWS] = stage[1].astype(F32)

    def cotangent_step(w, carry):
        place_cotangent(info, w, ext, cot, cot_own)
        mask = row_mask(*window_place(info, w)[3:5])
        own[window_at(w), :] = jnp.where(mask, jnp.ones((WIN, QUAD), F32), 0.0)
        return carry

    lax.fori_loop(0, WINDOWS, cotangent_step, 0, unroll=4)


def normalized(values):
    mean = jnp.mean(values, axis=-1, keepdims=True)
    centered = values - mean
    variance = jnp.mean(centered * centered, axis=-1, keepdims=True)
    scale = lax.rsqrt(variance + epsilon)
    return centered * scale, scale


def norm_back(grad, unit, scale):
    mean_one = jnp.mean(grad, axis=-1, keepdims=True)
    mean_two = jnp.mean(grad * unit, axis=-1, keepdims=True)
    return scale * (grad - mean_one - unit * mean_two)


def head_masks():
    lane = lax.broadcasted_iota(jnp.int32, (1, QUAD), 1) // HEAD_DIM
    return [(lane == h).astype(BF16) for h in range(QUAD // HEAD_DIM)]


def spread(block, masks):
    return jnp.concatenate([block * mask for mask in masks], axis=0)


def gathered(product, lane):
    parts = [product[h * WIN : (h + 1) * WIN] for h in range(QUAD // HEAD_DIM)]
    return jnp.where(
        lane < 1, parts[0], jnp.where(lane < 2, parts[1], jnp.where(lane < 3, parts[2], parts[3]))
    )


def sum_kernel(plan, *refs):
    ins, outs = refs[: -len(plan)], refs[-len(plan) :]
    for out, pieces in zip(outs, plan):
        for target, source in pieces:
            value = ins[0][source].astype(F32)
            for part in ins[1:]:
                value = value + part[source].astype(F32)
            out[target] = value.astype(out.dtype)


def add(plan, shapes, *operands):
    return pl.pallas_call(
        functools.partial(sum_kernel, plan),
        out_shape=[jax.ShapeDtypeStruct(*s) for s in shapes],
        in_specs=[VMEM] * len(operands),
        out_specs=[VMEM] * len(shapes),
        compiler_params=pltpu.CompilerParams(vmem_limit_bytes=SMALL),
    )(*[near_core(a) for a in operands])


def pair_kernel(keep, *refs):
    for m, (part, out) in enumerate(zip(refs[:4], refs[4:])):
        out[...] = (keep[m].astype(F32) + part[...].astype(F32)).astype(out.dtype)


def add_pairs(keep, parts):
    slot = keep.shape[1:]
    return pl.pallas_call(
        pair_kernel,
        out_shape=[jax.ShapeDtypeStruct(slot, kind) for kind in (F32, BF16, BF16, BF16)],
        in_specs=[VMEM] * 5,
        out_specs=[VMEM] * 4,
        compiler_params=pltpu.CompilerParams(vmem_limit_bytes=SMALL),
    )(*[near_core(a) for a in (keep, *parts)])


def chunks_kernel(keep_first, keep_rest, keep_out, first, rest, out, *refs):
    own, near, pair, *low = refs
    block, share = keep_first.shape[1], keep_out.shape[1] // CHUNKS

    def sums(slot, k):
        a, b, row = (keep_first, first, 0) if k == 0 else (keep_rest, rest, (k - 1) * block)
        rows, out_rows = slice(row, row + block), slice(share * k, share * (k + 1))
        return (
            a[slot, rows].astype(F32) + b[slot, rows].astype(F32),
            keep_out[slot, out_rows].astype(F32) + out[slot, out_rows].astype(F32),
        )

    for slot in range(4):
        for k in range(CHUNKS):
            if k < 2:
                target, row = (own, near)[k].at[slot], 0
            else:
                target, row = ([pair] + low)[slot], (k - 2) * (block + share)
            one, two = sums(slot, k)
            target[row : row + block, :] = one.astype(target.dtype)
            target[row + block : row + block + share, :] = two.astype(target.dtype)


def add_chunks(keeps, parts):
    rows = keeps[0].shape[1] + keeps[2].shape[1] // CHUNKS
    shapes = [((4, rows, D), F32), ((4, rows, D), BF16), ((2 * rows, D), F32)]
    shapes += [((2 * rows, D), BF16)] * 3
    return pl.pallas_call(
        chunks_kernel,
        out_shape=[jax.ShapeDtypeStruct(*s) for s in shapes],
        in_specs=[VMEM] * 6,
        out_specs=[VMEM] * 6,
        compiler_params=pltpu.CompilerParams(vmem_limit_bytes=SMALL),
    )(*[near_core(a) for a in (*keeps, *parts)])


def finish_kernel(own, one, two, three, grad, *norm_grads):
    total = own[...] + (one[...].astype(F32) + two[...].astype(F32) + three[...].astype(F32))
    grad[...] = total[:, : 3 * D]
    rows = jnp.transpose(total[:, 3 * D :])
    for i, norm_grad in enumerate(norm_grads):
        norm_grad[...] = rows[i : i + 1]


def finish_first(own, parts):
    share = own.shape[0]
    shapes = [(share, 3 * D)] + [(1, share)] * 4
    return pl.pallas_call(
        finish_kernel,
        out_shape=[jax.ShapeDtypeStruct(dims, F32) for dims in shapes],
        in_specs=[VMEM] * (1 + len(parts)),
        out_specs=[VMEM] * len(shapes),
        compiler_params=pltpu.CompilerParams(vmem_limit_bytes=SMALL),
    )(*[near_core(a) for a in (own, *parts)])


def add_slots(*operands):
    slot = operands[0].shape[1:]
    plan = [[(slice(None), i)] for i in range(4)]
    return add(plan, [(slot, F32)] + [(slot, BF16)] * 3, *operands)


def prepare_kernel(tokens, cotangent, w_qkv, w_out, w_up, w_down, *refs):
    norms, (with_near, first, with_far, second, up_near, up_far, vectors, sems) = refs[:4], refs[4:]
    share, width = first.shape
    block = w_up.shape[0]
    odd = lax.axis_index("seq") % 2
    pairs = [(norm, vectors.at[i]) for i, norm in enumerate(norms)]
    for target in (with_near, first, with_far):
        pairs += [(w_qkv, target.at[:, : 3 * D]), (w_out, target.at[:, 3 * D : 4 * D])]
    for target, up_target, is_head in ((with_near, up_near, odd), (with_far, up_far, 1 - odd)):
        start = pl.multiple_of((1 - is_head) * (ROWS - HALO), HALO)
        for j in range(2):
            at = width + j * D
            rows = pl.ds(start + j * (HALO // 2), HALO // 2)
            pairs.append((tokens.at[rows, :], target.at[:, at : at + D]))
        pairs.append((cotangent.at[pl.ds(start, HALO), :], up_target.at[2 * block :, :]))
    for target in (second, up_near, up_far):
        pairs += [(w_up, target.at[0:block]), (w_down, target.at[block : 2 * block])]
    first_row = 2 * block
    for i, source in enumerate([w_qkv.at[:, j * D : (j + 1) * D] for j in range(3)] + [w_out]):
        pairs.append((source, second.at[first_row + share * i : first_row + share * (i + 1), :]))
    copies = copy_all(pairs, sems)
    wait_all(copies[: len(norms)])
    columns = jnp.concatenate(
        [vectors[i].astype(F32) for i in range(4)] + [jnp.zeros((NORMS - 4, share), F32)], axis=0
    )
    columns = jnp.transpose(columns).astype(BF16)
    for target in (with_near, first, with_far):
        target[:, 4 * D : width] = columns
    second[first_row + 4 * share :, :] = jnp.concatenate([columns] * (D // NORMS), axis=1)
    wait_all(copies[len(norms) :])


def attention_kernel(direct, info, rows, near, far, x_in, *refs):
    pieces, refs = (refs[:4], refs[4:]) if direct else (refs[:1], refs[1:])
    x_out, qkv_out, mixed_out, probs_out, w_out, norms_out, ext, edges, halos, sems = refs
    width = w_out.shape[1]
    near, far = [
        [a.at[:, width + j * D : width + (j + 1) * D] for j in range(2)] if direct else [a]
        for a in (near, far)
    ]
    edge_copy = copy_all(edge_copies(rows, near, far, edges, halos), sems)
    x_out[...] = x_in[...]
    if direct:
        count, share = pieces[0].shape[1] + 1, pieces[0].shape[2]
        for core, piece in enumerate(pieces[:2]):
            for chip in range(4):
                for k in range(1, count):
                    owner = (2 * chip + (info[9] % 2 ^ core)) * count + (info[10] ^ k)
                    at = pl.multiple_of(owner * share, share)
                    w_out[pl.ds(at, share), :] = piece[chip, k - 1]
        for i, partner in enumerate(ORDER):
            owner = (info[9] ^ partner) * count + info[10]
            at = pl.ds(pl.multiple_of(owner * share, share), share)
            for j in range(5):
                cols = min(D, width - j * D)
                row = D // 4 + j * share
                part = pieces[2 + i // 4][i % 4, row : row + share, 0:cols]
                w_out[at, j * D : j * D + cols] = part
    else:
        w_out[...] = pieces[0][...]
    wait_all(edge_copy)
    pad_edges(info, ext, edges, halos)
    for w in EDGES:
        place_rows(info, w, ext, x_out)
    norms_out[...] = jnp.transpose(w_out[:, 4 * D :].astype(F32))[:8]
    gain, shift = norms_out[0:1], norms_out[1:2]

    def project(i, carry):
        at = tile_at(i)
        unit, _ = normalized(x_out[at, :].astype(F32))
        low = (unit * gain + shift).astype(BF16)
        for part in range(3):
            cols = slice(part * D, (part + 1) * D)
            qkv_out[at, cols] = mm(low, w_out[:, cols]).astype(BF16)
        return carry

    lax.fori_loop(0, WROWS // TILE, project, 0)
    masks = head_masks()
    lane = lax.broadcasted_iota(jnp.int32, (1, QUAD), 1) // HEAD_DIM
    key_row = lax.broadcasted_iota(jnp.int32, (WIN, QUAD), 0)
    query_row = lax.broadcasted_iota(jnp.int32, (WIN, QUAD), 1) % WIN
    key_freq, query_freq = key_row % FREQ, query_row % FREQ

    def attend(w, carry):
        _, low, high, _, _, shift_freq = window_place(info, w)
        at = pl.ds(pl.multiple_of(w * WIN, WIN), WIN)
        key_group = (key_freq + 4 - shift_freq) >> 2
        query_group = (query_freq + 4 - shift_freq) >> 2
        allowed = (key_group == query_group) & (key_row >= low) & (key_row < high)
        quads = range(D // QUAD)
        raw = []
        for quad in quads:
            query = qkv_out[at, quad * QUAD : (quad + 1) * QUAD]
            key = qkv_out[at, D + quad * QUAD : D + (quad + 1) * QUAD]
            raw.append(mm_right(key, spread(query, masks)))
        scores = [jnp.where(allowed, r * HEAD_DIM**-0.5, -1e30) for r in raw]
        weights = [jnp.exp(s - jnp.max(s, axis=0, keepdims=True)) for s in scores]
        probs = [(p / jnp.sum(p, axis=0, keepdims=True)).astype(BF16) for p in weights]
        products = []
        for quad in quads:
            probs_out[at, quad * QUAD : (quad + 1) * QUAD] = probs[quad]
            value = qkv_out[at, 2 * D + quad * QUAD : 2 * D + (quad + 1) * QUAD]
            products.append(mm_left(probs[quad], value))
        for quad in quads:
            mixed = gathered(products[quad], lane).astype(BF16)
            mixed_out[at, quad * QUAD : (quad + 1) * QUAD] = mixed
        return carry

    lax.fori_loop(0, WINDOWS, attend, 0, unroll=12)


def gelu_parts(values):
    half_exp = jnp.exp(-0.5 * values * values)
    t = 1.0 / (1.0 + (0.3275911 * 0.7071067811865476) * jnp.abs(values))
    poly = t * (
        0.5 * 0.254829592
        + t
        * (
            0.5 * -0.284496736
            + t * (0.5 * 1.421413741 + t * (0.5 * -1.453152027 + t * (0.5 * 1.061405429)))
        )
    )
    tail = poly * half_exp
    return jnp.where(values >= 0, 1.0 - tail, tail), half_exp * 0.3989422804014327


def place_feed(info, pieces, up, down):
    block = D // 8
    for piece, partner in zip(pieces, ORDER):
        at = pl.ds(pl.multiple_of((info[9] ^ partner) * block, block), block)
        for c in range(up.shape[0]):
            up[c, at, :] = piece[c, 0:block, :]
            down[c, at, :] = piece[c, block : 2 * block, :]


def feed_rows(at, up, down, normed, cot, hidden, pre):
    values = mm(normed[at, :], up)
    grad_hidden = mm(cot[at, :], down)
    below, density = gelu_parts(values)
    hidden_low = (values * below).astype(BF16)
    grad_low = (grad_hidden * (below + values * density)).astype(BF16)
    hidden[at, :] = hidden_low
    pre[at, :] = grad_low
    return mm_right(hidden_low, down), mm_right(grad_low, up)


def feed_grads(direct, info, row, normed_own, cot_own, hidden, pre, space, refs):
    block = D // 8
    for i, product in enumerate(((normed_own, pre), (cot_own, hidden))):
        grad = mm_left(product[0][...], product[1][...])
        if not direct:
            refs[i][row // (2 * block)] = grad
            continue
        space[0:D, :] = grad
        for partner in range(8):
            at = pl.multiple_of((info[9] ^ partner) * block, block)
            first = row + i * block
            refs[partner & 1][partner >> 1, first : first + block, :] = space[
                pl.ds(at, block), :
            ].astype(BF16)


def feed_first_kernel(
    direct, info, rows, near, far, cot_in, cot_own_in, own, x_in, mixed_in, norms, w_all, *refs
):
    pieces, refs = refs[:2], refs[2:]
    middle, total, grad, normed, normed_own, cot, cot_own = refs[:7]
    grads, (up, down, ext, hidden, pre, edges, halos, sems) = refs[7:9], refs[9:]
    near, far = [[a.at[a.shape[0] - HALO :, :]] for a in (near, far)]
    edge_copy = copy_all(edge_copies(rows, near, far, edges, halos), sems)
    cot[...], cot_own[...] = cot_in[...], cot_own_in[...]
    if direct:
        own_pieces = [piece.at[m : m + 1] for piece in pieces for m in range(4)]
        place_feed(info, own_pieces, up, down)
    else:
        up[...], down[...] = pieces[0][0:1], pieces[1][0:1]
    wait_all(edge_copy)
    pad_edges(info, ext, edges, halos)
    for w in EDGES:
        place_cotangent(info, w, ext, cot, cot_own)
    gain, shift = norms[2:3], norms[3:4]

    def before(i, carry):
        at = tile_at(i)
        values = x_in[at, :].astype(F32) + mm(mixed_in[at, :], w_all[:, 3 * D : 4 * D])
        middle[at, :] = values
        unit, _ = normalized(values)
        low = unit * gain + shift
        normed[at, :] = low.astype(BF16)
        normed_own[at, :] = (low * own[at, 0:1]).astype(BF16)
        return carry

    lax.fori_loop(0, WROWS // TILE, before, 0)
    for i in range(WROWS // TILE):
        at = slice(i * TILE, (i + 1) * TILE)
        branch, back = feed_rows(at, up[0], down[0], normed, cot, hidden, pre)
        total[at, :] = middle[at, :] + branch
        grad[at, :] = back
    feed_grads(direct, info, 0, normed_own, cot_own, hidden, pre, ext, grads)


def feed_rest_kernel(direct, info, total_in, grad_in, normed, normed_own, cot, cot_own, *refs):
    pieces, refs = (refs[:8], refs[8:]) if direct else (refs[:2], refs[2:])
    total, grad, *grads, up, down, ext, hidden, pre = refs
    if direct:
        place_feed(info, pieces, up, down)
    else:
        up[...], down[...] = pieces[0][1:CHUNKS], pieces[1][1:CHUNKS]
    for c in range(CHUNKS - 1):
        for i in range(WROWS // TILE):
            at = slice(i * TILE, (i + 1) * TILE)
            branch, back = feed_rows(at, up[c], down[c], normed, cot, hidden, pre)
            total[at, :] = (total if c else total_in)[at, :] + branch
            grad[at, :] = (grad if c else grad_in)[at, :] + back
        feed_grads(direct, info, c * (D // 4), normed_own, cot_own, hidden, pre, ext, grads)


def feed_last_kernel(direct, info, middle, grad, cot, own, mixed_in, norms, w_all, *refs):
    grad_middle, grad_mixed, grad_norms, *grads, ext, grad_own = refs
    gain = norms[2:3]
    grad_norms[...] = jnp.zeros(grad_norms.shape, F32)
    for i in range(WROWS // TILE):
        at = slice(i * TILE, (i + 1) * TILE)
        unit, scale = normalized(middle[at, :])
        part = grad[at, :]
        masked = part * own[at, 0:1]
        grad_norms[0:1] += jnp.sum(masked * unit, axis=0, keepdims=True)
        grad_norms[1:2] += jnp.sum(masked, axis=0, keepdims=True)
        result = cot[at, :].astype(F32) + norm_back(part * gain, unit, scale)
        grad_middle[at, :] = result
        grad_mixed[at, :] = mm_right(result.astype(BF16), w_all[:, 3 * D : 4 * D]).astype(BF16)
        grad_own[at, :] = (result * own[at, 0:1]).astype(BF16)
    grad_out = mm_left(mixed_in[...], grad_own[...])
    if direct:
        ext[0:D, :] = grad_out
        share = grads[0].shape[1] // CHUNKS
        for partner in range(8):
            for k in range(CHUNKS):
                owner = (info[9] ^ partner) * CHUNKS + (info[10] ^ k)
                row = pl.multiple_of(owner * share, share)
                grads[partner & 1][partner >> 1, share * k : share * (k + 1), :] = ext[
                    pl.ds(row, share), :
                ].astype(BF16)
    else:
        grads[0][...] = grad_out


def finish_rows_kernel(info, values, out, ext):
    unplace(info, values, ext, out)


def unplace(info, values, ext, out):
    def back(w, carry):
        row, low, high, _, _, _ = window_place(info, w)
        at = pl.ds(pl.multiple_of(w * WIN, WIN), WIN)
        place = pl.ds(row, WIN)
        ext[place, :] = jnp.where(row_mask(low, high), values[at, :], ext[place, :])
        return carry

    lax.fori_loop(0, WINDOWS, back, 0, unroll=4)
    out[...] = ext[HALO : HALO + ROWS].astype(BF16)


def back_kernel(
    direct, info, x_in, own, qkv, probs_in, grad_mixed, grad_middle, w_qkv, norms, grad_norms, *refs
):
    grad_tokens, refs = refs[0], refs[1:]
    if direct:
        (keep, send), refs = refs[:2], refs[2:]
    else:
        w_grad, refs = refs[0], refs[1:]
    normed, grad_qkv, gains, grad_w = refs
    masks = head_masks()
    lane = lax.broadcasted_iota(jnp.int32, (1, QUAD), 1) // HEAD_DIM

    def attend_back(w, carry):
        at = window_at(w)
        quads = range(D // QUAD)
        cols = [slice(quad * QUAD, (quad + 1) * QUAD) for quad in quads]
        cols_key = [slice(D + quad * QUAD, D + (quad + 1) * QUAD) for quad in quads]
        cols_value = [slice(2 * D + quad * QUAD, 2 * D + (quad + 1) * QUAD) for quad in quads]
        grad_out = [spread(grad_mixed[at, c], masks) for c in cols]
        grad_probs = [mm_right(qkv[at, c], g) for c, g in zip(cols_value, grad_out)]
        low = [probs_in[at, c] for c in cols]
        probs = [p.astype(F32) for p in low]
        delta = [jnp.sum(p * g, axis=0, keepdims=True) for p, g in zip(probs, grad_probs)]
        grad_scores = [
            (p * (g - d) * HEAD_DIM**-0.5).astype(BF16)
            for p, g, d in zip(probs, grad_probs, delta)
        ]
        grad_value = [mm(p, g) for p, g in zip(low, grad_out)]
        grad_query = [mm_left(g, qkv[at, c]) for g, c in zip(grad_scores, cols_key)]
        grad_key = [mm(g, spread(qkv[at, c], masks)) for g, c in zip(grad_scores, cols)]
        for quad in quads:
            grad_qkv[at, cols_value[quad]] = grad_value[quad].astype(BF16)
            grad_qkv[at, cols_key[quad]] = grad_key[quad].astype(BF16)
            grad_qkv[at, cols[quad]] = gathered(grad_query[quad], lane).astype(BF16)
        return carry

    lax.fori_loop(0, WINDOWS, attend_back, 0, unroll=12)
    gain, shift = norms[0:1], norms[1:2]
    gains[...] = jnp.zeros(gains.shape, F32)

    def after(i, carry):
        at = tile_at(i)
        unit, scale = normalized(x_in[at, :].astype(F32))
        mask = own[at, 0:1]
        normed[at, :] = ((unit * gain + shift) * mask).astype(BF16)
        part = mm_right(grad_qkv[at, :], w_qkv[:, : 3 * D])
        masked = part * mask
        gains[0:1] += jnp.sum(masked * unit, axis=0, keepdims=True)
        gains[1:2] += jnp.sum(masked, axis=0, keepdims=True)
        grad_tokens[at, :] = grad_middle[at, :] + norm_back(part * gain, unit, scale)
        return carry

    lax.fori_loop(0, WROWS // TILE, after, 0)
    gains[2:4] = grad_norms[0:2]
    for part in range(3):
        cols = slice(part * D, (part + 1) * D)
        grad_w[:, cols] = mm_left(normed[...], grad_qkv[:, cols])
    grad_w[:, 3 * D :] = jnp.transpose(gains[...])
    if direct:
        count = keep.shape[1]
        for partner in range(8):
            target = send if partner & 1 else keep
            for k in range(count):
                row = pl.multiple_of(((info[9] ^ partner) * count + (info[10] ^ k)) * 16, 16)
                target[partner >> 1, k] = grad_w[pl.ds(row, 16), :].astype(BF16)
    else:
        w_grad[...] = grad_w[...]


ORDER = (0, 2, 4, 6, 1, 3, 5, 7)
CHIPS = [[0, 2, 4, 6], [1, 3, 5, 7]]
LIMIT = 20 * 1024 * 1024
SMALL = 8 * 1024 * 1024
SMEM = pl.BlockSpec(memory_space=pltpu.SMEM)
VMEM = pl.BlockSpec(memory_space=pltpu.VMEM)
ANY = pl.BlockSpec(memory_space=pl.ANY)


def near_core(array):
    return pltpu.with_memory_space_constraint(array, pltpu.VMEM)


def far_core(array):
    return pltpu.with_memory_space_constraint(array, pltpu.HBM)


def run_kernel(body, out_shape, scratch, flops, info, *operands):
    specs = [ANY if isinstance(a, list) else VMEM for a in operands]
    operands = [a[0] if isinstance(a, list) else near_core(a) for a in operands]
    moved = sum(a.size * a.dtype.itemsize for a in operands)
    return pl.pallas_call(
        body,
        out_shape=out_shape,
        in_specs=[SMEM] + specs,
        out_specs=[VMEM] * len(out_shape),
        scratch_shapes=scratch,
        cost_estimate=pl.CostEstimate(
            flops=flops, bytes_accessed=moved, transcendentals=flops // 1024
        ),
        compiler_params=pltpu.CompilerParams(vmem_limit_bytes=LIMIT),
    )(info, *operands)


def swap(array, axis, bit):
    return lax.ppermute(array, axis, [(i, i ^ bit) for i in range(lax.axis_size(axis))])


def together(*values):
    return lax.optimization_barrier(values)


def along_seq(shard):
    return [swap(shard, "seq", k) for k in (1, 2, 3)]


def along_plane(column):
    return [swap(column, "dp", partner) for partner in (2, 4, 6)]


def along_core(pieces):
    return [swap(piece, "dp", 1) for piece in pieces]


def add_parts(own, parts):
    return own.astype(F32) + sum(part.astype(F32) for part in parts)


def shape(dims, kind):
    return pltpu.VMEM(dims, kind)


def per_device(
    tokens,
    cotangent,
    w_qkv,
    w_out,
    w_up,
    w_down,
    norm1_gain,
    norm1_shift,
    norm2_gain,
    norm2_shift,
    clip_steps,
    window_shifts,
):
    n_dp, n_seq = lax.axis_size("dp"), lax.axis_size("seq")
    share = w_qkv.shape[0]
    direct = n_dp == 8 and share % 16 == 0
    info = jnp.concatenate(
        [
            clip_steps.reshape(3),
            window_shifts.reshape(6),
            lax.axis_index("dp").reshape(1).astype(jnp.int32),
            lax.axis_index("seq").reshape(1).astype(jnp.int32),
        ]
    )
    width = 4 * D + NORMS
    vectors = (norm1_gain, norm1_shift, norm2_gain, norm2_shift)

    def in_hbm(arrays):
        return [[a] for a in arrays]

    x, cot, cot_own, own = run_kernel(
        layout_kernel,
        [shape((WROWS, D), BF16)] * 3 + [shape((WROWS, QUAD), F32)],
        [
            pltpu.VMEM((ROWS + 2 * HALO, D), F32),
            pltpu.VMEM((2, ROWS, D), BF16),
            pltpu.SemaphoreType.DMA((2,)),
        ],
        2 * WROWS * D * D,
        info,
        *in_hbm((tokens, cotangent)),
    )
    if direct:
        with_near, first, with_far, second, up_near, up_far = pl.pallas_call(
            prepare_kernel,
            out_shape=[
                jax.ShapeDtypeStruct((share, width + 2 * D), BF16),
                jax.ShapeDtypeStruct((share, width), BF16),
                jax.ShapeDtypeStruct((share, width + 2 * D), BF16),
                jax.ShapeDtypeStruct((2 * w_up.shape[0] + 5 * share, D), BF16),
                jax.ShapeDtypeStruct((2 * w_up.shape[0] + HALO, D), BF16),
                jax.ShapeDtypeStruct((2 * w_up.shape[0] + HALO, D), BF16),
            ],
            in_specs=[ANY] * 10,
            out_specs=[VMEM] * 6,
            scratch_shapes=[
                pltpu.VMEM((4, 1, share), BF16),
                pltpu.SemaphoreType.DMA((26,)),
            ],
            compiler_params=pltpu.CompilerParams(vmem_limit_bytes=LIMIT),
        )(
            *[
                far_core(a)
                for a in (tokens, cotangent, w_qkv, w_out, w_up, w_down.T)
                + tuple(v.reshape(1, -1) for v in vectors)
            ]
        )
        block = w_up.shape[0]
        own_x, own_y, near, middle, far, x, cot, cot_own, own = together(
            swap(second, "dp", 2),
            swap(second, "dp", 4),
            swap(with_near, "seq", 1),
            swap(first, "seq", 2),
            swap(with_far, "seq", 3),
            x,
            cot,
            cot_own,
            own,
        )
        column = jnp.stack([near[:, :width], middle, far[:, :width]])
        column, second = together(column, second)
        first_half = lax.all_gather(column, "dp", axis_index_groups=CHIPS)
        first_half, own_d, *rest = together(
            first_half,
            swap(second, "dp", 6),
            swap(up_near, "seq", 1),
            swap(second[: 2 * block], "seq", 2),
            swap(up_far, "seq", 3),
        )
        second_own = jnp.stack([second, own_x, own_y, own_d])
        near_cot, far_cot = rest[0], rest[2]
        rest = [rest[0][: 2 * block], rest[1], rest[2][: 2 * block]]
        rest = jnp.stack(rest)
        first_half, rest, second_own = together(first_half, rest, second_own)
        second_own = [second_own, *along_core([second_own])]
        first_all = [first_half, *along_core([first_half]), *second_own]
        second_plane = along_plane(rest)
    else:
        norms = jnp.pad(jnp.stack(vectors, axis=1), ((0, 0), (0, NORMS - 4)))
        first = jnp.concatenate([w_qkv, w_out, norms], axis=1)
        both = jnp.stack([tokens, cotangent])
        head, tail = both[:, :HALO], both[:, ROWS - HALO :]
        odd = lax.axis_index("seq") % 2 == 1
        first_all = [lax.all_gather(first, ("dp", "seq"), axis=0, tiled=True)]
        up_all = lax.all_gather(lax.all_gather(w_up, "dp", axis=0, tiled=True), "seq", axis=0)
        down_all = lax.all_gather(lax.all_gather(w_down.T, "dp", axis=0, tiled=True), "seq", axis=0)
        second_own = second_all = [up_all, down_all]
        from_left = lax.ppermute(tail, "seq", [(i, i + 1) for i in range(n_seq - 1)])
        from_right = lax.ppermute(head, "seq", [(i + 1, i) for i in range(n_seq - 1)])
        near, near_cot = jnp.where(odd, from_left, from_right)
        far, far_cot = jnp.where(odd, from_right, from_left)

    x, qkv, mixed, probs, w_all, norms_all = run_kernel(
        functools.partial(attention_kernel, direct),
        [
            shape((WROWS, D), BF16),
            shape((WROWS, 3 * D), BF16),
            shape((WROWS, D), BF16),
            shape((WROWS, D), BF16),
            shape((D, width), BF16),
            shape((8, D), F32),
        ],
        [
            pltpu.VMEM((ROWS + 2 * HALO, D), F32),
            pltpu.VMEM((3 * HALO, D), BF16),
            pltpu.VMEM((2, HALO, D), BF16),
            pltpu.SemaphoreType.DMA((6,)),
        ],
        2 * WROWS * D * 3 * D * 2,
        info,
        *in_hbm((tokens, near, far)),
        x,
        *first_all,
    )
    if direct:
        grads_shape = [shape((4, 2 * block, D), BF16)] * 2
    else:
        grads_shape = [shape((1, D, CHUNK), F32)] * 2
    *state, keep, send = run_kernel(
        functools.partial(feed_first_kernel, direct),
        [shape((WROWS, D), F32)] * 3
        + [shape((WROWS, D), BF16)] * 4
        + grads_shape,
        [
            pltpu.VMEM((1, D, CHUNK), BF16),
            pltpu.VMEM((1, D, CHUNK), BF16),
            pltpu.VMEM((ROWS + 2 * HALO, D), F32),
            pltpu.VMEM((WROWS, CHUNK), BF16),
            pltpu.VMEM((WROWS, CHUNK), BF16),
            pltpu.VMEM((3 * HALO, D), BF16),
            pltpu.VMEM((2, HALO, D), BF16),
            pltpu.SemaphoreType.DMA((4,)),
        ],
        2 * WROWS * D * (6 * CHUNK + D),
        info,
        *in_hbm((cotangent, near_cot, far_cot)),
        cot,
        cot_own,
        own,
        x,
        mixed,
        norms_all,
        w_all,
        *second_own,
    )
    if direct:
        *second_plane, total = together(*second_plane, state[1])
        state[1] = total
        second_plane = [rest, *second_plane]
        second_all = second_plane + along_core(second_plane)
        first_grads = [keep, send]
        extra = (CHUNKS - 1) * 2 * block
        grads_shape = [shape((4, extra, D), BF16)] * 2
        out_shape = [shape((4, n_seq * share, D), BF16)] * 2
    else:
        first_grads = [keep, send]
        grads_shape = [shape((CHUNKS - 1, D, CHUNK), F32)] * 2
        out_shape = [shape((D, D), F32)]
    middle, total, grad, normed, normed_own, cot, cot_own = state
    total, grad, *grads = run_kernel(
        functools.partial(feed_rest_kernel, direct),
        [shape((WROWS, D), F32)] * 2 + grads_shape,
        [
            pltpu.VMEM((CHUNKS - 1, D, CHUNK), BF16),
            pltpu.VMEM((CHUNKS - 1, D, CHUNK), BF16),
            pltpu.VMEM((D, D), F32),
            pltpu.VMEM((WROWS, CHUNK), BF16),
            pltpu.VMEM((WROWS, CHUNK), BF16),
        ],
        2 * WROWS * D * 18 * CHUNK,
        info,
        total,
        grad,
        normed,
        normed_own,
        cot,
        cot_own,
        *second_all,
    )
    if direct:
        from_core = along_core([first_grads[1], grads[1]])
    grad_middle, grad_mixed, grad_norms, *out_grads = run_kernel(
        functools.partial(feed_last_kernel, direct),
        [
            shape((WROWS, D), F32),
            shape((WROWS, D), BF16),
            shape((8, D), F32),
            *out_shape,
        ],
        [pltpu.VMEM((D, D), F32), pltpu.VMEM((WROWS, D), BF16)],
        2 * WROWS * D * 2 * D,
        info,
        middle,
        grad,
        cot,
        own,
        mixed,
        norms_all,
        w_all,
    )
    if direct:
        from_core = [*from_core, *along_core(out_grads[1:])]
        keeps, from_core = [first_grads[0], grads[0], out_grads[0]], together(*from_core)
        own_pair, to_near, pair, *low = add_chunks(keeps, from_core)
        to_near, *low, grad_mixed = together(to_near, *low, grad_mixed)
        parts = [swap(part, "dp", 2 * m + 2) for m, part in enumerate(low)]
        parts.append(swap(to_near, "seq", 1))
        grads_shape = [shape((4, n_seq, share, 3 * D + NORMS), BF16)] * 2
    else:
        grads_up, grads_down = [
            jnp.concatenate([a, b], axis=0) for a, b in zip(first_grads, grads)
        ]
        grad_up = lax.psum_scatter(grads_up, "seq", scatter_dimension=0)
        grad_up = lax.psum_scatter(grad_up, "dp", scatter_dimension=0, tiled=True)
        grad_down = lax.psum_scatter(grads_down, "seq", scatter_dimension=0)
        grad_down = lax.psum_scatter(grad_down, "dp", scatter_dimension=0, tiled=True).T
        grad_out = lax.psum_scatter(out_grads[0], ("dp", "seq"), scatter_dimension=0, tiled=True)
        grads_shape = [shape((D, 3 * D + NORMS), F32)]
    grad_tokens, *grads = run_kernel(
        functools.partial(back_kernel, direct),
        [shape((WROWS, D), F32), *grads_shape],
        [
            pltpu.VMEM((WROWS, D), BF16),
            pltpu.VMEM((WROWS, 3 * D), BF16),
            pltpu.VMEM((NORMS, D), F32),
            pltpu.VMEM((D, 3 * D + NORMS), F32),
        ],
        2 * WROWS * D * (6 * D + 3 * D),
        info,
        x,
        own,
        qkv,
        probs,
        grad_mixed,
        grad_middle,
        w_all,
        norms_all,
        grad_norms,
    )
    if direct:
        grad_tokens, *grads = together(grad_tokens, *grads)
    out, tokens_grad = [
        run_kernel(
            finish_rows_kernel,
            [jax.ShapeDtypeStruct((ROWS, D), BF16)],
            [pltpu.VMEM((ROWS + 2 * HALO, D), F32)],
            2 * WROWS * D * D,
            info,
            values,
        )[0]
        for values in (total, grad_tokens)
    ]
    if direct:
        keep, send, *parts, from_near = together(*grads, *parts)
        rows = 2 * block + share
        plan = [[(slice(None), (slice(k * rows, (k + 1) * rows),))] for k in range(2)]
        low = add(plan, [((rows, D), BF16)] * 2, pair, *parts)
        second_far, from_near_far = together(low[1], swap(low[0], "seq", 1))
        (second_far,) = add([[(slice(None), slice(None))]], [(low[1].shape, BF16)], second_far, from_near_far)
        second = [swap(second_far, "seq", 3)]
        from_core, tokens_grad = together(*along_core([send]), tokens_grad)
        first_pair, *first_low = add_slots(keep, from_core)
        first = [swap(part, "dp", 2 * m + 2) for m, part in enumerate(first_low)]
        own_pair, *own_low = add_slots(own_pair, from_near)
        *first, own0, own1, own2 = together(*first, *own_low)
        first_own, *first_low = add_slots(first_pair, *first)
        first_parts = [swap(part, "seq", k + 1) for k, part in enumerate(first_low)]
        own_parts = [swap(part, "dp", 2 * m + 2) for m, part in enumerate((own0, own1, own2))]
        everything, bounds = slice(None), (0, block, 2 * block, rows)
        grad_up, grad_down, grad_out = add(
            [[(everything, (slice(a, b),))] for a, b in zip(bounds, bounds[1:])],
            [((b - a, D), F32) for a, b in zip(bounds, bounds[1:])],
            own_pair,
            *own_parts,
            *second,
        )
        first_own, grad_up, grad_down, grad_out = together(
            first_own, grad_up, grad_down, grad_out
        )
        grad_down = grad_down.T
        w_qkv_grad, *norm_grads = finish_first(first_own, first_parts)
        norm_grads = [grad.reshape(share) for grad in norm_grads]
    else:
        first_sum = lax.psum_scatter(grads[0], ("dp", "seq"), scatter_dimension=0, tiled=True)
        w_qkv_grad = first_sum[:, : 3 * D]
        norm_grads = [first_sum[:, 3 * D + i] for i in range(4)]
    return (
        out,
        tokens_grad,
        w_qkv_grad,
        grad_out,
        grad_up,
        grad_down,
        *norm_grads,
    )


def solution(mesh):
    rows = P(("dp", "seq"), None)
    vector = P(("dp", "seq"))
    return jax.shard_map(
        per_device,
        mesh=mesh,
        in_specs=(
            rows,
            rows,
            rows,
            rows,
            P("dp", "seq"),
            P("seq", "dp"),
            vector,
            vector,
            vector,
            vector,
            P("dp", None),
            P("dp", None, None),
        ),
        out_specs=(
            rows,
            rows,
            rows,
            rows,
            P("dp", "seq"),
            P("seq", "dp"),
            vector,
            vector,
            vector,
            vector,
        ),
        check_vma=False,
    )
```

```python
import functools

import jax
import jax.numpy as jnp
from jax import lax
from jax.experimental import pallas as pl
from jax.experimental.pallas import tpu as pltpu
from jax.sharding import PartitionSpec as P

D = 512
HEADS = 16
HEAD_DIM = D // HEADS
FF = 2048
FREQ = 8
STEPS_DEV = 88
HALO = 4 * FREQ
ROWS = STEPS_DEV * FREQ
WIN = 4 * FREQ
WINDOWS = STEPS_DEV // 4 + 2
WROWS = WINDOWS * WIN
TILE = 768
QUAD = 128
NORMS = 128
CHUNK = 512
CHUNKS = FF // CHUNK
epsilon = 1e-06
F32 = jnp.float32
BF16 = jnp.bfloat16


def mm(left, right):
    return jnp.dot(left, right, preferred_element_type=F32)


def mm_right(left, right):
    return lax.dot_general(left, right, (((1,), (1,)), ((), ())), preferred_element_type=F32)


def mm_left(left, right):
    return lax.dot_general(left, right, (((0,), (0,)), ((), ())), preferred_element_type=F32)


def window_place(info, w):
    lead, mid, trail = info[0], info[1], info[2]
    seq = info[10]
    base = seq * STEPS_DEV
    n_lead = lead // 4 + 1
    n_mid = mid // 4 + 1
    index = jnp.where(seq == 0, 0, base // 4 + 1) + w
    in_mid = index >= n_lead
    in_trail = index >= n_lead + n_mid
    before = jnp.where(in_trail, n_lead + n_mid, jnp.where(in_mid, n_lead, 0))
    start = jnp.where(in_trail, lead + mid, jnp.where(in_mid, lead, 0))
    steps = jnp.where(in_trail, trail, jnp.where(in_mid, mid, lead))
    shift_time = jnp.where(in_trail, info[7], jnp.where(in_mid, info[5], info[3]))
    shift_freq = jnp.where(in_trail, info[8], jnp.where(in_mid, info[6], info[4]))
    first = start - 4 + shift_time + 4 * (index - before)
    here = first < base + STEPS_DEV
    low = jnp.clip(start - first, 0, 4)
    high = jnp.where(here, jnp.clip(start + steps - first, 0, 4), 0)
    own_low = jnp.clip(base - first, 0, 4)
    own_high = jnp.clip(base + STEPS_DEV - first, 0, 4)
    row = jnp.clip(first - base + 4, 0, STEPS_DEV + 4) * FREQ
    row = pl.multiple_of(row, FREQ)
    return (
        row,
        low * FREQ,
        high * FREQ,
        jnp.maximum(low, own_low) * FREQ,
        jnp.minimum(high, own_high) * FREQ,
        shift_freq,
    )


def window_at(w):
    return pl.ds(pl.multiple_of(w * WIN, WIN), WIN)


def tile_at(i):
    return pl.ds(pl.multiple_of(i * TILE, TILE), TILE)


def row_mask(low, high):
    index = lax.broadcasted_iota(jnp.int32, (WIN, 1), 0)
    return (index >= low) & (index < high)


def copy_all(pairs, sems, first=0):
    copies = [
        pltpu.make_async_copy(source, target, sems.at[first + i])
        for i, (source, target) in enumerate(pairs)
    ]
    for copy in copies:
        copy.start()
    return copies


def wait_all(copies):
    for copy in copies:
        copy.wait()


def edge_copies(rows, near, far, ext_low, halos):
    pairs = [
        (rows.at[0:HALO, :], ext_low.at[0:HALO, :]),
        (rows.at[ROWS - 2 * HALO :, :], ext_low.at[HALO:, :]),
    ]
    for i, parts in enumerate((near, far)):
        size = HALO // len(parts)
        pairs += [
            (part, halos.at[i, j * size : (j + 1) * size, :]) for j, part in enumerate(parts)
        ]
    return pairs


def pad_edges(info, ext, ext_low, halos):
    ext[HALO : 2 * HALO] = ext_low[0:HALO].astype(F32)
    ext[ROWS - HALO : ROWS + HALO] = ext_low[HALO:].astype(F32)
    odd = info[10] % 2 == 1
    for i, is_left in enumerate((odd, jnp.logical_not(odd))):
        at = pl.multiple_of(jnp.where(is_left, 0, HALO + ROWS), HALO)
        ext[pl.ds(at, HALO), :] = halos[i].astype(F32)


EDGES = (0, WINDOWS - 2, WINDOWS - 1)


def place_rows(info, w, ext, out):
    row, low, high, _, _, _ = window_place(info, w)
    values = jnp.where(row_mask(low, high), ext[pl.ds(row, WIN), :], 0.0)
    out[window_at(w), :] = values.astype(BF16)


def place_cotangent(info, w, ext, cot, cot_own):
    row, low, high, own_low, own_high, _ = window_place(info, w)
    values = ext[pl.ds(row, WIN), :]
    cot[window_at(w), :] = jnp.where(row_mask(low, high), values, 0.0).astype(BF16)
    cot_own[window_at(w), :] = jnp.where(row_mask(own_low, own_high), values, 0.0).astype(BF16)


def layout_kernel(info, tokens, cotangent, x_out, cot, cot_own, own, ext, stage, sems):
    copies = copy_all([(tokens, stage.at[0]), (cotangent, stage.at[1])], sems)
    for edge in (slice(0, HALO), slice(HALO + ROWS, 2 * HALO + ROWS)):
        ext[edge, :] = jnp.zeros((HALO, D), F32)
    copies[0].wait()
    ext[HALO : HALO + ROWS] = stage[0].astype(F32)

    def tokens_step(w, carry):
        place_rows(info, w, ext, x_out)
        return carry

    lax.fori_loop(0, WINDOWS, tokens_step, 0, unroll=4)
    copies[1].wait()
    ext[HALO : HALO + ROWS] = stage[1].astype(F32)

    def cotangent_step(w, carry):
        place_cotangent(info, w, ext, cot, cot_own)
        mask = row_mask(*window_place(info, w)[3:5])
        own[window_at(w), :] = jnp.where(mask, jnp.ones((WIN, QUAD), F32), 0.0)
        return carry

    lax.fori_loop(0, WINDOWS, cotangent_step, 0, unroll=4)


def normalized(values):
    mean = jnp.mean(values, axis=-1, keepdims=True)
    centered = values - mean
    variance = jnp.mean(centered * centered, axis=-1, keepdims=True)
    scale = lax.rsqrt(variance + epsilon)
    return centered * scale, scale


def norm_back(grad, unit, scale):
    mean_one = jnp.mean(grad, axis=-1, keepdims=True)
    mean_two = jnp.mean(grad * unit, axis=-1, keepdims=True)
    return scale * (grad - mean_one - unit * mean_two)


def head_masks():
    lane = lax.broadcasted_iota(jnp.int32, (1, QUAD), 1) // HEAD_DIM
    return [(lane == h).astype(BF16) for h in range(QUAD // HEAD_DIM)]


def spread(block, masks):
    return jnp.concatenate([block * mask for mask in masks], axis=0)


def gathered(product, lane):
    parts = [product[h * WIN : (h + 1) * WIN] for h in range(QUAD // HEAD_DIM)]
    return jnp.where(
        lane < 1, parts[0], jnp.where(lane < 2, parts[1], jnp.where(lane < 3, parts[2], parts[3]))
    )


def sum_kernel(plan, *refs):
    ins, outs = refs[: -len(plan)], refs[-len(plan) :]
    for out, pieces in zip(outs, plan):
        for target, source in pieces:
            value = ins[0][source].astype(F32)
            for part in ins[1:]:
                value = value + part[source].astype(F32)
            out[target] = value.astype(out.dtype)


def add(plan, shapes, *operands):
    return pl.pallas_call(
        functools.partial(sum_kernel, plan),
        out_shape=[jax.ShapeDtypeStruct(*s) for s in shapes],
        in_specs=[VMEM] * len(operands),
        out_specs=[VMEM] * len(shapes),
        compiler_params=pltpu.CompilerParams(vmem_limit_bytes=SMALL),
    )(*[near_core(a) for a in operands])


def pair_kernel(keep, *refs):
    for m, (part, out) in enumerate(zip(refs[:4], refs[4:])):
        out[...] = (keep[m].astype(F32) + part[...].astype(F32)).astype(out.dtype)


def add_pairs(keep, parts):
    slot = keep.shape[1:]
    return pl.pallas_call(
        pair_kernel,
        out_shape=[jax.ShapeDtypeStruct(slot, kind) for kind in (F32, BF16, BF16, BF16)],
        in_specs=[VMEM] * 5,
        out_specs=[VMEM] * 4,
        compiler_params=pltpu.CompilerParams(vmem_limit_bytes=SMALL),
    )(*[near_core(a) for a in (keep, *parts)])


def chunks_kernel(keep_first, keep_rest, keep_out, first, rest, out, *refs):
    own, near, pair, *low = refs
    block, share = keep_first.shape[1], keep_out.shape[1] // CHUNKS

    def sums(slot, k):
        a, b, row = (keep_first, first, 0) if k == 0 else (keep_rest, rest, (k - 1) * block)
        rows, out_rows = slice(row, row + block), slice(share * k, share * (k + 1))
        return (
            a[slot, rows].astype(F32) + b[slot, rows].astype(F32),
            keep_out[slot, out_rows].astype(F32) + out[slot, out_rows].astype(F32),
        )

    for slot in range(4):
        for k in range(CHUNKS):
            if k < 2:
                target, row = (own, near)[k].at[slot], 0
            else:
                target, row = ([pair] + low)[slot], (k - 2) * (block + share)
            one, two = sums(slot, k)
            target[row : row + block, :] = one.astype(target.dtype)
            target[row + block : row + block + share, :] = two.astype(target.dtype)


def add_chunks(keeps, parts):
    rows = keeps[0].shape[1] + keeps[2].shape[1] // CHUNKS
    shapes = [((4, rows, D), F32), ((4, rows, D), BF16), ((2 * rows, D), F32)]
    shapes += [((2 * rows, D), BF16)] * 3
    return pl.pallas_call(
        chunks_kernel,
        out_shape=[jax.ShapeDtypeStruct(*s) for s in shapes],
        in_specs=[VMEM] * 6,
        out_specs=[VMEM] * 6,
        compiler_params=pltpu.CompilerParams(vmem_limit_bytes=SMALL),
    )(*[near_core(a) for a in (*keeps, *parts)])


def far_kernel(own, pair, out):
    out[...] = (own[...] + pair[1].astype(F32)).astype(BF16)


def add_far(own, pair):
    return pl.pallas_call(
        far_kernel,
        out_shape=[jax.ShapeDtypeStruct(own.shape, BF16)],
        in_specs=[VMEM] * 2,
        out_specs=[VMEM],
        compiler_params=pltpu.CompilerParams(vmem_limit_bytes=SMALL),
    )(near_core(own), near_core(pair))[0]


def finish_kernel(own, pair, far, grad, *norm_grads):
    total = own[...] + (pair[0].astype(F32) + far[...].astype(F32))
    grad[...] = total[:, : 3 * D]
    rows = jnp.transpose(total[:, 3 * D :])
    for i, norm_grad in enumerate(norm_grads):
        norm_grad[...] = rows[i : i + 1]


def finish_first(own, parts):
    share = own.shape[0]
    shapes = [(share, 3 * D)] + [(1, share)] * 4
    return pl.pallas_call(
        finish_kernel,
        out_shape=[jax.ShapeDtypeStruct(dims, F32) for dims in shapes],
        in_specs=[VMEM] * (1 + len(parts)),
        out_specs=[VMEM] * len(shapes),
        compiler_params=pltpu.CompilerParams(vmem_limit_bytes=SMALL),
    )(*[near_core(a) for a in (own, *parts)])


def add_slots(*operands):
    slot = operands[0].shape[1:]
    plan = [[(slice(None), i)] for i in range(4)]
    return add(plan, [(slot, F32)] + [(slot, BF16)] * 3, *operands)


def prepare_kernel(tokens, cotangent, w_qkv, w_out, w_up, w_down, *refs):
    norms, (with_near, first, with_far, second, up_near, up_far, vectors, sems) = refs[:4], refs[4:]
    share, width = first.shape
    block = w_up.shape[0]
    odd = lax.axis_index("seq") % 2
    pairs = [(norm, vectors.at[i]) for i, norm in enumerate(norms)]
    for target in (with_near, first, with_far):
        pairs += [(w_qkv, target.at[:, : 3 * D]), (w_out, target.at[:, 3 * D : 4 * D])]
    for target, up_target, is_head in ((with_near, up_near, odd), (with_far, up_far, 1 - odd)):
        start = pl.multiple_of((1 - is_head) * (ROWS - HALO), HALO)
        for j in range(2):
            at = width + j * D
            rows = pl.ds(start + j * (HALO // 2), HALO // 2)
            pairs.append((tokens.at[rows, :], target.at[:, at : at + D]))
        pairs.append((cotangent.at[pl.ds(start, HALO), :], up_target.at[2 * block :, :]))
    for target in (second, up_near, up_far):
        pairs += [(w_up, target.at[0:block]), (w_down, target.at[block : 2 * block])]
    first_row = 2 * block
    for i, source in enumerate([w_qkv.at[:, j * D : (j + 1) * D] for j in range(3)] + [w_out]):
        pairs.append((source, second.at[first_row + share * i : first_row + share * (i + 1), :]))
    copies = copy_all(pairs, sems)
    wait_all(copies[: len(norms)])
    columns = jnp.concatenate(
        [vectors[i].astype(F32) for i in range(4)] + [jnp.zeros((NORMS - 4, share), F32)], axis=0
    )
    columns = jnp.transpose(columns).astype(BF16)
    for target in (with_near, first, with_far):
        target[:, 4 * D : width] = columns
    second[first_row + 4 * share :, :] = jnp.concatenate([columns] * (D // NORMS), axis=1)
    wait_all(copies[len(norms) :])


def attention_kernel(direct, info, rows, near, far, x_in, *refs):
    pieces, refs = (refs[:4], refs[4:]) if direct else (refs[:1], refs[1:])
    x_out, qkv_out, mixed_out, probs_out, w_out, norms_out, ext, edges, halos, sems = refs
    width = w_out.shape[1]
    near, far = [
        [a.at[:, width + j * D : width + (j + 1) * D] for j in range(2)] if direct else [a]
        for a in (near, far)
    ]
    edge_copy = copy_all(edge_copies(rows, near, far, edges, halos), sems)
    x_out[...] = x_in[...]
    if direct:
        count, share = pieces[0].shape[1] + 1, pieces[0].shape[2]
        for core, piece in enumerate(pieces[:2]):
            for chip in range(4):
                for k in range(1, count):
                    owner = (2 * chip + (info[9] % 2 ^ core)) * count + (info[10] ^ k)
                    at = pl.multiple_of(owner * share, share)
                    w_out[pl.ds(at, share), :] = piece[chip, k - 1]
        for i, partner in enumerate(ORDER):
            owner = (info[9] ^ partner) * count + info[10]
            at = pl.ds(pl.multiple_of(owner * share, share), share)
            for j in range(5):
                cols = min(D, width - j * D)
                row = D // 4 + j * share
                part = pieces[2 + i // 4][i % 4, row : row + share, 0:cols]
                w_out[at, j * D : j * D + cols] = part
    else:
        w_out[...] = pieces[0][...]
    wait_all(edge_copy)
    pad_edges(info, ext, edges, halos)
    for w in EDGES:
        place_rows(info, w, ext, x_out)
    norms_out[...] = jnp.transpose(w_out[:, 4 * D :].astype(F32))[:8]
    gain, shift = norms_out[0:1], norms_out[1:2]

    def project(i, carry):
        at = tile_at(i)
        unit, _ = normalized(x_out[at, :].astype(F32))
        low = (unit * gain + shift).astype(BF16)
        for part in range(3):
            cols = slice(part * D, (part + 1) * D)
            qkv_out[at, cols] = mm(low, w_out[:, cols]).astype(BF16)
        return carry

    lax.fori_loop(0, WROWS // TILE, project, 0)
    masks = head_masks()
    lane = lax.broadcasted_iota(jnp.int32, (1, QUAD), 1) // HEAD_DIM
    key_row = lax.broadcasted_iota(jnp.int32, (WIN, QUAD), 0)
    query_row = lax.broadcasted_iota(jnp.int32, (WIN, QUAD), 1) % WIN
    key_freq, query_freq = key_row % FREQ, query_row % FREQ

    def attend(w, carry):
        _, low, high, _, _, shift_freq = window_place(info, w)
        at = pl.ds(pl.multiple_of(w * WIN, WIN), WIN)
        key_group = (key_freq + 4 - shift_freq) >> 2
        query_group = (query_freq + 4 - shift_freq) >> 2
        allowed = (key_group == query_group) & (key_row >= low) & (key_row < high)
        quads = range(D // QUAD)
        raw = []
        for quad in quads:
            query = qkv_out[at, quad * QUAD : (quad + 1) * QUAD]
            key = qkv_out[at, D + quad * QUAD : D + (quad + 1) * QUAD]
            raw.append(mm_right(key, spread(query, masks)))
        scores = [jnp.where(allowed, r * HEAD_DIM**-0.5, -1e30) for r in raw]
        weights = [jnp.exp(s - jnp.max(s, axis=0, keepdims=True)) for s in scores]
        probs = [(p / jnp.sum(p, axis=0, keepdims=True)).astype(BF16) for p in weights]
        products = []
        for quad in quads:
            probs_out[at, quad * QUAD : (quad + 1) * QUAD] = probs[quad]
            value = qkv_out[at, 2 * D + quad * QUAD : 2 * D + (quad + 1) * QUAD]
            products.append(mm_left(probs[quad], value))
        for quad in quads:
            mixed = gathered(products[quad], lane).astype(BF16)
            mixed_out[at, quad * QUAD : (quad + 1) * QUAD] = mixed
        return carry

    lax.fori_loop(0, WINDOWS, attend, 0, unroll=12)


def gelu_parts(values):
    half_exp = jnp.exp(-0.5 * values * values)
    t = 1.0 / (1.0 + (0.3275911 * 0.7071067811865476) * jnp.abs(values))
    poly = t * (
        0.5 * 0.254829592
        + t
        * (
            0.5 * -0.284496736
            + t * (0.5 * 1.421413741 + t * (0.5 * -1.453152027 + t * (0.5 * 1.061405429)))
        )
    )
    tail = poly * half_exp
    return jnp.where(values >= 0, 1.0 - tail, tail), half_exp * 0.3989422804014327


def place_feed(info, pieces, up, down):
    block = D // 8
    for piece, partner in zip(pieces, ORDER):
        at = pl.ds(pl.multiple_of((info[9] ^ partner) * block, block), block)
        for c in range(up.shape[0]):
            up[c, at, :] = piece[c, 0:block, :]
            down[c, at, :] = piece[c, block : 2 * block, :]


def feed_rows(at, up, down, normed, cot, hidden, pre):
    values = mm(normed[at, :], up)
    grad_hidden = mm(cot[at, :], down)
    below, density = gelu_parts(values)
    hidden_low = (values * below).astype(BF16)
    grad_low = (grad_hidden * (below + values * density)).astype(BF16)
    hidden[at, :] = hidden_low
    pre[at, :] = grad_low
    return mm_right(hidden_low, down), mm_right(grad_low, up)


def feed_grads(direct, info, row, normed_own, cot_own, hidden, pre, space, refs):
    block = D // 8
    for i, product in enumerate(((normed_own, pre), (cot_own, hidden))):
        grad = mm_left(product[0][...], product[1][...])
        if not direct:
            refs[i][row // (2 * block)] = grad
            continue
        space[0:D, :] = grad
        for partner in range(8):
            at = pl.multiple_of((info[9] ^ partner) * block, block)
            first = row + i * block
            refs[partner & 1][partner >> 1, first : first + block, :] = space[
                pl.ds(at, block), :
            ].astype(BF16)


def feed_first_kernel(
    direct, info, rows, near, far, cot_in, cot_own_in, own, x_in, mixed_in, norms, w_all, *refs
):
    pieces, refs = refs[:2], refs[2:]
    middle, total, grad, normed, normed_own, cot, cot_own = refs[:7]
    grads, (up, down, ext, hidden, pre, edges, halos, sems) = refs[7:9], refs[9:]
    near, far = [[a.at[a.shape[0] - HALO :, :]] for a in (near, far)]
    edge_copy = copy_all(edge_copies(rows, near, far, edges, halos), sems)
    cot[...], cot_own[...] = cot_in[...], cot_own_in[...]
    if direct:
        own_pieces = [piece.at[m : m + 1] for piece in pieces for m in range(4)]
        place_feed(info, own_pieces, up, down)
    else:
        up[...], down[...] = pieces[0][0:1], pieces[1][0:1]
    wait_all(edge_copy)
    pad_edges(info, ext, edges, halos)
    for w in EDGES:
        place_cotangent(info, w, ext, cot, cot_own)
    gain, shift = norms[2:3], norms[3:4]

    def before(i, carry):
        at = tile_at(i)
        values = x_in[at, :].astype(F32) + mm(mixed_in[at, :], w_all[:, 3 * D : 4 * D])
        middle[at, :] = values
        unit, _ = normalized(values)
        low = unit * gain + shift
        normed[at, :] = low.astype(BF16)
        normed_own[at, :] = (low * own[at, 0:1]).astype(BF16)
        return carry

    lax.fori_loop(0, WROWS // TILE, before, 0)
    for i in range(WROWS // TILE):
        at = slice(i * TILE, (i + 1) * TILE)
        branch, back = feed_rows(at, up[0], down[0], normed, cot, hidden, pre)
        total[at, :] = middle[at, :] + branch
        grad[at, :] = back
    feed_grads(direct, info, 0, normed_own, cot_own, hidden, pre, ext, grads)


def feed_rest_kernel(direct, info, total_in, grad_in, normed, normed_own, cot, cot_own, *refs):
    pieces, refs = (refs[:8], refs[8:]) if direct else (refs[:2], refs[2:])
    total, grad, *grads, up, down, ext, hidden, pre = refs
    if direct:
        place_feed(info, pieces, up, down)
    else:
        up[...], down[...] = pieces[0][1:CHUNKS], pieces[1][1:CHUNKS]
    for c in range(CHUNKS - 1):
        for i in range(WROWS // TILE):
            at = slice(i * TILE, (i + 1) * TILE)
            branch, back = feed_rows(at, up[c], down[c], normed, cot, hidden, pre)
            total[at, :] = (total if c else total_in)[at, :] + branch
            grad[at, :] = (grad if c else grad_in)[at, :] + back
        feed_grads(direct, info, c * (D // 4), normed_own, cot_own, hidden, pre, ext, grads)


def feed_last_kernel(direct, info, middle, grad, cot, own, mixed_in, norms, w_all, *refs):
    grad_middle, grad_mixed, grad_norms, *grads, ext, grad_own = refs
    gain = norms[2:3]
    grad_norms[...] = jnp.zeros(grad_norms.shape, F32)
    for i in range(WROWS // TILE):
        at = slice(i * TILE, (i + 1) * TILE)
        unit, scale = normalized(middle[at, :])
        part = grad[at, :]
        masked = part * own[at, 0:1]
        grad_norms[0:1] += jnp.sum(masked * unit, axis=0, keepdims=True)
        grad_norms[1:2] += jnp.sum(masked, axis=0, keepdims=True)
        result = cot[at, :].astype(F32) + norm_back(part * gain, unit, scale)
        grad_middle[at, :] = result
        grad_mixed[at, :] = mm_right(result.astype(BF16), w_all[:, 3 * D : 4 * D]).astype(BF16)
        grad_own[at, :] = (result * own[at, 0:1]).astype(BF16)
    grad_out = mm_left(mixed_in[...], grad_own[...])
    if direct:
        ext[0:D, :] = grad_out
        share = grads[0].shape[1] // CHUNKS
        for partner in range(8):
            for k in range(CHUNKS):
                owner = (info[9] ^ partner) * CHUNKS + (info[10] ^ k)
                row = pl.multiple_of(owner * share, share)
                grads[partner & 1][partner >> 1, share * k : share * (k + 1), :] = ext[
                    pl.ds(row, share), :
                ].astype(BF16)
    else:
        grads[0][...] = grad_out


def finish_rows_kernel(info, values, out, ext):
    unplace(info, values, ext, out)


def unplace(info, values, ext, out):
    def back(w, carry):
        row, low, high, _, _, _ = window_place(info, w)
        at = pl.ds(pl.multiple_of(w * WIN, WIN), WIN)
        place = pl.ds(row, WIN)
        ext[place, :] = jnp.where(row_mask(low, high), values[at, :], ext[place, :])
        return carry

    lax.fori_loop(0, WINDOWS, back, 0, unroll=4)
    out[...] = ext[HALO : HALO + ROWS].astype(BF16)


def back_kernel(
    direct, info, x_in, own, qkv, probs_in, grad_mixed, grad_middle, w_qkv, norms, grad_norms, *refs
):
    grad_tokens, refs = refs[0], refs[1:]
    if direct:
        (keep, send), refs = refs[:2], refs[2:]
    else:
        w_grad, refs = refs[0], refs[1:]
    normed, grad_qkv, gains, grad_w = refs
    masks = head_masks()
    lane = lax.broadcasted_iota(jnp.int32, (1, QUAD), 1) // HEAD_DIM

    def attend_back(w, carry):
        at = window_at(w)
        quads = range(D // QUAD)
        cols = [slice(quad * QUAD, (quad + 1) * QUAD) for quad in quads]
        cols_key = [slice(D + quad * QUAD, D + (quad + 1) * QUAD) for quad in quads]
        cols_value = [slice(2 * D + quad * QUAD, 2 * D + (quad + 1) * QUAD) for quad in quads]
        grad_out = [spread(grad_mixed[at, c], masks) for c in cols]
        grad_probs = [mm_right(qkv[at, c], g) for c, g in zip(cols_value, grad_out)]
        low = [probs_in[at, c] for c in cols]
        probs = [p.astype(F32) for p in low]
        delta = [jnp.sum(p * g, axis=0, keepdims=True) for p, g in zip(probs, grad_probs)]
        grad_scores = [
            (p * (g - d) * HEAD_DIM**-0.5).astype(BF16)
            for p, g, d in zip(probs, grad_probs, delta)
        ]
        grad_value = [mm(p, g) for p, g in zip(low, grad_out)]
        grad_query = [mm_left(g, qkv[at, c]) for g, c in zip(grad_scores, cols_key)]
        grad_key = [mm(g, spread(qkv[at, c], masks)) for g, c in zip(grad_scores, cols)]
        for quad in quads:
            grad_qkv[at, cols_value[quad]] = grad_value[quad].astype(BF16)
            grad_qkv[at, cols_key[quad]] = grad_key[quad].astype(BF16)
            grad_qkv[at, cols[quad]] = gathered(grad_query[quad], lane).astype(BF16)
        return carry

    lax.fori_loop(0, WINDOWS, attend_back, 0, unroll=12)
    gain, shift = norms[0:1], norms[1:2]
    gains[...] = jnp.zeros(gains.shape, F32)

    def after(i, carry):
        at = tile_at(i)
        unit, scale = normalized(x_in[at, :].astype(F32))
        mask = own[at, 0:1]
        normed[at, :] = ((unit * gain + shift) * mask).astype(BF16)
        part = mm_right(grad_qkv[at, :], w_qkv[:, : 3 * D])
        masked = part * mask
        gains[0:1] += jnp.sum(masked * unit, axis=0, keepdims=True)
        gains[1:2] += jnp.sum(masked, axis=0, keepdims=True)
        grad_tokens[at, :] = grad_middle[at, :] + norm_back(part * gain, unit, scale)
        return carry

    lax.fori_loop(0, WROWS // TILE, after, 0)
    gains[2:4] = grad_norms[0:2]
    for part in range(3):
        cols = slice(part * D, (part + 1) * D)
        grad_w[:, cols] = mm_left(normed[...], grad_qkv[:, cols])
    grad_w[:, 3 * D :] = jnp.transpose(gains[...])
    if direct:
        count = keep.shape[1]
        for partner in range(8):
            target = send if partner & 1 else keep
            for k in range(count):
                row = pl.multiple_of(((info[9] ^ partner) * count + (info[10] ^ k)) * 16, 16)
                target[partner >> 1, k] = grad_w[pl.ds(row, 16), :].astype(BF16)
    else:
        w_grad[...] = grad_w[...]


ORDER = (0, 2, 4, 6, 1, 3, 5, 7)
CHIPS = [[0, 2, 4, 6], [1, 3, 5, 7]]
LIMIT = 20 * 1024 * 1024
SMALL = 8 * 1024 * 1024
SMEM = pl.BlockSpec(memory_space=pltpu.SMEM)
VMEM = pl.BlockSpec(memory_space=pltpu.VMEM)
ANY = pl.BlockSpec(memory_space=pl.ANY)


def near_core(array):
    return pltpu.with_memory_space_constraint(array, pltpu.VMEM)


def far_core(array):
    return pltpu.with_memory_space_constraint(array, pltpu.HBM)


def run_kernel(body, out_shape, scratch, flops, info, *operands):
    specs = [ANY if isinstance(a, list) else VMEM for a in operands]
    operands = [a[0] if isinstance(a, list) else near_core(a) for a in operands]
    moved = sum(a.size * a.dtype.itemsize for a in operands)
    return pl.pallas_call(
        body,
        out_shape=out_shape,
        in_specs=[SMEM] + specs,
        out_specs=[VMEM] * len(out_shape),
        scratch_shapes=scratch,
        cost_estimate=pl.CostEstimate(
            flops=flops, bytes_accessed=moved, transcendentals=flops // 1024
        ),
        compiler_params=pltpu.CompilerParams(vmem_limit_bytes=LIMIT),
    )(info, *operands)


def swap(array, axis, bit):
    return lax.ppermute(array, axis, [(i, i ^ bit) for i in range(lax.axis_size(axis))])


def together(*values):
    return lax.optimization_barrier(values)


def along_seq(shard):
    return [swap(shard, "seq", k) for k in (1, 2, 3)]


def along_plane(column):
    return [swap(column, "dp", partner) for partner in (2, 4, 6)]


def along_core(pieces):
    return [swap(piece, "dp", 1) for piece in pieces]


def add_parts(own, parts):
    return own.astype(F32) + sum(part.astype(F32) for part in parts)


def shape(dims, kind):
    return pltpu.VMEM(dims, kind)


def per_device(
    tokens,
    cotangent,
    w_qkv,
    w_out,
    w_up,
    w_down,
    norm1_gain,
    norm1_shift,
    norm2_gain,
    norm2_shift,
    clip_steps,
    window_shifts,
):
    n_dp, n_seq = lax.axis_size("dp"), lax.axis_size("seq")
    share = w_qkv.shape[0]
    direct = n_dp == 8 and share % 16 == 0
    info = jnp.concatenate(
        [
            clip_steps.reshape(3),
            window_shifts.reshape(6),
            lax.axis_index("dp").reshape(1).astype(jnp.int32),
            lax.axis_index("seq").reshape(1).astype(jnp.int32),
        ]
    )
    width = 4 * D + NORMS
    vectors = (norm1_gain, norm1_shift, norm2_gain, norm2_shift)

    def in_hbm(arrays):
        return [[a] for a in arrays]

    x, cot, cot_own, own = run_kernel(
        layout_kernel,
        [shape((WROWS, D), BF16)] * 3 + [shape((WROWS, QUAD), F32)],
        [
            pltpu.VMEM((ROWS + 2 * HALO, D), F32),
            pltpu.VMEM((2, ROWS, D), BF16),
            pltpu.SemaphoreType.DMA((2,)),
        ],
        2 * WROWS * D * D,
        info,
        *in_hbm((tokens, cotangent)),
    )
    if direct:
        with_near, first, with_far, second, up_near, up_far = pl.pallas_call(
            prepare_kernel,
            out_shape=[
                jax.ShapeDtypeStruct((share, width + 2 * D), BF16),
                jax.ShapeDtypeStruct((share, width), BF16),
                jax.ShapeDtypeStruct((share, width + 2 * D), BF16),
                jax.ShapeDtypeStruct((2 * w_up.shape[0] + 5 * share, D), BF16),
                jax.ShapeDtypeStruct((2 * w_up.shape[0] + HALO, D), BF16),
                jax.ShapeDtypeStruct((2 * w_up.shape[0] + HALO, D), BF16),
            ],
            in_specs=[ANY] * 10,
            out_specs=[VMEM] * 6,
            scratch_shapes=[
                pltpu.VMEM((4, 1, share), BF16),
                pltpu.SemaphoreType.DMA((26,)),
            ],
            compiler_params=pltpu.CompilerParams(vmem_limit_bytes=LIMIT),
        )(
            *[
                far_core(a)
                for a in (tokens, cotangent, w_qkv, w_out, w_up, w_down.T)
                + tuple(v.reshape(1, -1) for v in vectors)
            ]
        )
        block = w_up.shape[0]
        own_x, own_y, near, middle, far, x, cot, cot_own, own = together(
            swap(second, "dp", 2),
            swap(second, "dp", 4),
            swap(with_near, "seq", 1),
            swap(first, "seq", 2),
            swap(with_far, "seq", 3),
            x,
            cot,
            cot_own,
            own,
        )
        column = jnp.stack([near[:, :width], middle, far[:, :width]])
        column, second = together(column, second)
        first_half = lax.all_gather(column, "dp", axis_index_groups=CHIPS)
        first_half, own_d, *rest = together(
            first_half,
            swap(second, "dp", 6),
            swap(up_near, "seq", 1),
            swap(second[: 2 * block], "seq", 2),
            swap(up_far, "seq", 3),
        )
        second_own = jnp.stack([second, own_x, own_y, own_d])
        near_cot, far_cot = rest[0], rest[2]
        rest = [rest[0][: 2 * block], rest[1], rest[2][: 2 * block]]
        rest = jnp.stack(rest)
        first_half, rest, second_own = together(first_half, rest, second_own)
        second_own = [second_own, *along_core([second_own])]
        first_all = [first_half, *along_core([first_half]), *second_own]
        second_plane = along_plane(rest)
    else:
        norms = jnp.pad(jnp.stack(vectors, axis=1), ((0, 0), (0, NORMS - 4)))
        first = jnp.concatenate([w_qkv, w_out, norms], axis=1)
        both = jnp.stack([tokens, cotangent])
        head, tail = both[:, :HALO], both[:, ROWS - HALO :]
        odd = lax.axis_index("seq") % 2 == 1
        first_all = [lax.all_gather(first, ("dp", "seq"), axis=0, tiled=True)]
        up_all = lax.all_gather(lax.all_gather(w_up, "dp", axis=0, tiled=True), "seq", axis=0)
        down_all = lax.all_gather(lax.all_gather(w_down.T, "dp", axis=0, tiled=True), "seq", axis=0)
        second_own = second_all = [up_all, down_all]
        from_left = lax.ppermute(tail, "seq", [(i, i + 1) for i in range(n_seq - 1)])
        from_right = lax.ppermute(head, "seq", [(i + 1, i) for i in range(n_seq - 1)])
        near, near_cot = jnp.where(odd, from_left, from_right)
        far, far_cot = jnp.where(odd, from_right, from_left)

    x, qkv, mixed, probs, w_all, norms_all = run_kernel(
        functools.partial(attention_kernel, direct),
        [
            shape((WROWS, D), BF16),
            shape((WROWS, 3 * D), BF16),
            shape((WROWS, D), BF16),
            shape((WROWS, D), BF16),
            shape((D, width), BF16),
            shape((8, D), F32),
        ],
        [
            pltpu.VMEM((ROWS + 2 * HALO, D), F32),
            pltpu.VMEM((3 * HALO, D), BF16),
            pltpu.VMEM((2, HALO, D), BF16),
            pltpu.SemaphoreType.DMA((6,)),
        ],
        2 * WROWS * D * 3 * D * 2,
        info,
        *in_hbm((tokens, near, far)),
        x,
        *first_all,
    )
    if direct:
        grads_shape = [shape((4, 2 * block, D), BF16)] * 2
    else:
        grads_shape = [shape((1, D, CHUNK), F32)] * 2
    *state, keep, send = run_kernel(
        functools.partial(feed_first_kernel, direct),
        [shape((WROWS, D), F32)] * 3
        + [shape((WROWS, D), BF16)] * 4
        + grads_shape,
        [
            pltpu.VMEM((1, D, CHUNK), BF16),
            pltpu.VMEM((1, D, CHUNK), BF16),
            pltpu.VMEM((ROWS + 2 * HALO, D), F32),
            pltpu.VMEM((WROWS, CHUNK), BF16),
            pltpu.VMEM((WROWS, CHUNK), BF16),
            pltpu.VMEM((3 * HALO, D), BF16),
            pltpu.VMEM((2, HALO, D), BF16),
            pltpu.SemaphoreType.DMA((4,)),
        ],
        2 * WROWS * D * (6 * CHUNK + D),
        info,
        *in_hbm((cotangent, near_cot, far_cot)),
        cot,
        cot_own,
        own,
        x,
        mixed,
        norms_all,
        w_all,
        *second_own,
    )
    if direct:
        *second_plane, total = together(*second_plane, state[1])
        state[1] = total
        second_plane = [rest, *second_plane]
        second_all = second_plane + along_core(second_plane)
        first_grads = [keep, send]
        extra = (CHUNKS - 1) * 2 * block
        grads_shape = [shape((4, extra, D), BF16)] * 2
        out_shape = [shape((4, n_seq * share, D), BF16)] * 2
    else:
        first_grads = [keep, send]
        grads_shape = [shape((CHUNKS - 1, D, CHUNK), F32)] * 2
        out_shape = [shape((D, D), F32)]
    middle, total, grad, normed, normed_own, cot, cot_own = state
    total, grad, *grads = run_kernel(
        functools.partial(feed_rest_kernel, direct),
        [shape((WROWS, D), F32)] * 2 + grads_shape,
        [
            pltpu.VMEM((CHUNKS - 1, D, CHUNK), BF16),
            pltpu.VMEM((CHUNKS - 1, D, CHUNK), BF16),
            pltpu.VMEM((D, D), F32),
            pltpu.VMEM((WROWS, CHUNK), BF16),
            pltpu.VMEM((WROWS, CHUNK), BF16),
        ],
        2 * WROWS * D * 18 * CHUNK,
        info,
        total,
        grad,
        normed,
        normed_own,
        cot,
        cot_own,
        *second_all,
    )
    if direct:
        from_core = along_core([first_grads[1], grads[1]])
    grad_middle, grad_mixed, grad_norms, *out_grads = run_kernel(
        functools.partial(feed_last_kernel, direct),
        [
            shape((WROWS, D), F32),
            shape((WROWS, D), BF16),
            shape((8, D), F32),
            *out_shape,
        ],
        [pltpu.VMEM((D, D), F32), pltpu.VMEM((WROWS, D), BF16)],
        2 * WROWS * D * 2 * D,
        info,
        middle,
        grad,
        cot,
        own,
        mixed,
        norms_all,
        w_all,
    )
    if direct:
        from_core = [*from_core, *along_core(out_grads[1:])]
        keeps, from_core = [first_grads[0], grads[0], out_grads[0]], together(*from_core)
        own_pair, to_near, pair, *low = add_chunks(keeps, from_core)
        to_near, *low, grad_mixed = together(to_near, *low, grad_mixed)
        parts = [swap(part, "dp", 2 * m + 2) for m, part in enumerate(low)]
        parts.append(swap(to_near, "seq", 1))
        grads_shape = [shape((4, n_seq, share, 3 * D + NORMS), BF16)] * 2
    else:
        grads_up, grads_down = [
            jnp.concatenate([a, b], axis=0) for a, b in zip(first_grads, grads)
        ]
        grad_up = lax.psum_scatter(grads_up, "seq", scatter_dimension=0)
        grad_up = lax.psum_scatter(grad_up, "dp", scatter_dimension=0, tiled=True)
        grad_down = lax.psum_scatter(grads_down, "seq", scatter_dimension=0)
        grad_down = lax.psum_scatter(grad_down, "dp", scatter_dimension=0, tiled=True).T
        grad_out = lax.psum_scatter(out_grads[0], ("dp", "seq"), scatter_dimension=0, tiled=True)
        grads_shape = [shape((D, 3 * D + NORMS), F32)]
    grad_tokens, *grads = run_kernel(
        functools.partial(back_kernel, direct),
        [shape((WROWS, D), F32), *grads_shape],
        [
            pltpu.VMEM((WROWS, D), BF16),
            pltpu.VMEM((WROWS, 3 * D), BF16),
            pltpu.VMEM((NORMS, D), F32),
            pltpu.VMEM((D, 3 * D + NORMS), F32),
        ],
        2 * WROWS * D * (6 * D + 3 * D),
        info,
        x,
        own,
        qkv,
        probs,
        grad_mixed,
        grad_middle,
        w_all,
        norms_all,
        grad_norms,
    )
    if direct:
        grad_tokens, *grads = together(grad_tokens, *grads)
    out, tokens_grad = [
        run_kernel(
            finish_rows_kernel,
            [jax.ShapeDtypeStruct((ROWS, D), BF16)],
            [pltpu.VMEM((ROWS + 2 * HALO, D), F32)],
            2 * WROWS * D * D,
            info,
            values,
        )[0]
        for values in (total, grad_tokens)
    ]
    if direct:
        keep, send, *parts, from_near = together(*grads, *parts)
        rows = 2 * block + share
        plan = [[(slice(None), (slice(k * rows, (k + 1) * rows),))] for k in range(2)]
        low = add(plan, [((rows, D), BF16)] * 2, pair, *parts)
        second_far, from_near_far = together(low[1], swap(low[0], "seq", 1))
        (second_far,) = add([[(slice(None), slice(None))]], [(low[1].shape, BF16)], second_far, from_near_far)
        second = [swap(second_far, "seq", 3)]
        from_core, tokens_grad = together(*along_core([send]), tokens_grad)
        first_pair, *first_low = add_slots(keep, from_core)
        first = [swap(part, "dp", 2 * m + 2) for m, part in enumerate(first_low)]
        own_pair, *own_low = add_slots(own_pair, from_near)
        *first, second[0], own0, own1, own2, out = together(*first, *second, *own_low, out)
        everything = slice(None)
        slot = first_pair.shape[1:]
        first_own, to_near, to_far = add(
            [[(everything, 0)], [(0, 1), (1, 2)], [(everything, 3)]],
            [(slot, F32), ((2, *slot), BF16), (slot, F32)],
            first_pair,
            *first,
        )
        near_part = swap(to_near, "seq", 1)
        first_parts = [near_part, swap(add_far(to_far, near_part), "seq", 3)]
        own_parts = [swap(part, "dp", 2 * m + 2) for m, part in enumerate((own0, own1, own2))]
        everything, bounds = slice(None), (0, block, 2 * block, rows)
        grad_up, grad_down, grad_out = add(
            [[(everything, (slice(a, b),))] for a, b in zip(bounds, bounds[1:])],
            [((b - a, D), F32) for a, b in zip(bounds, bounds[1:])],
            own_pair,
            *own_parts,
            *second,
        )
        first_own, grad_up, grad_down, grad_out = together(
            first_own, grad_up, grad_down, grad_out
        )
        grad_down = grad_down.T
        w_qkv_grad, *norm_grads = finish_first(first_own, first_parts)
        norm_grads = [grad.reshape(share) for grad in norm_grads]
    else:
        first_sum = lax.psum_scatter(grads[0], ("dp", "seq"), scatter_dimension=0, tiled=True)
        w_qkv_grad = first_sum[:, : 3 * D]
        norm_grads = [first_sum[:, 3 * D + i] for i in range(4)]
    return (
        out,
        tokens_grad,
        w_qkv_grad,
        grad_out,
        grad_up,
        grad_down,
        *norm_grads,
    )


def solution(mesh):
    rows = P(("dp", "seq"), None)
    vector = P(("dp", "seq"))
    return jax.shard_map(
        per_device,
        mesh=mesh,
        in_specs=(
            rows,
            rows,
            rows,
            rows,
            P("dp", "seq"),
            P("seq", "dp"),
            vector,
            vector,
            vector,
            vector,
            P("dp", None),
            P("dp", None, None),
        ),
        out_specs=(
            rows,
            rows,
            rows,
            rows,
            P("dp", "seq"),
            P("seq", "dp"),
            vector,
            vector,
            vector,
            vector,
        ),
        check_vma=False,
    )
```

```python
import functools

import jax
import jax.numpy as jnp
from jax import lax
from jax.experimental import pallas as pl
from jax.experimental.pallas import tpu as pltpu
from jax.sharding import PartitionSpec as P

D = 512
HEADS = 16
HEAD_DIM = D // HEADS
FF = 2048
FREQ = 8
STEPS_DEV = 88
HALO = 4 * FREQ
ROWS = STEPS_DEV * FREQ
WIN = 4 * FREQ
WINDOWS = STEPS_DEV // 4 + 2
WROWS = WINDOWS * WIN
TILE = 768
QUAD = 128
NORMS = 128
CHUNK = 512
CHUNKS = FF // CHUNK
epsilon = 1e-06
F32 = jnp.float32
BF16 = jnp.bfloat16


def mm(left, right):
    return jnp.dot(left, right, preferred_element_type=F32)


def mm_right(left, right):
    return lax.dot_general(left, right, (((1,), (1,)), ((), ())), preferred_element_type=F32)


def mm_left(left, right):
    return lax.dot_general(left, right, (((0,), (0,)), ((), ())), preferred_element_type=F32)


def window_place(info, w):
    lead, mid, trail = info[0], info[1], info[2]
    seq = info[10]
    base = seq * STEPS_DEV
    n_lead = lead // 4 + 1
    n_mid = mid // 4 + 1
    index = jnp.where(seq == 0, 0, base // 4 + 1) + w
    in_mid = index >= n_lead
    in_trail = index >= n_lead + n_mid
    before = jnp.where(in_trail, n_lead + n_mid, jnp.where(in_mid, n_lead, 0))
    start = jnp.where(in_trail, lead + mid, jnp.where(in_mid, lead, 0))
    steps = jnp.where(in_trail, trail, jnp.where(in_mid, mid, lead))
    shift_time = jnp.where(in_trail, info[7], jnp.where(in_mid, info[5], info[3]))
    shift_freq = jnp.where(in_trail, info[8], jnp.where(in_mid, info[6], info[4]))
    first = start - 4 + shift_time + 4 * (index - before)
    here = first < base + STEPS_DEV
    low = jnp.clip(start - first, 0, 4)
    high = jnp.where(here, jnp.clip(start + steps - first, 0, 4), 0)
    own_low = jnp.clip(base - first, 0, 4)
    own_high = jnp.clip(base + STEPS_DEV - first, 0, 4)
    row = jnp.clip(first - base + 4, 0, STEPS_DEV + 4) * FREQ
    row = pl.multiple_of(row, FREQ)
    return (
        row,
        low * FREQ,
        high * FREQ,
        jnp.maximum(low, own_low) * FREQ,
        jnp.minimum(high, own_high) * FREQ,
        shift_freq,
    )


def window_at(w):
    return pl.ds(pl.multiple_of(w * WIN, WIN), WIN)


def tile_at(i):
    return pl.ds(pl.multiple_of(i * TILE, TILE), TILE)


def row_mask(low, high):
    index = lax.broadcasted_iota(jnp.int32, (WIN, 1), 0)
    return (index >= low) & (index < high)


def copy_all(pairs, sems, first=0):
    copies = [
        pltpu.make_async_copy(source, target, sems.at[first + i])
        for i, (source, target) in enumerate(pairs)
    ]
    for copy in copies:
        copy.start()
    return copies


def wait_all(copies):
    for copy in copies:
        copy.wait()


def edge_copies(rows, near, far, ext_low, halos):
    pairs = [
        (rows.at[0:HALO, :], ext_low.at[0:HALO, :]),
        (rows.at[ROWS - 2 * HALO :, :], ext_low.at[HALO:, :]),
    ]
    for i, parts in enumerate((near, far)):
        size = HALO // len(parts)
        pairs += [
            (part, halos.at[i, j * size : (j + 1) * size, :]) for j, part in enumerate(parts)
        ]
    return pairs


def pad_edges(info, ext, ext_low, halos):
    ext[HALO : 2 * HALO] = ext_low[0:HALO].astype(F32)
    ext[ROWS - HALO : ROWS + HALO] = ext_low[HALO:].astype(F32)
    odd = info[10] % 2 == 1
    for i, is_left in enumerate((odd, jnp.logical_not(odd))):
        at = pl.multiple_of(jnp.where(is_left, 0, HALO + ROWS), HALO)
        ext[pl.ds(at, HALO), :] = halos[i].astype(F32)


EDGES = (0, WINDOWS - 2, WINDOWS - 1)


def place_rows(info, w, ext, out):
    row, low, high, _, _, _ = window_place(info, w)
    values = jnp.where(row_mask(low, high), ext[pl.ds(row, WIN), :], 0.0)
    out[window_at(w), :] = values.astype(BF16)


def place_cotangent(info, w, ext, cot, cot_own):
    row, low, high, own_low, own_high, _ = window_place(info, w)
    values = ext[pl.ds(row, WIN), :]
    cot[window_at(w), :] = jnp.where(row_mask(low, high), values, 0.0).astype(BF16)
    cot_own[window_at(w), :] = jnp.where(row_mask(own_low, own_high), values, 0.0).astype(BF16)


def layout_kernel(info, tokens, cotangent, x_out, cot, cot_own, own, ext, stage, sems):
    copies = copy_all([(tokens, stage.at[0]), (cotangent, stage.at[1])], sems)
    for edge in (slice(0, HALO), slice(HALO + ROWS, 2 * HALO + ROWS)):
        ext[edge, :] = jnp.zeros((HALO, D), F32)
    copies[0].wait()
    ext[HALO : HALO + ROWS] = stage[0].astype(F32)

    def tokens_step(w, carry):
        place_rows(info, w, ext, x_out)
        return carry

    lax.fori_loop(0, WINDOWS, tokens_step, 0, unroll=4)
    copies[1].wait()
    ext[HALO : HALO + ROWS] = stage[1].astype(F32)

    def cotangent_step(w, carry):
        place_cotangent(info, w, ext, cot, cot_own)
        mask = row_mask(*window_place(info, w)[3:5])
        own[window_at(w), :] = jnp.where(mask, jnp.ones((WIN, QUAD), F32), 0.0)
        return carry

    lax.fori_loop(0, WINDOWS, cotangent_step, 0, unroll=4)


def normalized(values):
    mean = jnp.mean(values, axis=-1, keepdims=True)
    centered = values - mean
    variance = jnp.mean(centered * centered, axis=-1, keepdims=True)
    scale = lax.rsqrt(variance + epsilon)
    return centered * scale, scale


def norm_back(grad, unit, scale):
    mean_one = jnp.mean(grad, axis=-1, keepdims=True)
    mean_two = jnp.mean(grad * unit, axis=-1, keepdims=True)
    return scale * (grad - mean_one - unit * mean_two)


def head_masks():
    lane = lax.broadcasted_iota(jnp.int32, (1, QUAD), 1) // HEAD_DIM
    return [(lane == h).astype(BF16) for h in range(QUAD // HEAD_DIM)]


def spread(block, masks):
    return jnp.concatenate([block * mask for mask in masks], axis=0)


def gathered(product, lane):
    parts = [product[h * WIN : (h + 1) * WIN] for h in range(QUAD // HEAD_DIM)]
    return jnp.where(
        lane < 1, parts[0], jnp.where(lane < 2, parts[1], jnp.where(lane < 3, parts[2], parts[3]))
    )


def sum_kernel(plan, *refs):
    ins, outs = refs[: -len(plan)], refs[-len(plan) :]
    for out, pieces in zip(outs, plan):
        for target, source in pieces:
            value = ins[0][source].astype(F32)
            for part in ins[1:]:
                value = value + part[source].astype(F32)
            out[target] = value.astype(out.dtype)


def add(plan, shapes, *operands):
    return pl.pallas_call(
        functools.partial(sum_kernel, plan),
        out_shape=[jax.ShapeDtypeStruct(*s) for s in shapes],
        in_specs=[VMEM] * len(operands),
        out_specs=[VMEM] * len(shapes),
        compiler_params=pltpu.CompilerParams(vmem_limit_bytes=SMALL),
    )(*[near_core(a) for a in operands])


def small_call(body, shapes, *operands, flops=0):
    moved = sum(a.size * a.dtype.itemsize for a in operands)
    return pl.pallas_call(
        body,
        out_shape=[jax.ShapeDtypeStruct(*s) for s in shapes],
        in_specs=[VMEM] * len(operands),
        out_specs=[VMEM] * len(shapes),
        cost_estimate=pl.CostEstimate(flops=flops, bytes_accessed=moved, transcendentals=0),
        compiler_params=pltpu.CompilerParams(vmem_limit_bytes=SMALL),
    )(*[near_core(a) for a in operands])


def stack_kernel(*refs):
    *parts, out = refs
    for i, part in enumerate(parts):
        out[i] = part[:, 0 : out.shape[2]]


def chunks_kernel(keep_first, keep_rest, keep_out, first, rest, out, *refs):
    own, near, pair, *low = refs
    block, share = keep_first.shape[1], keep_out.shape[1] // CHUNKS

    def sums(slot, k):
        a, b, row = (keep_first, first, 0) if k == 0 else (keep_rest, rest, (k - 1) * block)
        rows, out_rows = slice(row, row + block), slice(share * k, share * (k + 1))
        return (
            a[slot, rows].astype(F32) + b[slot, rows].astype(F32),
            keep_out[slot, out_rows].astype(F32) + out[slot, out_rows].astype(F32),
        )

    for slot in range(4):
        for k in range(CHUNKS):
            if k < 2:
                target, row = (own, near)[k].at[slot], 0
            else:
                target, row = ([pair] + low)[slot], (k - 2) * (block + share)
            one, two = sums(slot, k)
            target[row : row + block, :] = one.astype(target.dtype)
            target[row + block : row + block + share, :] = two.astype(target.dtype)


def add_chunks(keeps, parts):
    rows = keeps[0].shape[1] + keeps[2].shape[1] // CHUNKS
    shapes = [((4, rows, D), F32), ((4, rows, D), BF16), ((2 * rows, D), F32)]
    shapes += [((2 * rows, D), BF16)] * 3
    return pl.pallas_call(
        chunks_kernel,
        out_shape=[jax.ShapeDtypeStruct(*s) for s in shapes],
        in_specs=[VMEM] * 6,
        out_specs=[VMEM] * 6,
        compiler_params=pltpu.CompilerParams(vmem_limit_bytes=SMALL),
    )(*[near_core(a) for a in (*keeps, *parts)])


def far_kernel(own, pair, out):
    out[...] = (own[...] + pair[1].astype(F32)).astype(BF16)


def finish_kernel(chunk, first, one, two, three, second, pair, far, *outs):
    total = chunk[...] + second[...].astype(F32)
    for part in (one, two, three):
        total = total + part[...].astype(F32)
    row = 0
    for out in outs[:3]:
        out[...] = total[row : row + out.shape[0]]
        row += out.shape[0]
    total = first[...] + (pair[0].astype(F32) + far[...].astype(F32))
    outs[3][...] = total[:, : 3 * D]
    rows = jnp.transpose(total[:, 3 * D :])
    for i, out in enumerate(outs[4:]):
        out[...] = rows[i : i + 1]


def add_slots(*operands):
    slot = operands[0].shape[1:]
    plan = [[(slice(None), i)] for i in range(4)]
    return add(plan, [(slot, F32)] + [(slot, BF16)] * 3, *operands)


def prepare_kernel(tokens, cotangent, w_qkv, w_out, w_up, w_down, *refs):
    norms, (with_near, first, with_far, second, up_near, up_far, vectors, sems) = refs[:4], refs[4:]
    share, width = first.shape
    block = w_up.shape[0]
    odd = lax.axis_index("seq") % 2
    pairs = [(norm, vectors.at[i]) for i, norm in enumerate(norms)]
    for target in (with_near, first, with_far):
        pairs += [(w_qkv, target.at[:, : 3 * D]), (w_out, target.at[:, 3 * D : 4 * D])]
    for target, up_target, is_head in ((with_near, up_near, odd), (with_far, up_far, 1 - odd)):
        start = pl.multiple_of((1 - is_head) * (ROWS - HALO), HALO)
        for j in range(2):
            at = width + j * D
            rows = pl.ds(start + j * (HALO // 2), HALO // 2)
            pairs.append((tokens.at[rows, :], target.at[:, at : at + D]))
        pairs.append((cotangent.at[pl.ds(start, HALO), :], up_target.at[2 * block :, :]))
    for target in (second, up_near, up_far):
        pairs += [(w_up, target.at[0:block]), (w_down, target.at[block : 2 * block])]
    first_row = 2 * block
    for i, source in enumerate([w_qkv.at[:, j * D : (j + 1) * D] for j in range(3)] + [w_out]):
        pairs.append((source, second.at[first_row + share * i : first_row + share * (i + 1), :]))
    copies = copy_all(pairs, sems)
    wait_all(copies[: len(norms)])
    columns = jnp.concatenate(
        [vectors[i].astype(F32) for i in range(4)] + [jnp.zeros((NORMS - 4, share), F32)], axis=0
    )
    columns = jnp.transpose(columns).astype(BF16)
    for target in (with_near, first, with_far):
        target[:, 4 * D : width] = columns
    second[first_row + 4 * share :, :] = jnp.concatenate([columns] * (D // NORMS), axis=1)
    wait_all(copies[len(norms) :])


def attention_kernel(direct, info, rows, near, far, x_in, *refs):
    pieces, refs = (refs[:4], refs[4:]) if direct else (refs[:1], refs[1:])
    x_out, qkv_out, mixed_out, probs_out, w_out, norms_out, ext, edges, halos, sems = refs
    width = w_out.shape[1]
    near, far = [
        [a.at[:, width + j * D : width + (j + 1) * D] for j in range(2)] if direct else [a]
        for a in (near, far)
    ]
    edge_copy = copy_all(edge_copies(rows, near, far, edges, halos), sems)
    x_out[...] = x_in[...]
    if direct:
        count, share = pieces[0].shape[1] + 1, pieces[0].shape[2]
        for core, piece in enumerate(pieces[:2]):
            for chip in range(4):
                for k in range(1, count):
                    owner = (2 * chip + (info[9] % 2 ^ core)) * count + (info[10] ^ k)
                    at = pl.multiple_of(owner * share, share)
                    w_out[pl.ds(at, share), :] = piece[chip, k - 1]
        for i, partner in enumerate(ORDER):
            owner = (info[9] ^ partner) * count + info[10]
            at = pl.ds(pl.multiple_of(owner * share, share), share)
            for j in range(5):
                cols = min(D, width - j * D)
                row = D // 4 + j * share
                part = pieces[2 + i // 4][i % 4, row : row + share, 0:cols]
                w_out[at, j * D : j * D + cols] = part
    else:
        w_out[...] = pieces[0][...]
    wait_all(edge_copy)
    pad_edges(info, ext, edges, halos)
    for w in EDGES:
        place_rows(info, w, ext, x_out)
    norms_out[...] = jnp.transpose(w_out[:, 4 * D :].astype(F32))[:8]
    gain, shift = norms_out[0:1], norms_out[1:2]

    def project(i, carry):
        at = tile_at(i)
        unit, _ = normalized(x_out[at, :].astype(F32))
        low = (unit * gain + shift).astype(BF16)
        for part in range(3):
            cols = slice(part * D, (part + 1) * D)
            qkv_out[at, cols] = mm(low, w_out[:, cols]).astype(BF16)
        return carry

    lax.fori_loop(0, WROWS // TILE, project, 0)
    masks = head_masks()
    lane = lax.broadcasted_iota(jnp.int32, (1, QUAD), 1) // HEAD_DIM
    key_row = lax.broadcasted_iota(jnp.int32, (WIN, QUAD), 0)
    query_row = lax.broadcasted_iota(jnp.int32, (WIN, QUAD), 1) % WIN
    key_freq, query_freq = key_row % FREQ, query_row % FREQ

    def attend(w, carry):
        _, low, high, _, _, shift_freq = window_place(info, w)
        at = pl.ds(pl.multiple_of(w * WIN, WIN), WIN)
        key_group = (key_freq + 4 - shift_freq) >> 2
        query_group = (query_freq + 4 - shift_freq) >> 2
        allowed = (key_group == query_group) & (key_row >= low) & (key_row < high)
        quads = range(D // QUAD)
        raw = []
        for quad in quads:
            query = qkv_out[at, quad * QUAD : (quad + 1) * QUAD]
            key = qkv_out[at, D + quad * QUAD : D + (quad + 1) * QUAD]
            raw.append(mm_right(key, spread(query, masks)))
        scores = [jnp.where(allowed, r * HEAD_DIM**-0.5, -1e30) for r in raw]
        weights = [jnp.exp(s - jnp.max(s, axis=0, keepdims=True)) for s in scores]
        probs = [(p / jnp.sum(p, axis=0, keepdims=True)).astype(BF16) for p in weights]
        products = []
        for quad in quads:
            probs_out[at, quad * QUAD : (quad + 1) * QUAD] = probs[quad]
            value = qkv_out[at, 2 * D + quad * QUAD : 2 * D + (quad + 1) * QUAD]
            products.append(mm_left(probs[quad], value))
        for quad in quads:
            mixed = gathered(products[quad], lane).astype(BF16)
            mixed_out[at, quad * QUAD : (quad + 1) * QUAD] = mixed
        return carry

    lax.fori_loop(0, WINDOWS, attend, 0, unroll=12)


def gelu_parts(values):
    half_exp = jnp.exp(-0.5 * values * values)
    t = 1.0 / (1.0 + (0.3275911 * 0.7071067811865476) * jnp.abs(values))
    poly = t * (
        0.5 * 0.254829592
        + t
        * (
            0.5 * -0.284496736
            + t * (0.5 * 1.421413741 + t * (0.5 * -1.453152027 + t * (0.5 * 1.061405429)))
        )
    )
    tail = poly * half_exp
    return jnp.where(values >= 0, 1.0 - tail, tail), half_exp * 0.3989422804014327


def place_feed(info, pieces, up, down):
    block = D // 8
    for piece, partner in zip(pieces, ORDER):
        at = pl.ds(pl.multiple_of((info[9] ^ partner) * block, block), block)
        for c in range(up.shape[0]):
            up[c, at, :] = piece[c, 0:block, :]
            down[c, at, :] = piece[c, block : 2 * block, :]


def feed_rows(at, up, down, normed, cot, hidden, pre):
    values = mm(normed[at, :], up)
    grad_hidden = mm(cot[at, :], down)
    below, density = gelu_parts(values)
    hidden_low = (values * below).astype(BF16)
    grad_low = (grad_hidden * (below + values * density)).astype(BF16)
    hidden[at, :] = hidden_low
    pre[at, :] = grad_low
    return mm_right(hidden_low, down), mm_right(grad_low, up)


def feed_grads(direct, info, row, normed_own, cot_own, hidden, pre, space, refs):
    block = D // 8
    for i, product in enumerate(((normed_own, pre), (cot_own, hidden))):
        grad = mm_left(product[0][...], product[1][...])
        if not direct:
            refs[i][row // (2 * block)] = grad
            continue
        space[0:D, :] = grad
        for partner in range(8):
            at = pl.multiple_of((info[9] ^ partner) * block, block)
            first = row + i * block
            refs[partner & 1][partner >> 1, first : first + block, :] = space[
                pl.ds(at, block), :
            ].astype(BF16)


def feed_first_kernel(
    direct, info, rows, near, far, cot_in, cot_own_in, own, x_in, mixed_in, norms, w_all, *refs
):
    pieces, refs = refs[:2], refs[2:]
    middle, total, grad, normed, normed_own, cot, cot_own = refs[:7]
    grads, (up, down, ext, hidden, pre, edges, halos, sems) = refs[7:9], refs[9:]
    near, far = [[a.at[a.shape[0] - HALO :, :]] for a in (near, far)]
    edge_copy = copy_all(edge_copies(rows, near, far, edges, halos), sems)
    cot[...], cot_own[...] = cot_in[...], cot_own_in[...]
    if direct:
        own_pieces = [piece.at[m : m + 1] for piece in pieces for m in range(4)]
        place_feed(info, own_pieces, up, down)
    else:
        up[...], down[...] = pieces[0][0:1], pieces[1][0:1]
    wait_all(edge_copy)
    pad_edges(info, ext, edges, halos)
    for w in EDGES:
        place_cotangent(info, w, ext, cot, cot_own)
    gain, shift = norms[2:3], norms[3:4]

    def before(i, carry):
        at = tile_at(i)
        values = x_in[at, :].astype(F32) + mm(mixed_in[at, :], w_all[:, 3 * D : 4 * D])
        middle[at, :] = values
        unit, _ = normalized(values)
        low = unit * gain + shift
        normed[at, :] = low.astype(BF16)
        normed_own[at, :] = (low * own[at, 0:1]).astype(BF16)
        return carry

    lax.fori_loop(0, WROWS // TILE, before, 0)
    for i in range(WROWS // TILE):
        at = slice(i * TILE, (i + 1) * TILE)
        branch, back = feed_rows(at, up[0], down[0], normed, cot, hidden, pre)
        total[at, :] = middle[at, :] + branch
        grad[at, :] = back
    feed_grads(direct, info, 0, normed_own, cot_own, hidden, pre, ext, grads)


def feed_rest_kernel(direct, info, total_in, grad_in, normed, normed_own, cot, cot_own, *refs):
    pieces, refs = (refs[:8], refs[8:]) if direct else (refs[:2], refs[2:])
    total, grad, *grads, up, down, ext, hidden, pre = refs
    if direct:
        place_feed(info, pieces, up, down)
    else:
        up[...], down[...] = pieces[0][1:CHUNKS], pieces[1][1:CHUNKS]
    for c in range(CHUNKS - 1):
        for i in range(WROWS // TILE):
            at = slice(i * TILE, (i + 1) * TILE)
            branch, back = feed_rows(at, up[c], down[c], normed, cot, hidden, pre)
            total[at, :] = (total if c else total_in)[at, :] + branch
            grad[at, :] = (grad if c else grad_in)[at, :] + back
        feed_grads(direct, info, c * (D // 4), normed_own, cot_own, hidden, pre, ext, grads)


def feed_last_kernel(direct, info, middle, grad, cot, own, mixed_in, norms, w_all, *refs):
    grad_middle, grad_mixed, grad_norms, *grads, ext, grad_own = refs
    gain = norms[2:3]
    grad_norms[...] = jnp.zeros(grad_norms.shape, F32)
    for i in range(WROWS // TILE):
        at = slice(i * TILE, (i + 1) * TILE)
        unit, scale = normalized(middle[at, :])
        part = grad[at, :]
        masked = part * own[at, 0:1]
        grad_norms[0:1] += jnp.sum(masked * unit, axis=0, keepdims=True)
        grad_norms[1:2] += jnp.sum(masked, axis=0, keepdims=True)
        result = cot[at, :].astype(F32) + norm_back(part * gain, unit, scale)
        grad_middle[at, :] = result
        grad_mixed[at, :] = mm_right(result.astype(BF16), w_all[:, 3 * D : 4 * D]).astype(BF16)
        grad_own[at, :] = (result * own[at, 0:1]).astype(BF16)
    grad_out = mm_left(mixed_in[...], grad_own[...])
    if direct:
        ext[0:D, :] = grad_out
        share = grads[0].shape[1] // CHUNKS
        for partner in range(8):
            for k in range(CHUNKS):
                owner = (info[9] ^ partner) * CHUNKS + (info[10] ^ k)
                row = pl.multiple_of(owner * share, share)
                grads[partner & 1][partner >> 1, share * k : share * (k + 1), :] = ext[
                    pl.ds(row, share), :
                ].astype(BF16)
    else:
        grads[0][...] = grad_out


def finish_rows_kernel(info, values, out, ext):
    unplace(info, values, ext, out)


def unplace(info, values, ext, out):
    def back(w, carry):
        row, low, high, _, _, _ = window_place(info, w)
        at = pl.ds(pl.multiple_of(w * WIN, WIN), WIN)
        place = pl.ds(row, WIN)
        ext[place, :] = jnp.where(row_mask(low, high), values[at, :], ext[place, :])
        return carry

    lax.fori_loop(0, WINDOWS, back, 0, unroll=4)
    out[...] = ext[HALO : HALO + ROWS].astype(BF16)


def back_kernel(
    direct, info, x_in, own, qkv, probs_in, grad_mixed, grad_middle, w_qkv, norms, grad_norms, *refs
):
    grad_tokens, refs = refs[0], refs[1:]
    if direct:
        (keep, send), refs = refs[:2], refs[2:]
    else:
        w_grad, refs = refs[0], refs[1:]
    normed, grad_qkv, gains, grad_w = refs
    masks = head_masks()
    lane = lax.broadcasted_iota(jnp.int32, (1, QUAD), 1) // HEAD_DIM

    def attend_back(w, carry):
        at = window_at(w)
        quads = range(D // QUAD)
        cols = [slice(quad * QUAD, (quad + 1) * QUAD) for quad in quads]
        cols_key = [slice(D + quad * QUAD, D + (quad + 1) * QUAD) for quad in quads]
        cols_value = [slice(2 * D + quad * QUAD, 2 * D + (quad + 1) * QUAD) for quad in quads]
        grad_out = [spread(grad_mixed[at, c], masks) for c in cols]
        grad_probs = [mm_right(qkv[at, c], g) for c, g in zip(cols_value, grad_out)]
        low = [probs_in[at, c] for c in cols]
        probs = [p.astype(F32) for p in low]
        delta = [jnp.sum(p * g, axis=0, keepdims=True) for p, g in zip(probs, grad_probs)]
        grad_scores = [
            (p * (g - d) * HEAD_DIM**-0.5).astype(BF16)
            for p, g, d in zip(probs, grad_probs, delta)
        ]
        grad_value = [mm(p, g) for p, g in zip(low, grad_out)]
        grad_query = [mm_left(g, qkv[at, c]) for g, c in zip(grad_scores, cols_key)]
        grad_key = [mm(g, spread(qkv[at, c], masks)) for g, c in zip(grad_scores, cols)]
        for quad in quads:
            grad_qkv[at, cols_value[quad]] = grad_value[quad].astype(BF16)
            grad_qkv[at, cols_key[quad]] = grad_key[quad].astype(BF16)
            grad_qkv[at, cols[quad]] = gathered(grad_query[quad], lane).astype(BF16)
        return carry

    lax.fori_loop(0, WINDOWS, attend_back, 0, unroll=12)
    gain, shift = norms[0:1], norms[1:2]
    gains[...] = jnp.zeros(gains.shape, F32)

    def after(i, carry):
        at = tile_at(i)
        unit, scale = normalized(x_in[at, :].astype(F32))
        mask = own[at, 0:1]
        normed[at, :] = ((unit * gain + shift) * mask).astype(BF16)
        part = mm_right(grad_qkv[at, :], w_qkv[:, : 3 * D])
        masked = part * mask
        gains[0:1] += jnp.sum(masked * unit, axis=0, keepdims=True)
        gains[1:2] += jnp.sum(masked, axis=0, keepdims=True)
        grad_tokens[at, :] = grad_middle[at, :] + norm_back(part * gain, unit, scale)
        return carry

    lax.fori_loop(0, WROWS // TILE, after, 0)
    gains[2:4] = grad_norms[0:2]
    for part in range(3):
        cols = slice(part * D, (part + 1) * D)
        grad_w[:, cols] = mm_left(normed[...], grad_qkv[:, cols])
    grad_w[:, 3 * D :] = jnp.transpose(gains[...])
    if direct:
        count = keep.shape[1]
        for partner in range(8):
            target = send if partner & 1 else keep
            for k in range(count):
                row = pl.multiple_of(((info[9] ^ partner) * count + (info[10] ^ k)) * 16, 16)
                target[partner >> 1, k] = grad_w[pl.ds(row, 16), :].astype(BF16)
    else:
        w_grad[...] = grad_w[...]


ORDER = (0, 2, 4, 6, 1, 3, 5, 7)
CHIPS = [[0, 2, 4, 6], [1, 3, 5, 7]]
LIMIT = 20 * 1024 * 1024
SMALL = 8 * 1024 * 1024
EARLY = 4 * 10**9
SMEM = pl.BlockSpec(memory_space=pltpu.SMEM)
VMEM = pl.BlockSpec(memory_space=pltpu.VMEM)
ANY = pl.BlockSpec(memory_space=pl.ANY)


def near_core(array):
    return pltpu.with_memory_space_constraint(array, pltpu.VMEM)


def far_core(array):
    return pltpu.with_memory_space_constraint(array, pltpu.HBM)


def run_kernel(body, out_shape, scratch, flops, info, *operands):
    specs = [ANY if isinstance(a, list) else VMEM for a in operands]
    operands = [a[0] if isinstance(a, list) else near_core(a) for a in operands]
    moved = sum(a.size * a.dtype.itemsize for a in operands)
    return pl.pallas_call(
        body,
        out_shape=out_shape,
        in_specs=[SMEM] + specs,
        out_specs=[VMEM] * len(out_shape),
        scratch_shapes=scratch,
        cost_estimate=pl.CostEstimate(
            flops=flops, bytes_accessed=moved, transcendentals=flops // 1024
        ),
        compiler_params=pltpu.CompilerParams(vmem_limit_bytes=LIMIT),
    )(info, *operands)


def swap(array, axis, bit):
    return lax.ppermute(array, axis, [(i, i ^ bit) for i in range(lax.axis_size(axis))])


def together(*values):
    return lax.optimization_barrier(values)


def along_seq(shard):
    return [swap(shard, "seq", k) for k in (1, 2, 3)]


def along_plane(column):
    return [swap(column, "dp", partner) for partner in (2, 4, 6)]


def along_core(pieces):
    return [swap(piece, "dp", 1) for piece in pieces]


def add_parts(own, parts):
    return own.astype(F32) + sum(part.astype(F32) for part in parts)


def shape(dims, kind):
    return pltpu.VMEM(dims, kind)


def per_device(
    tokens,
    cotangent,
    w_qkv,
    w_out,
    w_up,
    w_down,
    norm1_gain,
    norm1_shift,
    norm2_gain,
    norm2_shift,
    clip_steps,
    window_shifts,
):
    n_dp, n_seq = lax.axis_size("dp"), lax.axis_size("seq")
    share = w_qkv.shape[0]
    direct = n_dp == 8 and share % 16 == 0
    info = jnp.concatenate(
        [
            clip_steps.reshape(3),
            window_shifts.reshape(6),
            lax.axis_index("dp").reshape(1).astype(jnp.int32),
            lax.axis_index("seq").reshape(1).astype(jnp.int32),
        ]
    )
    width = 4 * D + NORMS
    vectors = (norm1_gain, norm1_shift, norm2_gain, norm2_shift)

    def in_hbm(arrays):
        return [[a] for a in arrays]

    x, cot, cot_own, own = run_kernel(
        layout_kernel,
        [shape((WROWS, D), BF16)] * 3 + [shape((WROWS, QUAD), F32)],
        [
            pltpu.VMEM((ROWS + 2 * HALO, D), F32),
            pltpu.VMEM((2, ROWS, D), BF16),
            pltpu.SemaphoreType.DMA((2,)),
        ],
        2 * WROWS * D * D,
        info,
        *in_hbm((tokens, cotangent)),
    )
    if direct:
        with_near, first, with_far, second, up_near, up_far = pl.pallas_call(
            prepare_kernel,
            out_shape=[
                jax.ShapeDtypeStruct((share, width + 2 * D), BF16),
                jax.ShapeDtypeStruct((share, width), BF16),
                jax.ShapeDtypeStruct((share, width + 2 * D), BF16),
                jax.ShapeDtypeStruct((2 * w_up.shape[0] + 5 * share, D), BF16),
                jax.ShapeDtypeStruct((2 * w_up.shape[0] + HALO, D), BF16),
                jax.ShapeDtypeStruct((2 * w_up.shape[0] + HALO, D), BF16),
            ],
            in_specs=[ANY] * 10,
            out_specs=[VMEM] * 6,
            scratch_shapes=[
                pltpu.VMEM((4, 1, share), BF16),
                pltpu.SemaphoreType.DMA((26,)),
            ],
            compiler_params=pltpu.CompilerParams(vmem_limit_bytes=LIMIT),
        )(
            *[
                far_core(a)
                for a in (tokens, cotangent, w_qkv, w_out, w_up, w_down.T)
                + tuple(v.reshape(1, -1) for v in vectors)
            ]
        )
        block = w_up.shape[0]
        own_x, own_y, near, middle, far, x, cot, cot_own, own = together(
            swap(second, "dp", 2),
            swap(second, "dp", 4),
            swap(with_near, "seq", 1),
            swap(first, "seq", 2),
            swap(with_far, "seq", 3),
            x,
            cot,
            cot_own,
            own,
        )
        column = jnp.stack([near[:, :width], middle, far[:, :width]])
        column, second = together(column, second)
        first_half = lax.all_gather(column, "dp", axis_index_groups=CHIPS)
        first_half, own_d, *rest = together(
            first_half,
            swap(second, "dp", 6),
            swap(up_near, "seq", 1),
            swap(second[: 2 * block], "seq", 2),
            swap(up_far, "seq", 3),
        )
        second_own = jnp.stack([second, own_x, own_y, own_d])
        near_cot, far_cot = rest[0], rest[2]
        rest = [rest[0][: 2 * block], rest[1], rest[2][: 2 * block]]
        rest = jnp.stack(rest)
        first_half, rest, second_own = together(first_half, rest, second_own)
        second_own = [second_own, *along_core([second_own])]
        first_all = [first_half, *along_core([first_half]), *second_own]
        second_plane = along_plane(rest)
    else:
        norms = jnp.pad(jnp.stack(vectors, axis=1), ((0, 0), (0, NORMS - 4)))
        first = jnp.concatenate([w_qkv, w_out, norms], axis=1)
        both = jnp.stack([tokens, cotangent])
        head, tail = both[:, :HALO], both[:, ROWS - HALO :]
        odd = lax.axis_index("seq") % 2 == 1
        first_all = [lax.all_gather(first, ("dp", "seq"), axis=0, tiled=True)]
        up_all = lax.all_gather(lax.all_gather(w_up, "dp", axis=0, tiled=True), "seq", axis=0)
        down_all = lax.all_gather(lax.all_gather(w_down.T, "dp", axis=0, tiled=True), "seq", axis=0)
        second_own = second_all = [up_all, down_all]
        from_left = lax.ppermute(tail, "seq", [(i, i + 1) for i in range(n_seq - 1)])
        from_right = lax.ppermute(head, "seq", [(i + 1, i) for i in range(n_seq - 1)])
        near, near_cot = jnp.where(odd, from_left, from_right)
        far, far_cot = jnp.where(odd, from_right, from_left)

    x, qkv, mixed, probs, w_all, norms_all = run_kernel(
        functools.partial(attention_kernel, direct),
        [
            shape((WROWS, D), BF16),
            shape((WROWS, 3 * D), BF16),
            shape((WROWS, D), BF16),
            shape((WROWS, D), BF16),
            shape((D, width), BF16),
            shape((8, D), F32),
        ],
        [
            pltpu.VMEM((ROWS + 2 * HALO, D), F32),
            pltpu.VMEM((3 * HALO, D), BF16),
            pltpu.VMEM((2, HALO, D), BF16),
            pltpu.SemaphoreType.DMA((6,)),
        ],
        2 * WROWS * D * 3 * D * 2,
        info,
        *in_hbm((tokens, near, far)),
        x,
        *first_all,
    )
    if direct:
        grads_shape = [shape((4, 2 * block, D), BF16)] * 2
    else:
        grads_shape = [shape((1, D, CHUNK), F32)] * 2
    *state, keep, send = run_kernel(
        functools.partial(feed_first_kernel, direct),
        [shape((WROWS, D), F32)] * 3
        + [shape((WROWS, D), BF16)] * 4
        + grads_shape,
        [
            pltpu.VMEM((1, D, CHUNK), BF16),
            pltpu.VMEM((1, D, CHUNK), BF16),
            pltpu.VMEM((ROWS + 2 * HALO, D), F32),
            pltpu.VMEM((WROWS, CHUNK), BF16),
            pltpu.VMEM((WROWS, CHUNK), BF16),
            pltpu.VMEM((3 * HALO, D), BF16),
            pltpu.VMEM((2, HALO, D), BF16),
            pltpu.SemaphoreType.DMA((4,)),
        ],
        2 * WROWS * D * (6 * CHUNK + D),
        info,
        *in_hbm((cotangent, near_cot, far_cot)),
        cot,
        cot_own,
        own,
        x,
        mixed,
        norms_all,
        w_all,
        *second_own,
    )
    if direct:
        *second_plane, total = together(*second_plane, state[1])
        state[1] = total
        second_plane = [rest, *second_plane]
        second_all = second_plane + along_core(second_plane)
        first_grads = [keep, send]
        extra = (CHUNKS - 1) * 2 * block
        grads_shape = [shape((4, extra, D), BF16)] * 2
        out_shape = [shape((4, n_seq * share, D), BF16)] * 2
    else:
        first_grads = [keep, send]
        grads_shape = [shape((CHUNKS - 1, D, CHUNK), F32)] * 2
        out_shape = [shape((D, D), F32)]
    middle, total, grad, normed, normed_own, cot, cot_own = state
    total, grad, *grads = run_kernel(
        functools.partial(feed_rest_kernel, direct),
        [shape((WROWS, D), F32)] * 2 + grads_shape,
        [
            pltpu.VMEM((CHUNKS - 1, D, CHUNK), BF16),
            pltpu.VMEM((CHUNKS - 1, D, CHUNK), BF16),
            pltpu.VMEM((D, D), F32),
            pltpu.VMEM((WROWS, CHUNK), BF16),
            pltpu.VMEM((WROWS, CHUNK), BF16),
        ],
        2 * WROWS * D * 18 * CHUNK,
        info,
        total,
        grad,
        normed,
        normed_own,
        cot,
        cot_own,
        *second_all,
    )
    if direct:
        from_core = along_core([first_grads[1], grads[1]])
    grad_middle, grad_mixed, grad_norms, *out_grads = run_kernel(
        functools.partial(feed_last_kernel, direct),
        [
            shape((WROWS, D), F32),
            shape((WROWS, D), BF16),
            shape((8, D), F32),
            *out_shape,
        ],
        [pltpu.VMEM((D, D), F32), pltpu.VMEM((WROWS, D), BF16)],
        2 * WROWS * D * 2 * D,
        info,
        middle,
        grad,
        cot,
        own,
        mixed,
        norms_all,
        w_all,
    )
    if direct:
        from_core = [*from_core, *along_core(out_grads[1:])]
        keeps, from_core = [first_grads[0], grads[0], out_grads[0]], together(*from_core)
        own_pair, to_near, pair, *low = add_chunks(keeps, from_core)
        to_near, *low, grad_mixed = together(to_near, *low, grad_mixed)
        parts = [swap(part, "dp", 2 * m + 2) for m, part in enumerate(low)]
        parts.append(swap(to_near, "seq", 1))
        grads_shape = [shape((4, n_seq, share, 3 * D + NORMS), BF16)] * 2
    else:
        grads_up, grads_down = [
            jnp.concatenate([a, b], axis=0) for a, b in zip(first_grads, grads)
        ]
        grad_up = lax.psum_scatter(grads_up, "seq", scatter_dimension=0)
        grad_up = lax.psum_scatter(grad_up, "dp", scatter_dimension=0, tiled=True)
        grad_down = lax.psum_scatter(grads_down, "seq", scatter_dimension=0)
        grad_down = lax.psum_scatter(grad_down, "dp", scatter_dimension=0, tiled=True).T
        grad_out = lax.psum_scatter(out_grads[0], ("dp", "seq"), scatter_dimension=0, tiled=True)
        grads_shape = [shape((D, 3 * D + NORMS), F32)]
    grad_tokens, *grads = run_kernel(
        functools.partial(back_kernel, direct),
        [shape((WROWS, D), F32), *grads_shape],
        [
            pltpu.VMEM((WROWS, D), BF16),
            pltpu.VMEM((WROWS, 3 * D), BF16),
            pltpu.VMEM((NORMS, D), F32),
            pltpu.VMEM((D, 3 * D + NORMS), F32),
        ],
        2 * WROWS * D * (6 * D + 3 * D),
        info,
        x,
        own,
        qkv,
        probs,
        grad_mixed,
        grad_middle,
        w_all,
        norms_all,
        grad_norms,
    )
    if direct:
        grad_tokens, *grads = together(grad_tokens, *grads)
    out, tokens_grad = [
        run_kernel(
            finish_rows_kernel,
            [jax.ShapeDtypeStruct((ROWS, D), BF16)],
            [pltpu.VMEM((ROWS + 2 * HALO, D), F32)],
            2 * WROWS * D * D,
            info,
            values,
        )[0]
        for values in (total, grad_tokens)
    ]
    if direct:
        keep, send, *parts, from_near = together(*grads, *parts)
        rows = 2 * block + share
        plan = [[(slice(None), (slice(k * rows, (k + 1) * rows),))] for k in range(2)]
        low = add(plan, [((rows, D), BF16)] * 2, pair, *parts)
        second_far, from_near_far = together(low[1], swap(low[0], "seq", 1))
        (second_far,) = add([[(slice(None), slice(None))]], [(low[1].shape, BF16)], second_far, from_near_far)
        second = [swap(second_far, "seq", 3)]
        (from_core,) = along_core([send])
        first_pair, *first_low = add_slots(keep, from_core)
        first = [swap(part, "dp", 2 * m + 2) for m, part in enumerate(first_low)]
        own_pair, *own_low = add_slots(own_pair, from_near)
        *first, second, own0, own1, own2, out, tokens_grad = together(
            *first, *second, *own_low, out, tokens_grad
        )
        everything = slice(None)
        slot = first_pair.shape[1:]
        first_own, to_near, to_far = add(
            [[(everything, 0)], [(0, 1), (1, 2)], [(everything, 3)]],
            [(slot, F32), ((2, *slot), BF16), (slot, F32)],
            first_pair,
            *first,
        )
        near_part = swap(to_near, "seq", 1)
        (far_low,) = small_call(far_kernel, [(slot, BF16)], to_far, near_part, flops=EARLY)
        far_part = swap(far_low, "seq", 3)
        own_parts = [swap(part, "dp", 2 * m + 2) for m, part in enumerate((own0, own1, own2))]
        shapes = [((block, D), F32)] * 2 + [((share, D), F32), ((share, 3 * D), F32)]
        shapes += [((1, share), F32)] * 4
        grad_up, grad_down, grad_out, w_qkv_grad, *norm_grads = small_call(
            finish_kernel,
            shapes,
            own_pair,
            first_own,
            *own_parts,
            second,
            near_part,
            far_part,
        )
        grad_down = grad_down.T
        norm_grads = [grad.reshape(share) for grad in norm_grads]
    else:
        first_sum = lax.psum_scatter(grads[0], ("dp", "seq"), scatter_dimension=0, tiled=True)
        w_qkv_grad = first_sum[:, : 3 * D]
        norm_grads = [first_sum[:, 3 * D + i] for i in range(4)]
    return (
        out,
        tokens_grad,
        w_qkv_grad,
        grad_out,
        grad_up,
        grad_down,
        *norm_grads,
    )


def solution(mesh):
    rows = P(("dp", "seq"), None)
    vector = P(("dp", "seq"))
    return jax.shard_map(
        per_device,
        mesh=mesh,
        in_specs=(
            rows,
            rows,
            rows,
            rows,
            P("dp", "seq"),
            P("seq", "dp"),
            vector,
            vector,
            vector,
            vector,
            P("dp", None),
            P("dp", None, None),
        ),
        out_specs=(
            rows,
            rows,
            rows,
            rows,
            P("dp", "seq"),
            P("seq", "dp"),
            vector,
            vector,
            vector,
            vector,
        ),
        check_vma=False,
    )
```

```python
import functools

import jax
import jax.numpy as jnp
from jax import lax
from jax.experimental import pallas as pl
from jax.experimental.pallas import tpu as pltpu
from jax.sharding import PartitionSpec as P

D = 512
HEADS = 16
HEAD_DIM = D // HEADS
FF = 2048
FREQ = 8
STEPS_DEV = 88
HALO = 4 * FREQ
ROWS = STEPS_DEV * FREQ
WIN = 4 * FREQ
WINDOWS = STEPS_DEV // 4 + 2
WROWS = WINDOWS * WIN
TILE = 768
QUAD = 128
NORMS = 128
CHUNK = 512
CHUNKS = FF // CHUNK
epsilon = 1e-06
F32 = jnp.float32
BF16 = jnp.bfloat16


def mm(left, right):
    return jnp.dot(left, right, preferred_element_type=F32)


def mm_right(left, right):
    return lax.dot_general(left, right, (((1,), (1,)), ((), ())), preferred_element_type=F32)


def mm_left(left, right):
    return lax.dot_general(left, right, (((0,), (0,)), ((), ())), preferred_element_type=F32)


def window_place(info, w):
    lead, mid, trail = info[0], info[1], info[2]
    seq = info[10]
    base = seq * STEPS_DEV
    n_lead = lead // 4 + 1
    n_mid = mid // 4 + 1
    index = jnp.where(seq == 0, 0, base // 4 + 1) + w
    in_mid = index >= n_lead
    in_trail = index >= n_lead + n_mid
    before = jnp.where(in_trail, n_lead + n_mid, jnp.where(in_mid, n_lead, 0))
    start = jnp.where(in_trail, lead + mid, jnp.where(in_mid, lead, 0))
    steps = jnp.where(in_trail, trail, jnp.where(in_mid, mid, lead))
    shift_time = jnp.where(in_trail, info[7], jnp.where(in_mid, info[5], info[3]))
    shift_freq = jnp.where(in_trail, info[8], jnp.where(in_mid, info[6], info[4]))
    first = start - 4 + shift_time + 4 * (index - before)
    here = first < base + STEPS_DEV
    low = jnp.clip(start - first, 0, 4)
    high = jnp.where(here, jnp.clip(start + steps - first, 0, 4), 0)
    own_low = jnp.clip(base - first, 0, 4)
    own_high = jnp.clip(base + STEPS_DEV - first, 0, 4)
    row = jnp.clip(first - base + 4, 0, STEPS_DEV + 4) * FREQ
    row = pl.multiple_of(row, FREQ)
    return (
        row,
        low * FREQ,
        high * FREQ,
        jnp.maximum(low, own_low) * FREQ,
        jnp.minimum(high, own_high) * FREQ,
        shift_freq,
    )


def window_at(w):
    return pl.ds(pl.multiple_of(w * WIN, WIN), WIN)


def tile_at(i):
    return pl.ds(pl.multiple_of(i * TILE, TILE), TILE)


def row_mask(low, high):
    index = lax.broadcasted_iota(jnp.int32, (WIN, 1), 0)
    return (index >= low) & (index < high)


def copy_all(pairs, sems, first=0):
    copies = [
        pltpu.make_async_copy(source, target, sems.at[first + i])
        for i, (source, target) in enumerate(pairs)
    ]
    for copy in copies:
        copy.start()
    return copies


def wait_all(copies):
    for copy in copies:
        copy.wait()


def edge_copies(rows, near, far, ext_low, halos):
    pairs = [
        (rows.at[0:HALO, :], ext_low.at[0:HALO, :]),
        (rows.at[ROWS - 2 * HALO :, :], ext_low.at[HALO:, :]),
    ]
    for i, parts in enumerate((near, far)):
        size = HALO // len(parts)
        pairs += [
            (part, halos.at[i, j * size : (j + 1) * size, :]) for j, part in enumerate(parts)
        ]
    return pairs


def pad_edges(info, ext, ext_low, halos):
    ext[HALO : 2 * HALO] = ext_low[0:HALO].astype(F32)
    ext[ROWS - HALO : ROWS + HALO] = ext_low[HALO:].astype(F32)
    odd = info[10] % 2 == 1
    for i, is_left in enumerate((odd, jnp.logical_not(odd))):
        at = pl.multiple_of(jnp.where(is_left, 0, HALO + ROWS), HALO)
        ext[pl.ds(at, HALO), :] = halos[i].astype(F32)


EDGES = (0, WINDOWS - 2, WINDOWS - 1)


def place_rows(info, w, ext, out):
    row, low, high, _, _, _ = window_place(info, w)
    values = jnp.where(row_mask(low, high), ext[pl.ds(row, WIN), :], 0.0)
    out[window_at(w), :] = values.astype(BF16)


def place_cotangent(info, w, ext, cot, cot_own):
    row, low, high, own_low, own_high, _ = window_place(info, w)
    values = ext[pl.ds(row, WIN), :]
    cot[window_at(w), :] = jnp.where(row_mask(low, high), values, 0.0).astype(BF16)
    cot_own[window_at(w), :] = jnp.where(row_mask(own_low, own_high), values, 0.0).astype(BF16)


def layout_kernel(info, tokens, cotangent, x_out, cot, cot_own, own, ext, stage, sems):
    copies = copy_all([(tokens, stage.at[0]), (cotangent, stage.at[1])], sems)
    for edge in (slice(0, HALO), slice(HALO + ROWS, 2 * HALO + ROWS)):
        ext[edge, :] = jnp.zeros((HALO, D), F32)
    copies[0].wait()
    ext[HALO : HALO + ROWS] = stage[0].astype(F32)

    def tokens_step(w, carry):
        place_rows(info, w, ext, x_out)
        return carry

    lax.fori_loop(0, WINDOWS, tokens_step, 0, unroll=4)
    copies[1].wait()
    ext[HALO : HALO + ROWS] = stage[1].astype(F32)

    def cotangent_step(w, carry):
        place_cotangent(info, w, ext, cot, cot_own)
        mask = row_mask(*window_place(info, w)[3:5])
        own[window_at(w), :] = jnp.where(mask, jnp.ones((WIN, QUAD), F32), 0.0)
        return carry

    lax.fori_loop(0, WINDOWS, cotangent_step, 0, unroll=4)


def normalized(values):
    mean = jnp.mean(values, axis=-1, keepdims=True)
    centered = values - mean
    variance = jnp.mean(centered * centered, axis=-1, keepdims=True)
    scale = lax.rsqrt(variance + epsilon)
    return centered * scale, scale


def norm_back(grad, unit, scale):
    mean_one = jnp.mean(grad, axis=-1, keepdims=True)
    mean_two = jnp.mean(grad * unit, axis=-1, keepdims=True)
    return scale * (grad - mean_one - unit * mean_two)


def head_masks():
    lane = lax.broadcasted_iota(jnp.int32, (1, QUAD), 1) // HEAD_DIM
    return [(lane == h).astype(BF16) for h in range(QUAD // HEAD_DIM)]


def spread(block, masks):
    return jnp.concatenate([block * mask for mask in masks], axis=0)


def gathered(product, lane):
    parts = [product[h * WIN : (h + 1) * WIN] for h in range(QUAD // HEAD_DIM)]
    return jnp.where(
        lane < 1, parts[0], jnp.where(lane < 2, parts[1], jnp.where(lane < 3, parts[2], parts[3]))
    )


def sum_kernel(plan, *refs):
    ins, outs = refs[: -len(plan)], refs[-len(plan) :]
    for out, pieces in zip(outs, plan):
        for target, source in pieces:
            value = ins[0][source].astype(F32)
            for part in ins[1:]:
                value = value + part[source].astype(F32)
            out[target] = value.astype(out.dtype)


def add(plan, shapes, *operands):
    return pl.pallas_call(
        functools.partial(sum_kernel, plan),
        out_shape=[jax.ShapeDtypeStruct(*s) for s in shapes],
        in_specs=[VMEM] * len(operands),
        out_specs=[VMEM] * len(shapes),
        compiler_params=pltpu.CompilerParams(vmem_limit_bytes=SMALL),
    )(*[near_core(a) for a in operands])


def small_call(body, shapes, *operands, flops=0):
    moved = sum(a.size * a.dtype.itemsize for a in operands)
    return pl.pallas_call(
        body,
        out_shape=[jax.ShapeDtypeStruct(*s) for s in shapes],
        in_specs=[VMEM] * len(operands),
        out_specs=[VMEM] * len(shapes),
        cost_estimate=pl.CostEstimate(flops=flops, bytes_accessed=moved, transcendentals=0),
        compiler_params=pltpu.CompilerParams(vmem_limit_bytes=SMALL),
    )(*[near_core(a) for a in operands])


def stack_kernel(*refs):
    *parts, out = refs
    for i, part in enumerate(parts):
        out[i] = part[:, 0 : out.shape[2]]


def chunks_kernel(keep_first, keep_rest, keep_out, first, rest, out, *refs):
    own, near, pair, *low = refs
    block, share = keep_first.shape[1], keep_out.shape[1] // CHUNKS

    def sums(slot, k):
        a, b, row = (keep_first, first, 0) if k == 0 else (keep_rest, rest, (k - 1) * block)
        rows, out_rows = slice(row, row + block), slice(share * k, share * (k + 1))
        return (
            a[slot, rows].astype(F32) + b[slot, rows].astype(F32),
            keep_out[slot, out_rows].astype(F32) + out[slot, out_rows].astype(F32),
        )

    for slot in range(4):
        for k in range(CHUNKS):
            if k < 2:
                target, row = (own, near)[k].at[slot], 0
            else:
                target, row = ([pair] + low)[slot], (k - 2) * (block + share)
            one, two = sums(slot, k)
            target[row : row + block, :] = one.astype(target.dtype)
            target[row + block : row + block + share, :] = two.astype(target.dtype)


def add_chunks(keeps, parts):
    rows = keeps[0].shape[1] + keeps[2].shape[1] // CHUNKS
    shapes = [((4, rows, D), F32), ((4, rows, D), BF16), ((2 * rows, D), F32)]
    shapes += [((2 * rows, D), BF16)] * 3
    return pl.pallas_call(
        chunks_kernel,
        out_shape=[jax.ShapeDtypeStruct(*s) for s in shapes],
        in_specs=[VMEM] * 6,
        out_specs=[VMEM] * 6,
        compiler_params=pltpu.CompilerParams(vmem_limit_bytes=SMALL),
    )(*[near_core(a) for a in (*keeps, *parts)])


def far_kernel(own, pair, out):
    out[...] = (own[...] + pair[1].astype(F32)).astype(BF16)


def finish_kernel(chunk, first, one, two, three, second, pair, far, *outs):
    total = chunk[...] + second[...].astype(F32)
    for part in (one, two, three):
        total = total + part[...].astype(F32)
    row = 0
    for out in outs[:3]:
        out[...] = total[row : row + out.shape[0]]
        row += out.shape[0]
    total = first[...] + (pair[0].astype(F32) + far[...].astype(F32))
    outs[3][...] = total[:, : 3 * D]
    rows = jnp.transpose(total[:, 3 * D :])
    for i, out in enumerate(outs[4:]):
        out[...] = rows[i : i + 1]


def add_slots(*operands):
    slot = operands[0].shape[1:]
    plan = [[(slice(None), i)] for i in range(4)]
    return add(plan, [(slot, F32)] + [(slot, BF16)] * 3, *operands)


def prepare_kernel(tokens, cotangent, w_qkv, w_out, w_up, w_down, *refs):
    norms, (with_near, first, with_far, second, up_near, up_far, vectors, sems) = refs[:4], refs[4:]
    share, width = first.shape
    block = w_up.shape[0]
    odd = lax.axis_index("seq") % 2
    pairs = [(norm, vectors.at[i]) for i, norm in enumerate(norms)]
    for target in (with_near, first, with_far):
        pairs += [(w_qkv, target.at[:, : 3 * D]), (w_out, target.at[:, 3 * D : 4 * D])]
    for target, up_target, is_head in ((with_near, up_near, odd), (with_far, up_far, 1 - odd)):
        start = pl.multiple_of((1 - is_head) * (ROWS - HALO), HALO)
        for j in range(2):
            at = width + j * D
            rows = pl.ds(start + j * (HALO // 2), HALO // 2)
            pairs.append((tokens.at[rows, :], target.at[:, at : at + D]))
        pairs.append((cotangent.at[pl.ds(start, HALO), :], up_target.at[2 * block :, :]))
    for target in (second, up_near, up_far):
        pairs += [(w_up, target.at[0:block]), (w_down, target.at[block : 2 * block])]
    first_row = 2 * block
    for i, source in enumerate([w_qkv.at[:, j * D : (j + 1) * D] for j in range(3)] + [w_out]):
        pairs.append((source, second.at[first_row + share * i : first_row + share * (i + 1), :]))
    copies = copy_all(pairs, sems)
    wait_all(copies[: len(norms)])
    columns = jnp.concatenate(
        [vectors[i].astype(F32) for i in range(4)] + [jnp.zeros((NORMS - 4, share), F32)], axis=0
    )
    columns = jnp.transpose(columns).astype(BF16)
    for target in (with_near, first, with_far):
        target[:, 4 * D : width] = columns
    second[first_row + 4 * share :, :] = jnp.concatenate([columns] * (D // NORMS), axis=1)
    wait_all(copies[len(norms) :])


def attention_kernel(direct, info, rows, near, far, x_in, *refs):
    pieces, refs = (refs[:4], refs[4:]) if direct else (refs[:1], refs[1:])
    x_out, qkv_out, mixed_out, probs_out, w_out, norms_out, ext, edges, halos, sems = refs
    width = w_out.shape[1]
    near, far = [
        [a.at[:, width + j * D : width + (j + 1) * D] for j in range(2)] if direct else [a]
        for a in (near, far)
    ]
    edge_copy = copy_all(edge_copies(rows, near, far, edges, halos), sems)
    x_out[...] = x_in[...]
    if direct:
        count, share = pieces[0].shape[1] + 1, pieces[0].shape[2]
        for core, piece in enumerate(pieces[:2]):
            for chip in range(4):
                for k in range(1, count):
                    owner = (2 * chip + (info[9] % 2 ^ core)) * count + (info[10] ^ k)
                    at = pl.multiple_of(owner * share, share)
                    w_out[pl.ds(at, share), :] = piece[chip, k - 1]
        for i, partner in enumerate(ORDER):
            owner = (info[9] ^ partner) * count + info[10]
            at = pl.ds(pl.multiple_of(owner * share, share), share)
            for j in range(5):
                cols = min(D, width - j * D)
                row = D // 4 + j * share
                part = pieces[2 + i // 4][i % 4, row : row + share, 0:cols]
                w_out[at, j * D : j * D + cols] = part
    else:
        w_out[...] = pieces[0][...]
    wait_all(edge_copy)
    pad_edges(info, ext, edges, halos)
    for w in EDGES:
        place_rows(info, w, ext, x_out)
    norms_out[...] = jnp.transpose(w_out[:, 4 * D :].astype(F32))[:8]
    gain, shift = norms_out[0:1], norms_out[1:2]

    def project(i, carry):
        at = tile_at(i)
        unit, _ = normalized(x_out[at, :].astype(F32))
        low = (unit * gain + shift).astype(BF16)
        for part in range(3):
            cols = slice(part * D, (part + 1) * D)
            qkv_out[at, cols] = mm(low, w_out[:, cols]).astype(BF16)
        return carry

    lax.fori_loop(0, WROWS // TILE, project, 0)
    masks = head_masks()
    lane = lax.broadcasted_iota(jnp.int32, (1, QUAD), 1) // HEAD_DIM
    key_row = lax.broadcasted_iota(jnp.int32, (WIN, QUAD), 0)
    query_row = lax.broadcasted_iota(jnp.int32, (WIN, QUAD), 1) % WIN
    key_freq, query_freq = key_row % FREQ, query_row % FREQ

    def attend(w, carry):
        _, low, high, _, _, shift_freq = window_place(info, w)
        at = pl.ds(pl.multiple_of(w * WIN, WIN), WIN)
        key_group = (key_freq + 4 - shift_freq) >> 2
        query_group = (query_freq + 4 - shift_freq) >> 2
        allowed = (key_group == query_group) & (key_row >= low) & (key_row < high)
        quads = range(D // QUAD)
        raw = []
        for quad in quads:
            query = qkv_out[at, quad * QUAD : (quad + 1) * QUAD]
            key = qkv_out[at, D + quad * QUAD : D + (quad + 1) * QUAD]
            raw.append(mm_right(key, spread(query, masks)))
        scores = [jnp.where(allowed, r * HEAD_DIM**-0.5, -1e30) for r in raw]
        weights = [jnp.exp(s - jnp.max(s, axis=0, keepdims=True)) for s in scores]
        probs = [(p / jnp.sum(p, axis=0, keepdims=True)).astype(BF16) for p in weights]
        products = []
        for quad in quads:
            probs_out[at, quad * QUAD : (quad + 1) * QUAD] = probs[quad]
            value = qkv_out[at, 2 * D + quad * QUAD : 2 * D + (quad + 1) * QUAD]
            products.append(mm_left(probs[quad], value))
        for quad in quads:
            mixed = gathered(products[quad], lane).astype(BF16)
            mixed_out[at, quad * QUAD : (quad + 1) * QUAD] = mixed
        return carry

    lax.fori_loop(0, WINDOWS, attend, 0, unroll=12)


def gelu_parts(values):
    half_exp = jnp.exp(-0.5 * values * values)
    t = 1.0 / (1.0 + (0.3275911 * 0.7071067811865476) * jnp.abs(values))
    poly = t * (
        0.5 * 0.254829592
        + t
        * (
            0.5 * -0.284496736
            + t * (0.5 * 1.421413741 + t * (0.5 * -1.453152027 + t * (0.5 * 1.061405429)))
        )
    )
    tail = poly * half_exp
    return jnp.where(values >= 0, 1.0 - tail, tail), half_exp * 0.3989422804014327


def place_feed(info, pieces, up, down):
    block = D // 8
    for piece, partner in zip(pieces, ORDER):
        at = pl.ds(pl.multiple_of((info[9] ^ partner) * block, block), block)
        for c in range(up.shape[0]):
            up[c, at, :] = piece[c, 0:block, :]
            down[c, at, :] = piece[c, block : 2 * block, :]


def feed_rows(at, up, down, normed, cot, hidden, pre):
    values = mm(normed[at, :], up)
    grad_hidden = mm(cot[at, :], down)
    below, density = gelu_parts(values)
    hidden_low = (values * below).astype(BF16)
    grad_low = (grad_hidden * (below + values * density)).astype(BF16)
    hidden[at, :] = hidden_low
    pre[at, :] = grad_low
    return mm_right(hidden_low, down), mm_right(grad_low, up)


def feed_grads(direct, info, row, normed_own, cot_own, hidden, pre, space, refs):
    block = D // 8
    for i, product in enumerate(((normed_own, pre), (cot_own, hidden))):
        grad = mm_left(product[0][...], product[1][...])
        if not direct:
            refs[i][row // (2 * block)] = grad
            continue
        space[0:D, :] = grad
        for partner in range(8):
            at = pl.multiple_of((info[9] ^ partner) * block, block)
            first = row + i * block
            refs[partner & 1][partner >> 1, first : first + block, :] = space[
                pl.ds(at, block), :
            ].astype(BF16)


def feed_first_kernel(
    direct, info, rows, near, far, cot_in, cot_own_in, own, x_in, mixed_in, norms, w_all, *refs
):
    pieces, refs = refs[:2], refs[2:]
    middle, total, grad, normed, normed_own, cot, cot_own = refs[:7]
    grads, (up, down, ext, hidden, pre, edges, halos, sems) = refs[7:9], refs[9:]
    near, far = [[a.at[a.shape[0] - HALO :, :]] for a in (near, far)]
    edge_copy = copy_all(edge_copies(rows, near, far, edges, halos), sems)
    cot[...], cot_own[...] = cot_in[...], cot_own_in[...]
    if direct:
        own_pieces = [piece.at[m : m + 1] for piece in pieces for m in range(4)]
        place_feed(info, own_pieces, up, down)
    else:
        up[...], down[...] = pieces[0][0:1], pieces[1][0:1]
    wait_all(edge_copy)
    pad_edges(info, ext, edges, halos)
    for w in EDGES:
        place_cotangent(info, w, ext, cot, cot_own)
    gain, shift = norms[2:3], norms[3:4]

    def before(i, carry):
        at = tile_at(i)
        values = x_in[at, :].astype(F32) + mm(mixed_in[at, :], w_all[:, 3 * D : 4 * D])
        middle[at, :] = values
        unit, _ = normalized(values)
        low = unit * gain + shift
        normed[at, :] = low.astype(BF16)
        normed_own[at, :] = (low * own[at, 0:1]).astype(BF16)
        return carry

    lax.fori_loop(0, WROWS // TILE, before, 0)
    for i in range(WROWS // TILE):
        at = slice(i * TILE, (i + 1) * TILE)
        branch, back = feed_rows(at, up[0], down[0], normed, cot, hidden, pre)
        total[at, :] = middle[at, :] + branch
        grad[at, :] = back
    feed_grads(direct, info, 0, normed_own, cot_own, hidden, pre, ext, grads)


def feed_rest_kernel(direct, info, total_in, grad_in, normed, normed_own, cot, cot_own, *refs):
    pieces, refs = (refs[:8], refs[8:]) if direct else (refs[:2], refs[2:])
    total, grad, *grads, up, down, ext, hidden, pre = refs
    if direct:
        place_feed(info, pieces, up, down)
    else:
        up[...], down[...] = pieces[0][1:CHUNKS], pieces[1][1:CHUNKS]
    for c in range(CHUNKS - 1):
        for i in range(WROWS // TILE):
            at = slice(i * TILE, (i + 1) * TILE)
            branch, back = feed_rows(at, up[c], down[c], normed, cot, hidden, pre)
            total[at, :] = (total if c else total_in)[at, :] + branch
            grad[at, :] = (grad if c else grad_in)[at, :] + back
        feed_grads(direct, info, c * (D // 4), normed_own, cot_own, hidden, pre, ext, grads)


def feed_last_kernel(direct, info, middle, grad, cot, own, mixed_in, norms, w_all, *refs):
    grad_middle, grad_mixed, grad_norms, *grads, ext, grad_own = refs
    gain = norms[2:3]
    grad_norms[...] = jnp.zeros(grad_norms.shape, F32)
    for i in range(WROWS // TILE):
        at = slice(i * TILE, (i + 1) * TILE)
        unit, scale = normalized(middle[at, :])
        part = grad[at, :]
        masked = part * own[at, 0:1]
        grad_norms[0:1] += jnp.sum(masked * unit, axis=0, keepdims=True)
        grad_norms[1:2] += jnp.sum(masked, axis=0, keepdims=True)
        result = cot[at, :].astype(F32) + norm_back(part * gain, unit, scale)
        grad_middle[at, :] = result
        grad_mixed[at, :] = mm_right(result.astype(BF16), w_all[:, 3 * D : 4 * D]).astype(BF16)
        grad_own[at, :] = (result * own[at, 0:1]).astype(BF16)
    grad_out = mm_left(mixed_in[...], grad_own[...])
    if direct:
        ext[0:D, :] = grad_out
        share = grads[0].shape[1] // CHUNKS
        for partner in range(8):
            for k in range(CHUNKS):
                owner = (info[9] ^ partner) * CHUNKS + (info[10] ^ k)
                row = pl.multiple_of(owner * share, share)
                grads[partner & 1][partner >> 1, share * k : share * (k + 1), :] = ext[
                    pl.ds(row, share), :
                ].astype(BF16)
    else:
        grads[0][...] = grad_out


def finish_rows_kernel(info, values, out, ext):
    unplace(info, values, ext, out)


def unplace(info, values, ext, out):
    def back(w, carry):
        row, low, high, _, _, _ = window_place(info, w)
        at = pl.ds(pl.multiple_of(w * WIN, WIN), WIN)
        place = pl.ds(row, WIN)
        ext[place, :] = jnp.where(row_mask(low, high), values[at, :], ext[place, :])
        return carry

    lax.fori_loop(0, WINDOWS, back, 0, unroll=4)
    out[...] = ext[HALO : HALO + ROWS].astype(BF16)


def back_kernel(
    direct, info, x_in, own, qkv, probs_in, grad_mixed, grad_middle, w_qkv, norms, grad_norms, *refs
):
    grad_tokens, refs = refs[0], refs[1:]
    if direct:
        (keep, send), refs = refs[:2], refs[2:]
    else:
        w_grad, refs = refs[0], refs[1:]
    normed, grad_qkv, gains, grad_w = refs
    masks = head_masks()
    lane = lax.broadcasted_iota(jnp.int32, (1, QUAD), 1) // HEAD_DIM

    def attend_back(w, carry):
        at = window_at(w)
        quads = range(D // QUAD)
        cols = [slice(quad * QUAD, (quad + 1) * QUAD) for quad in quads]
        cols_key = [slice(D + quad * QUAD, D + (quad + 1) * QUAD) for quad in quads]
        cols_value = [slice(2 * D + quad * QUAD, 2 * D + (quad + 1) * QUAD) for quad in quads]
        grad_out = [spread(grad_mixed[at, c], masks) for c in cols]
        grad_probs = [mm_right(qkv[at, c], g) for c, g in zip(cols_value, grad_out)]
        low = [probs_in[at, c] for c in cols]
        probs = [p.astype(F32) for p in low]
        delta = [jnp.sum(p * g, axis=0, keepdims=True) for p, g in zip(probs, grad_probs)]
        grad_scores = [
            (p * (g - d) * HEAD_DIM**-0.5).astype(BF16)
            for p, g, d in zip(probs, grad_probs, delta)
        ]
        grad_value = [mm(p, g) for p, g in zip(low, grad_out)]
        grad_query = [mm_left(g, qkv[at, c]) for g, c in zip(grad_scores, cols_key)]
        grad_key = [mm(g, spread(qkv[at, c], masks)) for g, c in zip(grad_scores, cols)]
        for quad in quads:
            grad_qkv[at, cols_value[quad]] = grad_value[quad].astype(BF16)
            grad_qkv[at, cols_key[quad]] = grad_key[quad].astype(BF16)
            grad_qkv[at, cols[quad]] = gathered(grad_query[quad], lane).astype(BF16)
        return carry

    lax.fori_loop(0, WINDOWS, attend_back, 0, unroll=12)
    gain, shift = norms[0:1], norms[1:2]
    gains[...] = jnp.zeros(gains.shape, F32)

    def after(i, carry):
        at = tile_at(i)
        unit, scale = normalized(x_in[at, :].astype(F32))
        mask = own[at, 0:1]
        normed[at, :] = ((unit * gain + shift) * mask).astype(BF16)
        part = mm_right(grad_qkv[at, :], w_qkv[:, : 3 * D])
        masked = part * mask
        gains[0:1] += jnp.sum(masked * unit, axis=0, keepdims=True)
        gains[1:2] += jnp.sum(masked, axis=0, keepdims=True)
        grad_tokens[at, :] = grad_middle[at, :] + norm_back(part * gain, unit, scale)
        return carry

    lax.fori_loop(0, WROWS // TILE, after, 0)
    gains[2:4] = grad_norms[0:2]
    for part in range(3):
        cols = slice(part * D, (part + 1) * D)
        grad_w[:, cols] = mm_left(normed[...], grad_qkv[:, cols])
    grad_w[:, 3 * D :] = jnp.transpose(gains[...])
    if direct:
        count = keep.shape[1]
        for partner in range(8):
            target = send if partner & 1 else keep
            for k in range(count):
                row = pl.multiple_of(((info[9] ^ partner) * count + (info[10] ^ k)) * 16, 16)
                target[partner >> 1, k] = grad_w[pl.ds(row, 16), :].astype(BF16)
    else:
        w_grad[...] = grad_w[...]


ORDER = (0, 2, 4, 6, 1, 3, 5, 7)
CHIPS = [[0, 2, 4, 6], [1, 3, 5, 7]]
LIMIT = 20 * 1024 * 1024
SMALL = 8 * 1024 * 1024
EARLY = 4 * 10**9
SMEM = pl.BlockSpec(memory_space=pltpu.SMEM)
VMEM = pl.BlockSpec(memory_space=pltpu.VMEM)
ANY = pl.BlockSpec(memory_space=pl.ANY)


def near_core(array):
    return pltpu.with_memory_space_constraint(array, pltpu.VMEM)


def far_core(array):
    return pltpu.with_memory_space_constraint(array, pltpu.HBM)


def run_kernel(body, out_shape, scratch, flops, info, *operands):
    specs = [ANY if isinstance(a, list) else VMEM for a in operands]
    operands = [a[0] if isinstance(a, list) else near_core(a) for a in operands]
    moved = sum(a.size * a.dtype.itemsize for a in operands)
    return pl.pallas_call(
        body,
        out_shape=out_shape,
        in_specs=[SMEM] + specs,
        out_specs=[VMEM] * len(out_shape),
        scratch_shapes=scratch,
        cost_estimate=pl.CostEstimate(
            flops=flops, bytes_accessed=moved, transcendentals=flops // 1024
        ),
        compiler_params=pltpu.CompilerParams(vmem_limit_bytes=LIMIT),
    )(info, *operands)


def swap(array, axis, bit):
    return lax.ppermute(array, axis, [(i, i ^ bit) for i in range(lax.axis_size(axis))])


def together(*values):
    return lax.optimization_barrier(values)


def along_seq(shard):
    return [swap(shard, "seq", k) for k in (1, 2, 3)]


def along_plane(column):
    return [swap(column, "dp", partner) for partner in (2, 4, 6)]


def along_core(pieces):
    return [swap(piece, "dp", 1) for piece in pieces]


def add_parts(own, parts):
    return own.astype(F32) + sum(part.astype(F32) for part in parts)


def shape(dims, kind):
    return pltpu.VMEM(dims, kind)


def per_device(
    tokens,
    cotangent,
    w_qkv,
    w_out,
    w_up,
    w_down,
    norm1_gain,
    norm1_shift,
    norm2_gain,
    norm2_shift,
    clip_steps,
    window_shifts,
):
    n_dp, n_seq = lax.axis_size("dp"), lax.axis_size("seq")
    share = w_qkv.shape[0]
    direct = n_dp == 8 and share % 16 == 0
    info = jnp.concatenate(
        [
            clip_steps.reshape(3),
            window_shifts.reshape(6),
            lax.axis_index("dp").reshape(1).astype(jnp.int32),
            lax.axis_index("seq").reshape(1).astype(jnp.int32),
        ]
    )
    width = 4 * D + NORMS
    vectors = (norm1_gain, norm1_shift, norm2_gain, norm2_shift)

    def in_hbm(arrays):
        return [[a] for a in arrays]

    x, cot, cot_own, own = run_kernel(
        layout_kernel,
        [shape((WROWS, D), BF16)] * 3 + [shape((WROWS, QUAD), F32)],
        [
            pltpu.VMEM((ROWS + 2 * HALO, D), F32),
            pltpu.VMEM((2, ROWS, D), BF16),
            pltpu.SemaphoreType.DMA((2,)),
        ],
        2 * WROWS * D * D,
        info,
        *in_hbm((tokens, cotangent)),
    )
    if direct:
        with_near, first, with_far, second, up_near, up_far = pl.pallas_call(
            prepare_kernel,
            out_shape=[
                jax.ShapeDtypeStruct((share, width + 2 * D), BF16),
                jax.ShapeDtypeStruct((share, width), BF16),
                jax.ShapeDtypeStruct((share, width + 2 * D), BF16),
                jax.ShapeDtypeStruct((2 * w_up.shape[0] + 5 * share, D), BF16),
                jax.ShapeDtypeStruct((2 * w_up.shape[0] + HALO, D), BF16),
                jax.ShapeDtypeStruct((2 * w_up.shape[0] + HALO, D), BF16),
            ],
            in_specs=[ANY] * 10,
            out_specs=[VMEM] * 6,
            scratch_shapes=[
                pltpu.VMEM((4, 1, share), BF16),
                pltpu.SemaphoreType.DMA((26,)),
            ],
            compiler_params=pltpu.CompilerParams(vmem_limit_bytes=LIMIT),
        )(
            *[
                far_core(a)
                for a in (tokens, cotangent, w_qkv, w_out, w_up, w_down.T)
                + tuple(v.reshape(1, -1) for v in vectors)
            ]
        )
        block = w_up.shape[0]
        own_x, own_y, near, middle, far, x, cot, cot_own, own = together(
            swap(second, "dp", 2),
            swap(second, "dp", 4),
            swap(with_near, "seq", 1),
            swap(first, "seq", 2),
            swap(with_far, "seq", 3),
            x,
            cot,
            cot_own,
            own,
        )
        column = jnp.stack([near[:, :width], middle, far[:, :width]])
        column, second = together(column, second)
        first_half = lax.all_gather(column, "dp", axis_index_groups=CHIPS)
        first_half, own_d, *rest = together(
            first_half,
            swap(second, "dp", 6),
            swap(up_near, "seq", 1),
            swap(second[: 2 * block], "seq", 2),
            swap(up_far, "seq", 3),
        )
        second_own = jnp.stack([second, own_x, own_y, own_d])
        near_cot, far_cot = rest[0], rest[2]
        rest = [rest[0][: 2 * block], rest[1], rest[2][: 2 * block]]
        rest = jnp.stack(rest)
        first_half, rest, second_own = together(first_half, rest, second_own)
        second_own = [second_own, *along_core([second_own])]
        first_all = [first_half, *along_core([first_half]), *second_own]
        second_plane = along_plane(rest)
    else:
        norms = jnp.pad(jnp.stack(vectors, axis=1), ((0, 0), (0, NORMS - 4)))
        first = jnp.concatenate([w_qkv, w_out, norms], axis=1)
        both = jnp.stack([tokens, cotangent])
        head, tail = both[:, :HALO], both[:, ROWS - HALO :]
        odd = lax.axis_index("seq") % 2 == 1
        first_all = [lax.all_gather(first, ("dp", "seq"), axis=0, tiled=True)]
        up_all = lax.all_gather(lax.all_gather(w_up, "dp", axis=0, tiled=True), "seq", axis=0)
        down_all = lax.all_gather(lax.all_gather(w_down.T, "dp", axis=0, tiled=True), "seq", axis=0)
        second_own = second_all = [up_all, down_all]
        from_left = lax.ppermute(tail, "seq", [(i, i + 1) for i in range(n_seq - 1)])
        from_right = lax.ppermute(head, "seq", [(i + 1, i) for i in range(n_seq - 1)])
        near, near_cot = jnp.where(odd, from_left, from_right)
        far, far_cot = jnp.where(odd, from_right, from_left)

    x, qkv, mixed, probs, w_all, norms_all = run_kernel(
        functools.partial(attention_kernel, direct),
        [
            shape((WROWS, D), BF16),
            shape((WROWS, 3 * D), BF16),
            shape((WROWS, D), BF16),
            shape((WROWS, D), BF16),
            shape((D, width), BF16),
            shape((8, D), F32),
        ],
        [
            pltpu.VMEM((ROWS + 2 * HALO, D), F32),
            pltpu.VMEM((3 * HALO, D), BF16),
            pltpu.VMEM((2, HALO, D), BF16),
            pltpu.SemaphoreType.DMA((6,)),
        ],
        2 * WROWS * D * 3 * D * 2,
        info,
        *in_hbm((tokens, near, far)),
        x,
        *first_all,
    )
    if direct:
        grads_shape = [shape((4, 2 * block, D), BF16)] * 2
    else:
        grads_shape = [shape((1, D, CHUNK), F32)] * 2
    *state, keep, send = run_kernel(
        functools.partial(feed_first_kernel, direct),
        [shape((WROWS, D), F32)] * 3
        + [shape((WROWS, D), BF16)] * 4
        + grads_shape,
        [
            pltpu.VMEM((1, D, CHUNK), BF16),
            pltpu.VMEM((1, D, CHUNK), BF16),
            pltpu.VMEM((ROWS + 2 * HALO, D), F32),
            pltpu.VMEM((WROWS, CHUNK), BF16),
            pltpu.VMEM((WROWS, CHUNK), BF16),
            pltpu.VMEM((3 * HALO, D), BF16),
            pltpu.VMEM((2, HALO, D), BF16),
            pltpu.SemaphoreType.DMA((4,)),
        ],
        2 * WROWS * D * (6 * CHUNK + D),
        info,
        *in_hbm((cotangent, near_cot, far_cot)),
        cot,
        cot_own,
        own,
        x,
        mixed,
        norms_all,
        w_all,
        *second_own,
    )
    if direct:
        *second_plane, total = together(*second_plane, state[1])
        state[1] = total
        second_plane = [rest, *second_plane]
        second_all = second_plane + along_core(second_plane)
        first_grads = [keep, send]
        extra = (CHUNKS - 1) * 2 * block
        grads_shape = [shape((4, extra, D), BF16)] * 2
        out_shape = [shape((4, n_seq * share, D), BF16)] * 2
    else:
        first_grads = [keep, send]
        grads_shape = [shape((CHUNKS - 1, D, CHUNK), F32)] * 2
        out_shape = [shape((D, D), F32)]
    middle, total, grad, normed, normed_own, cot, cot_own = state
    total, grad, *grads = run_kernel(
        functools.partial(feed_rest_kernel, direct),
        [shape((WROWS, D), F32)] * 2 + grads_shape,
        [
            pltpu.VMEM((CHUNKS - 1, D, CHUNK), BF16),
            pltpu.VMEM((CHUNKS - 1, D, CHUNK), BF16),
            pltpu.VMEM((D, D), F32),
            pltpu.VMEM((WROWS, CHUNK), BF16),
            pltpu.VMEM((WROWS, CHUNK), BF16),
        ],
        2 * WROWS * D * 18 * CHUNK,
        info,
        total,
        grad,
        normed,
        normed_own,
        cot,
        cot_own,
        *second_all,
    )
    if direct:
        total, *grads, from_first = together(total, *grads, *along_core([first_grads[1]]))
        from_core = [from_first, *along_core([grads[1]])]
    grad_middle, grad_mixed, grad_norms, *out_grads = run_kernel(
        functools.partial(feed_last_kernel, direct),
        [
            shape((WROWS, D), F32),
            shape((WROWS, D), BF16),
            shape((8, D), F32),
            *out_shape,
        ],
        [pltpu.VMEM((D, D), F32), pltpu.VMEM((WROWS, D), BF16)],
        2 * WROWS * D * 2 * D,
        info,
        middle,
        grad,
        cot,
        own,
        mixed,
        norms_all,
        w_all,
    )
    if direct:
        from_core = [*from_core, *along_core(out_grads[1:])]
        keeps, from_core = [first_grads[0], grads[0], out_grads[0]], together(*from_core)
        own_pair, to_near, pair, *low = add_chunks(keeps, from_core)
        to_near, *low, grad_mixed = together(to_near, *low, grad_mixed)
        parts = [swap(part, "dp", 2 * m + 2) for m, part in enumerate(low)]
        parts.append(swap(to_near, "seq", 1))
        grads_shape = [shape((4, n_seq, share, 3 * D + NORMS), BF16)] * 2
    else:
        grads_up, grads_down = [
            jnp.concatenate([a, b], axis=0) for a, b in zip(first_grads, grads)
        ]
        grad_up = lax.psum_scatter(grads_up, "seq", scatter_dimension=0)
        grad_up = lax.psum_scatter(grad_up, "dp", scatter_dimension=0, tiled=True)
        grad_down = lax.psum_scatter(grads_down, "seq", scatter_dimension=0)
        grad_down = lax.psum_scatter(grad_down, "dp", scatter_dimension=0, tiled=True).T
        grad_out = lax.psum_scatter(out_grads[0], ("dp", "seq"), scatter_dimension=0, tiled=True)
        grads_shape = [shape((D, 3 * D + NORMS), F32)]
    grad_tokens, *grads = run_kernel(
        functools.partial(back_kernel, direct),
        [shape((WROWS, D), F32), *grads_shape],
        [
            pltpu.VMEM((WROWS, D), BF16),
            pltpu.VMEM((WROWS, 3 * D), BF16),
            pltpu.VMEM((NORMS, D), F32),
            pltpu.VMEM((D, 3 * D + NORMS), F32),
        ],
        2 * WROWS * D * (6 * D + 3 * D),
        info,
        x,
        own,
        qkv,
        probs,
        grad_mixed,
        grad_middle,
        w_all,
        norms_all,
        grad_norms,
    )
    if direct:
        grad_tokens, *grads = together(grad_tokens, *grads)
    out, tokens_grad = [
        run_kernel(
            finish_rows_kernel,
            [jax.ShapeDtypeStruct((ROWS, D), BF16)],
            [pltpu.VMEM((ROWS + 2 * HALO, D), F32)],
            2 * WROWS * D * D,
            info,
            values,
        )[0]
        for values in (total, grad_tokens)
    ]
    if direct:
        keep, send, *parts, from_near = together(*grads, *parts)
        rows = 2 * block + share
        plan = [[(slice(None), (slice(k * rows, (k + 1) * rows),))] for k in range(2)]
        low = add(plan, [((rows, D), BF16)] * 2, pair, *parts)
        second_far, from_near_far = together(low[1], swap(low[0], "seq", 1))
        (second_far,) = add([[(slice(None), slice(None))]], [(low[1].shape, BF16)], second_far, from_near_far)
        second = [swap(second_far, "seq", 3)]
        (from_core,) = along_core([send])
        first_pair, *first_low = add_slots(keep, from_core)
        first = [swap(part, "dp", 2 * m + 2) for m, part in enumerate(first_low)]
        own_pair, *own_low = add_slots(own_pair, from_near)
        *first, second, own0, own1, own2, out, tokens_grad = together(
            *first, *second, *own_low, out, tokens_grad
        )
        everything = slice(None)
        slot = first_pair.shape[1:]
        first_own, to_near, to_far = add(
            [[(everything, 0)], [(0, 1), (1, 2)], [(everything, 3)]],
            [(slot, F32), ((2, *slot), BF16), (slot, F32)],
            first_pair,
            *first,
        )
        near_part = swap(to_near, "seq", 1)
        (far_low,) = small_call(far_kernel, [(slot, BF16)], to_far, near_part, flops=EARLY)
        far_part = swap(far_low, "seq", 3)
        own_parts = [swap(part, "dp", 2 * m + 2) for m, part in enumerate((own0, own1, own2))]
        shapes = [((block, D), F32)] * 2 + [((share, D), F32), ((share, 3 * D), F32)]
        shapes += [((1, share), F32)] * 4
        grad_up, grad_down, grad_out, w_qkv_grad, *norm_grads = small_call(
            finish_kernel,
            shapes,
            own_pair,
            first_own,
            *own_parts,
            second,
            near_part,
            far_part,
        )
        grad_down = grad_down.T
        norm_grads = [grad.reshape(share) for grad in norm_grads]
    else:
        first_sum = lax.psum_scatter(grads[0], ("dp", "seq"), scatter_dimension=0, tiled=True)
        w_qkv_grad = first_sum[:, : 3 * D]
        norm_grads = [first_sum[:, 3 * D + i] for i in range(4)]
    return (
        out,
        tokens_grad,
        w_qkv_grad,
        grad_out,
        grad_up,
        grad_down,
        *norm_grads,
    )


def solution(mesh):
    rows = P(("dp", "seq"), None)
    vector = P(("dp", "seq"))
    return jax.shard_map(
        per_device,
        mesh=mesh,
        in_specs=(
            rows,
            rows,
            rows,
            rows,
            P("dp", "seq"),
            P("seq", "dp"),
            vector,
            vector,
            vector,
            vector,
            P("dp", None),
            P("dp", None, None),
        ),
        out_specs=(
            rows,
            rows,
            rows,
            rows,
            P("dp", "seq"),
            P("seq", "dp"),
            vector,
            vector,
            vector,
            vector,
        ),
        check_vma=False,
    )
```

```python
import functools

import jax
import jax.numpy as jnp
from jax import lax
from jax.experimental import pallas as pl
from jax.experimental.pallas import tpu as pltpu
from jax.sharding import PartitionSpec as P

D = 512
HEADS = 16
HEAD_DIM = D // HEADS
FF = 2048
FREQ = 8
STEPS_DEV = 88
HALO = 4 * FREQ
ROWS = STEPS_DEV * FREQ
WIN = 4 * FREQ
WINDOWS = STEPS_DEV // 4 + 2
WROWS = WINDOWS * WIN
TILE = 768
QUAD = 128
NORMS = 128
CHUNK = 512
CHUNKS = FF // CHUNK
epsilon = 1e-06
F32 = jnp.float32
BF16 = jnp.bfloat16


def mm(left, right):
    return jnp.dot(left, right, preferred_element_type=F32)


def mm_right(left, right):
    return lax.dot_general(left, right, (((1,), (1,)), ((), ())), preferred_element_type=F32)


def mm_left(left, right):
    return lax.dot_general(left, right, (((0,), (0,)), ((), ())), preferred_element_type=F32)


def window_place(info, w):
    lead, mid, trail = info[0], info[1], info[2]
    seq = info[10]
    base = seq * STEPS_DEV
    n_lead = lead // 4 + 1
    n_mid = mid // 4 + 1
    index = jnp.where(seq == 0, 0, base // 4 + 1) + w
    in_mid = index >= n_lead
    in_trail = index >= n_lead + n_mid
    before = jnp.where(in_trail, n_lead + n_mid, jnp.where(in_mid, n_lead, 0))
    start = jnp.where(in_trail, lead + mid, jnp.where(in_mid, lead, 0))
    steps = jnp.where(in_trail, trail, jnp.where(in_mid, mid, lead))
    shift_time = jnp.where(in_trail, info[7], jnp.where(in_mid, info[5], info[3]))
    shift_freq = jnp.where(in_trail, info[8], jnp.where(in_mid, info[6], info[4]))
    first = start - 4 + shift_time + 4 * (index - before)
    here = first < base + STEPS_DEV
    low = jnp.clip(start - first, 0, 4)
    high = jnp.where(here, jnp.clip(start + steps - first, 0, 4), 0)
    own_low = jnp.clip(base - first, 0, 4)
    own_high = jnp.clip(base + STEPS_DEV - first, 0, 4)
    row = jnp.clip(first - base + 4, 0, STEPS_DEV + 4) * FREQ
    row = pl.multiple_of(row, FREQ)
    return (
        row,
        low * FREQ,
        high * FREQ,
        jnp.maximum(low, own_low) * FREQ,
        jnp.minimum(high, own_high) * FREQ,
        shift_freq,
    )


def window_at(w):
    return pl.ds(pl.multiple_of(w * WIN, WIN), WIN)


def tile_at(i):
    return pl.ds(pl.multiple_of(i * TILE, TILE), TILE)


def row_mask(low, high):
    index = lax.broadcasted_iota(jnp.int32, (WIN, 1), 0)
    return (index >= low) & (index < high)


def copy_all(pairs, sems, first=0):
    copies = [
        pltpu.make_async_copy(source, target, sems.at[first + i])
        for i, (source, target) in enumerate(pairs)
    ]
    for copy in copies:
        copy.start()
    return copies


def wait_all(copies):
    for copy in copies:
        copy.wait()


def edge_copies(rows, near, far, ext_low, halos):
    pairs = [
        (rows.at[0:HALO, :], ext_low.at[0:HALO, :]),
        (rows.at[ROWS - 2 * HALO :, :], ext_low.at[HALO:, :]),
    ]
    for i, parts in enumerate((near, far)):
        size = HALO // len(parts)
        pairs += [
            (part, halos.at[i, j * size : (j + 1) * size, :]) for j, part in enumerate(parts)
        ]
    return pairs


def pad_edges(info, ext, ext_low, halos):
    ext[HALO : 2 * HALO] = ext_low[0:HALO].astype(F32)
    ext[ROWS - HALO : ROWS + HALO] = ext_low[HALO:].astype(F32)
    odd = info[10] % 2 == 1
    for i, is_left in enumerate((odd, jnp.logical_not(odd))):
        at = pl.multiple_of(jnp.where(is_left, 0, HALO + ROWS), HALO)
        ext[pl.ds(at, HALO), :] = halos[i].astype(F32)


EDGES = (0, WINDOWS - 2, WINDOWS - 1)


def place_rows(info, w, ext, out):
    row, low, high, _, _, _ = window_place(info, w)
    values = jnp.where(row_mask(low, high), ext[pl.ds(row, WIN), :], 0.0)
    out[window_at(w), :] = values.astype(BF16)


def place_cotangent(info, w, ext, cot, cot_own):
    row, low, high, own_low, own_high, _ = window_place(info, w)
    values = ext[pl.ds(row, WIN), :]
    cot[window_at(w), :] = jnp.where(row_mask(low, high), values, 0.0).astype(BF16)
    cot_own[window_at(w), :] = jnp.where(row_mask(own_low, own_high), values, 0.0).astype(BF16)


def layout_kernel(info, tokens, cotangent, x_out, cot, cot_own, own, ext, stage, sems):
    copies = copy_all([(tokens, stage.at[0]), (cotangent, stage.at[1])], sems)
    for edge in (slice(0, HALO), slice(HALO + ROWS, 2 * HALO + ROWS)):
        ext[edge, :] = jnp.zeros((HALO, D), F32)
    copies[0].wait()
    ext[HALO : HALO + ROWS] = stage[0].astype(F32)

    def tokens_step(w, carry):
        place_rows(info, w, ext, x_out)
        return carry

    lax.fori_loop(0, WINDOWS, tokens_step, 0, unroll=4)
    copies[1].wait()
    ext[HALO : HALO + ROWS] = stage[1].astype(F32)

    def cotangent_step(w, carry):
        place_cotangent(info, w, ext, cot, cot_own)
        mask = row_mask(*window_place(info, w)[3:5])
        own[window_at(w), :] = jnp.where(mask, jnp.ones((WIN, QUAD), F32), 0.0)
        return carry

    lax.fori_loop(0, WINDOWS, cotangent_step, 0, unroll=4)


def normalized(values):
    mean = jnp.mean(values, axis=-1, keepdims=True)
    centered = values - mean
    variance = jnp.mean(centered * centered, axis=-1, keepdims=True)
    scale = lax.rsqrt(variance + epsilon)
    return centered * scale, scale


def norm_back(grad, unit, scale):
    mean_one = jnp.mean(grad, axis=-1, keepdims=True)
    mean_two = jnp.mean(grad * unit, axis=-1, keepdims=True)
    return scale * (grad - mean_one - unit * mean_two)


def head_masks():
    lane = lax.broadcasted_iota(jnp.int32, (1, QUAD), 1) // HEAD_DIM
    return [(lane == h).astype(BF16) for h in range(QUAD // HEAD_DIM)]


def spread(block, masks):
    return jnp.concatenate([block * mask for mask in masks], axis=0)


def gathered(product, lane):
    parts = [product[h * WIN : (h + 1) * WIN] for h in range(QUAD // HEAD_DIM)]
    return jnp.where(
        lane < 1, parts[0], jnp.where(lane < 2, parts[1], jnp.where(lane < 3, parts[2], parts[3]))
    )


def sum_kernel(plan, *refs):
    ins, outs = refs[: -len(plan)], refs[-len(plan) :]
    for out, pieces in zip(outs, plan):
        for target, source in pieces:
            value = ins[0][source].astype(F32)
            for part in ins[1:]:
                value = value + part[source].astype(F32)
            out[target] = value.astype(out.dtype)


def add(plan, shapes, *operands):
    return pl.pallas_call(
        functools.partial(sum_kernel, plan),
        out_shape=[jax.ShapeDtypeStruct(*s) for s in shapes],
        in_specs=[VMEM] * len(operands),
        out_specs=[VMEM] * len(shapes),
        compiler_params=pltpu.CompilerParams(vmem_limit_bytes=SMALL),
    )(*[near_core(a) for a in operands])


def small_call(body, shapes, *operands, flops=0):
    moved = sum(a.size * a.dtype.itemsize for a in operands)
    return pl.pallas_call(
        body,
        out_shape=[jax.ShapeDtypeStruct(*s) for s in shapes],
        in_specs=[VMEM] * len(operands),
        out_specs=[VMEM] * len(shapes),
        cost_estimate=pl.CostEstimate(flops=flops, bytes_accessed=moved, transcendentals=0),
        compiler_params=pltpu.CompilerParams(vmem_limit_bytes=SMALL),
    )(*[near_core(a) for a in operands])


def stack_kernel(*refs):
    *parts, out = refs
    for i, part in enumerate(parts):
        out[i] = part[:, 0 : out.shape[2]]


def chunks_kernel(keep_first, keep_rest, keep_out, first, rest, out, *refs):
    own, near, pair, *low = refs
    block, share = keep_first.shape[1], keep_out.shape[1] // CHUNKS

    def sums(slot, k):
        a, b, row = (keep_first, first, 0) if k == 0 else (keep_rest, rest, (k - 1) * block)
        rows, out_rows = slice(row, row + block), slice(share * k, share * (k + 1))
        return (
            a[slot, rows].astype(F32) + b[slot, rows].astype(F32),
            keep_out[slot, out_rows].astype(F32) + out[slot, out_rows].astype(F32),
        )

    for slot in range(4):
        for k in range(CHUNKS):
            if k < 2:
                target, row = (own, near)[k].at[slot], 0
            else:
                target, row = ([pair] + low)[slot], (k - 2) * (block + share)
            one, two = sums(slot, k)
            target[row : row + block, :] = one.astype(target.dtype)
            target[row + block : row + block + share, :] = two.astype(target.dtype)


def add_chunks(keeps, parts):
    rows = keeps[0].shape[1] + keeps[2].shape[1] // CHUNKS
    shapes = [((4, rows, D), F32), ((4, rows, D), BF16), ((2 * rows, D), F32)]
    shapes += [((2 * rows, D), BF16)] * 3
    return pl.pallas_call(
        chunks_kernel,
        out_shape=[jax.ShapeDtypeStruct(*s) for s in shapes],
        in_specs=[VMEM] * 6,
        out_specs=[VMEM] * 6,
        compiler_params=pltpu.CompilerParams(vmem_limit_bytes=SMALL),
    )(*[near_core(a) for a in (*keeps, *parts)])


def far_kernel(own, pair, out):
    out[...] = (own[...] + pair[1].astype(F32)).astype(BF16)


def finish_kernel(chunk, first, one, two, three, second, pair, far, *outs):
    total = chunk[...] + second[...].astype(F32)
    for part in (one, two, three):
        total = total + part[...].astype(F32)
    row = 0
    for out in outs[:3]:
        out[...] = total[row : row + out.shape[0]]
        row += out.shape[0]
    total = first[...] + (pair[0].astype(F32) + far[...].astype(F32))
    outs[3][...] = total[:, : 3 * D]
    rows = jnp.transpose(total[:, 3 * D :])
    for i, out in enumerate(outs[4:]):
        out[...] = rows[i : i + 1]


def add_slots(*operands):
    slot = operands[0].shape[1:]
    plan = [[(slice(None), i)] for i in range(4)]
    return add(plan, [(slot, F32)] + [(slot, BF16)] * 3, *operands)


def prepare_kernel(tokens, cotangent, w_qkv, w_out, w_up, w_down, *refs):
    norms, (with_near, first, with_far, second, up_near, up_far, vectors, sems) = refs[:4], refs[4:]
    share, width = first.shape
    block = w_up.shape[0]
    odd = lax.axis_index("seq") % 2
    pairs = [(norm, vectors.at[i]) for i, norm in enumerate(norms)]
    for target in (with_near, first, with_far):
        pairs += [(w_qkv, target.at[:, : 3 * D]), (w_out, target.at[:, 3 * D : 4 * D])]
    for target, up_target, is_head in ((with_near, up_near, odd), (with_far, up_far, 1 - odd)):
        start = pl.multiple_of((1 - is_head) * (ROWS - HALO), HALO)
        for j in range(2):
            at = width + j * D
            rows = pl.ds(start + j * (HALO // 2), HALO // 2)
            pairs.append((tokens.at[rows, :], target.at[:, at : at + D]))
        pairs.append((cotangent.at[pl.ds(start, HALO), :], up_target.at[2 * block :, :]))
    for target in (second, up_near, up_far):
        pairs += [(w_up, target.at[0:block]), (w_down, target.at[block : 2 * block])]
    first_row = 2 * block
    for i, source in enumerate([w_qkv.at[:, j * D : (j + 1) * D] for j in range(3)] + [w_out]):
        pairs.append((source, second.at[first_row + share * i : first_row + share * (i + 1), :]))
    copies = copy_all(pairs, sems)
    wait_all(copies[: len(norms)])
    columns = jnp.concatenate(
        [vectors[i].astype(F32) for i in range(4)] + [jnp.zeros((NORMS - 4, share), F32)], axis=0
    )
    columns = jnp.transpose(columns).astype(BF16)
    for target in (with_near, first, with_far):
        target[:, 4 * D : width] = columns
    second[first_row + 4 * share :, :] = jnp.concatenate([columns] * (D // NORMS), axis=1)
    wait_all(copies[len(norms) :])


def attention_kernel(direct, info, rows, near, far, x_in, *refs):
    pieces, refs = (refs[:4], refs[4:]) if direct else (refs[:1], refs[1:])
    x_out, qkv_out, mixed_out, probs_out, w_out, norms_out, ext, edges, halos, sems = refs
    width = w_out.shape[1]
    near, far = [
        [a.at[:, width + j * D : width + (j + 1) * D] for j in range(2)] if direct else [a]
        for a in (near, far)
    ]
    edge_copy = copy_all(edge_copies(rows, near, far, edges, halos), sems)
    x_out[...] = x_in[...]
    if direct:
        count, share = pieces[0].shape[1] + 1, pieces[0].shape[2]
        for core, piece in enumerate(pieces[:2]):
            for chip in range(4):
                for k in range(1, count):
                    owner = (2 * chip + (info[9] % 2 ^ core)) * count + (info[10] ^ k)
                    at = pl.multiple_of(owner * share, share)
                    w_out[pl.ds(at, share), :] = piece[chip, k - 1]
        for i, partner in enumerate(ORDER):
            owner = (info[9] ^ partner) * count + info[10]
            at = pl.ds(pl.multiple_of(owner * share, share), share)
            for j in range(5):
                cols = min(D, width - j * D)
                row = D // 4 + j * share
                part = pieces[2 + i // 4][i % 4, row : row + share, 0:cols]
                w_out[at, j * D : j * D + cols] = part
    else:
        w_out[...] = pieces[0][...]
    wait_all(edge_copy)
    pad_edges(info, ext, edges, halos)
    for w in EDGES:
        place_rows(info, w, ext, x_out)
    norms_out[...] = jnp.transpose(w_out[:, 4 * D :].astype(F32))[:8]
    gain, shift = norms_out[0:1], norms_out[1:2]

    def project(i, carry):
        at = tile_at(i)
        unit, _ = normalized(x_out[at, :].astype(F32))
        low = (unit * gain + shift).astype(BF16)
        for part in range(3):
            cols = slice(part * D, (part + 1) * D)
            qkv_out[at, cols] = mm(low, w_out[:, cols]).astype(BF16)
        return carry

    lax.fori_loop(0, WROWS // TILE, project, 0)
    masks = head_masks()
    lane = lax.broadcasted_iota(jnp.int32, (1, QUAD), 1) // HEAD_DIM
    key_row = lax.broadcasted_iota(jnp.int32, (WIN, QUAD), 0)
    query_row = lax.broadcasted_iota(jnp.int32, (WIN, QUAD), 1) % WIN
    key_freq, query_freq = key_row % FREQ, query_row % FREQ

    def attend(w, carry):
        _, low, high, _, _, shift_freq = window_place(info, w)
        at = pl.ds(pl.multiple_of(w * WIN, WIN), WIN)
        key_group = (key_freq + 4 - shift_freq) >> 2
        query_group = (query_freq + 4 - shift_freq) >> 2
        allowed = (key_group == query_group) & (key_row >= low) & (key_row < high)
        quads = range(D // QUAD)
        raw = []
        for quad in quads:
            query = qkv_out[at, quad * QUAD : (quad + 1) * QUAD]
            key = qkv_out[at, D + quad * QUAD : D + (quad + 1) * QUAD]
            raw.append(mm_right(key, spread(query, masks)))
        scores = [jnp.where(allowed, r * HEAD_DIM**-0.5, -1e30) for r in raw]
        weights = [jnp.exp(s - jnp.max(s, axis=0, keepdims=True)) for s in scores]
        probs = [(p / jnp.sum(p, axis=0, keepdims=True)).astype(BF16) for p in weights]
        products = []
        for quad in quads:
            probs_out[at, quad * QUAD : (quad + 1) * QUAD] = probs[quad]
            value = qkv_out[at, 2 * D + quad * QUAD : 2 * D + (quad + 1) * QUAD]
            products.append(mm_left(probs[quad], value))
        for quad in quads:
            mixed = gathered(products[quad], lane).astype(BF16)
            mixed_out[at, quad * QUAD : (quad + 1) * QUAD] = mixed
        return carry

    lax.fori_loop(0, WINDOWS, attend, 0, unroll=12)


def gelu_parts(values):
    half_exp = jnp.exp(-0.5 * values * values)
    t = 1.0 / (1.0 + (0.3275911 * 0.7071067811865476) * jnp.abs(values))
    poly = t * (
        0.5 * 0.254829592
        + t
        * (
            0.5 * -0.284496736
            + t * (0.5 * 1.421413741 + t * (0.5 * -1.453152027 + t * (0.5 * 1.061405429)))
        )
    )
    tail = poly * half_exp
    return jnp.where(values >= 0, 1.0 - tail, tail), half_exp * 0.3989422804014327


def place_feed(info, pieces, up, down):
    block = D // 8
    for piece, partner in zip(pieces, ORDER):
        at = pl.ds(pl.multiple_of((info[9] ^ partner) * block, block), block)
        for c in range(up.shape[0]):
            up[c, at, :] = piece[c, 0:block, :]
            down[c, at, :] = piece[c, block : 2 * block, :]


def feed_rows(at, up, down, normed, cot, hidden, pre):
    values = mm(normed[at, :], up)
    grad_hidden = mm(cot[at, :], down)
    below, density = gelu_parts(values)
    hidden_low = (values * below).astype(BF16)
    grad_low = (grad_hidden * (below + values * density)).astype(BF16)
    hidden[at, :] = hidden_low
    pre[at, :] = grad_low
    return mm_right(hidden_low, down), mm_right(grad_low, up)


def feed_grads(direct, info, row, normed_own, cot_own, hidden, pre, space, refs):
    block = D // 8
    for i, product in enumerate(((normed_own, pre), (cot_own, hidden))):
        grad = mm_left(product[0][...], product[1][...])
        if not direct:
            refs[i][row // (2 * block)] = grad
            continue
        space[0:D, :] = grad
        for partner in range(8):
            at = pl.multiple_of((info[9] ^ partner) * block, block)
            first = row + i * block
            refs[partner & 1][partner >> 1, first : first + block, :] = space[
                pl.ds(at, block), :
            ].astype(BF16)


def feed_first_kernel(
    direct, info, rows, near, far, cot_in, cot_own_in, own, x_in, mixed_in, norms, w_all, *refs
):
    pieces, refs = refs[:2], refs[2:]
    middle, total, grad, normed, normed_own, cot, cot_own = refs[:7]
    grads, (up, down, ext, hidden, pre, edges, halos, sems) = refs[7:9], refs[9:]
    near, far = [[a.at[a.shape[0] - HALO :, :]] for a in (near, far)]
    edge_copy = copy_all(edge_copies(rows, near, far, edges, halos), sems)
    cot[...], cot_own[...] = cot_in[...], cot_own_in[...]
    if direct:
        own_pieces = [piece.at[m : m + 1] for piece in pieces for m in range(4)]
        place_feed(info, own_pieces, up, down)
    else:
        up[...], down[...] = pieces[0][0:1], pieces[1][0:1]
    wait_all(edge_copy)
    pad_edges(info, ext, edges, halos)
    for w in EDGES:
        place_cotangent(info, w, ext, cot, cot_own)
    gain, shift = norms[2:3], norms[3:4]

    def before(i, carry):
        at = tile_at(i)
        values = x_in[at, :].astype(F32) + mm(mixed_in[at, :], w_all[:, 3 * D : 4 * D])
        middle[at, :] = values
        unit, _ = normalized(values)
        low = unit * gain + shift
        normed[at, :] = low.astype(BF16)
        normed_own[at, :] = (low * own[at, 0:1]).astype(BF16)
        return carry

    lax.fori_loop(0, WROWS // TILE, before, 0)
    for i in range(WROWS // TILE):
        at = slice(i * TILE, (i + 1) * TILE)
        branch, back = feed_rows(at, up[0], down[0], normed, cot, hidden, pre)
        total[at, :] = middle[at, :] + branch
        grad[at, :] = back
    feed_grads(direct, info, 0, normed_own, cot_own, hidden, pre, ext, grads)


def feed_rest_kernel(direct, info, total_in, grad_in, normed, normed_own, cot, cot_own, *refs):
    pieces, refs = (refs[:8], refs[8:]) if direct else (refs[:2], refs[2:])
    total, grad, *grads, up, down, ext, hidden, pre = refs
    if direct:
        place_feed(info, pieces, up, down)
    else:
        up[...], down[...] = pieces[0][1:CHUNKS], pieces[1][1:CHUNKS]
    for c in range(CHUNKS - 1):
        for i in range(WROWS // TILE):
            at = slice(i * TILE, (i + 1) * TILE)
            branch, back = feed_rows(at, up[c], down[c], normed, cot, hidden, pre)
            total[at, :] = (total if c else total_in)[at, :] + branch
            grad[at, :] = (grad if c else grad_in)[at, :] + back
        feed_grads(direct, info, c * (D // 4), normed_own, cot_own, hidden, pre, ext, grads)


def feed_last_kernel(direct, info, middle, grad, cot, own, mixed_in, norms, w_all, *refs):
    grad_middle, grad_norms, *grads, ext, grad_own = refs
    gain = norms[2:3]
    grad_norms[...] = jnp.zeros(grad_norms.shape, F32)
    for i in range(WROWS // TILE):
        at = slice(i * TILE, (i + 1) * TILE)
        unit, scale = normalized(middle[at, :])
        part = grad[at, :]
        masked = part * own[at, 0:1]
        grad_norms[0:1] += jnp.sum(masked * unit, axis=0, keepdims=True)
        grad_norms[1:2] += jnp.sum(masked, axis=0, keepdims=True)
        result = cot[at, :].astype(F32) + norm_back(part * gain, unit, scale)
        grad_middle[at, :] = result
        grad_own[at, :] = (result * own[at, 0:1]).astype(BF16)
    grad_out = mm_left(mixed_in[...], grad_own[...])
    if direct:
        ext[0:D, :] = grad_out
        share = grads[0].shape[1] // CHUNKS
        for partner in range(8):
            for k in range(CHUNKS):
                owner = (info[9] ^ partner) * CHUNKS + (info[10] ^ k)
                row = pl.multiple_of(owner * share, share)
                grads[partner & 1][partner >> 1, share * k : share * (k + 1), :] = ext[
                    pl.ds(row, share), :
                ].astype(BF16)
    else:
        grads[0][...] = grad_out


def finish_rows_kernel(info, values, out, ext):
    unplace(info, values, ext, out)


def mixed_kernel(info, grad_middle, w_all, grad_mixed):
    low = grad_middle[...].astype(BF16)
    grad_mixed[...] = mm_right(low, w_all[:, 3 * D : 4 * D]).astype(BF16)


def unplace(info, values, ext, out):
    def back(w, carry):
        row, low, high, _, _, _ = window_place(info, w)
        at = pl.ds(pl.multiple_of(w * WIN, WIN), WIN)
        place = pl.ds(row, WIN)
        ext[place, :] = jnp.where(row_mask(low, high), values[at, :], ext[place, :])
        return carry

    lax.fori_loop(0, WINDOWS, back, 0, unroll=4)
    out[...] = ext[HALO : HALO + ROWS].astype(BF16)


def back_kernel(
    direct, info, x_in, own, qkv, probs_in, grad_mixed, grad_middle, w_qkv, norms, grad_norms, *refs
):
    grad_tokens, refs = refs[0], refs[1:]
    if direct:
        (keep, send), refs = refs[:2], refs[2:]
    else:
        w_grad, refs = refs[0], refs[1:]
    normed, grad_qkv, gains, grad_w = refs
    masks = head_masks()
    lane = lax.broadcasted_iota(jnp.int32, (1, QUAD), 1) // HEAD_DIM

    def attend_back(w, carry):
        at = window_at(w)
        quads = range(D // QUAD)
        cols = [slice(quad * QUAD, (quad + 1) * QUAD) for quad in quads]
        cols_key = [slice(D + quad * QUAD, D + (quad + 1) * QUAD) for quad in quads]
        cols_value = [slice(2 * D + quad * QUAD, 2 * D + (quad + 1) * QUAD) for quad in quads]
        grad_out = [spread(grad_mixed[at, c], masks) for c in cols]
        grad_probs = [mm_right(qkv[at, c], g) for c, g in zip(cols_value, grad_out)]
        low = [probs_in[at, c] for c in cols]
        probs = [p.astype(F32) for p in low]
        delta = [jnp.sum(p * g, axis=0, keepdims=True) for p, g in zip(probs, grad_probs)]
        grad_scores = [
            (p * (g - d) * HEAD_DIM**-0.5).astype(BF16)
            for p, g, d in zip(probs, grad_probs, delta)
        ]
        grad_value = [mm(p, g) for p, g in zip(low, grad_out)]
        grad_query = [mm_left(g, qkv[at, c]) for g, c in zip(grad_scores, cols_key)]
        grad_key = [mm(g, spread(qkv[at, c], masks)) for g, c in zip(grad_scores, cols)]
        for quad in quads:
            grad_qkv[at, cols_value[quad]] = grad_value[quad].astype(BF16)
            grad_qkv[at, cols_key[quad]] = grad_key[quad].astype(BF16)
            grad_qkv[at, cols[quad]] = gathered(grad_query[quad], lane).astype(BF16)
        return carry

    lax.fori_loop(0, WINDOWS, attend_back, 0, unroll=12)
    gain, shift = norms[0:1], norms[1:2]
    gains[...] = jnp.zeros(gains.shape, F32)

    def after(i, carry):
        at = tile_at(i)
        unit, scale = normalized(x_in[at, :].astype(F32))
        mask = own[at, 0:1]
        normed[at, :] = ((unit * gain + shift) * mask).astype(BF16)
        part = mm_right(grad_qkv[at, :], w_qkv[:, : 3 * D])
        masked = part * mask
        gains[0:1] += jnp.sum(masked * unit, axis=0, keepdims=True)
        gains[1:2] += jnp.sum(masked, axis=0, keepdims=True)
        grad_tokens[at, :] = grad_middle[at, :] + norm_back(part * gain, unit, scale)
        return carry

    lax.fori_loop(0, WROWS // TILE, after, 0)
    gains[2:4] = grad_norms[0:2]
    for part in range(3):
        cols = slice(part * D, (part + 1) * D)
        grad_w[:, cols] = mm_left(normed[...], grad_qkv[:, cols])
    grad_w[:, 3 * D :] = jnp.transpose(gains[...])
    if direct:
        count = keep.shape[1]
        for partner in range(8):
            target = send if partner & 1 else keep
            for k in range(count):
                row = pl.multiple_of(((info[9] ^ partner) * count + (info[10] ^ k)) * 16, 16)
                target[partner >> 1, k] = grad_w[pl.ds(row, 16), :].astype(BF16)
    else:
        w_grad[...] = grad_w[...]


ORDER = (0, 2, 4, 6, 1, 3, 5, 7)
CHIPS = [[0, 2, 4, 6], [1, 3, 5, 7]]
LIMIT = 20 * 1024 * 1024
SMALL = 8 * 1024 * 1024
EARLY = 4 * 10**9
SMEM = pl.BlockSpec(memory_space=pltpu.SMEM)
VMEM = pl.BlockSpec(memory_space=pltpu.VMEM)
ANY = pl.BlockSpec(memory_space=pl.ANY)


def near_core(array):
    return pltpu.with_memory_space_constraint(array, pltpu.VMEM)


def far_core(array):
    return pltpu.with_memory_space_constraint(array, pltpu.HBM)


def run_kernel(body, out_shape, scratch, flops, info, *operands):
    specs = [ANY if isinstance(a, list) else VMEM for a in operands]
    operands = [a[0] if isinstance(a, list) else near_core(a) for a in operands]
    moved = sum(a.size * a.dtype.itemsize for a in operands)
    return pl.pallas_call(
        body,
        out_shape=out_shape,
        in_specs=[SMEM] + specs,
        out_specs=[VMEM] * len(out_shape),
        scratch_shapes=scratch,
        cost_estimate=pl.CostEstimate(
            flops=flops, bytes_accessed=moved, transcendentals=flops // 1024
        ),
        compiler_params=pltpu.CompilerParams(vmem_limit_bytes=LIMIT),
    )(info, *operands)


def swap(array, axis, bit):
    return lax.ppermute(array, axis, [(i, i ^ bit) for i in range(lax.axis_size(axis))])


def together(*values):
    return lax.optimization_barrier(values)


def along_seq(shard):
    return [swap(shard, "seq", k) for k in (1, 2, 3)]


def along_plane(column):
    return [swap(column, "dp", partner) for partner in (2, 4, 6)]


def along_core(pieces):
    return [swap(piece, "dp", 1) for piece in pieces]


def add_parts(own, parts):
    return own.astype(F32) + sum(part.astype(F32) for part in parts)


def shape(dims, kind):
    return pltpu.VMEM(dims, kind)


def per_device(
    tokens,
    cotangent,
    w_qkv,
    w_out,
    w_up,
    w_down,
    norm1_gain,
    norm1_shift,
    norm2_gain,
    norm2_shift,
    clip_steps,
    window_shifts,
):
    n_dp, n_seq = lax.axis_size("dp"), lax.axis_size("seq")
    share = w_qkv.shape[0]
    direct = n_dp == 8 and share % 16 == 0
    info = jnp.concatenate(
        [
            clip_steps.reshape(3),
            window_shifts.reshape(6),
            lax.axis_index("dp").reshape(1).astype(jnp.int32),
            lax.axis_index("seq").reshape(1).astype(jnp.int32),
        ]
    )
    width = 4 * D + NORMS
    vectors = (norm1_gain, norm1_shift, norm2_gain, norm2_shift)

    def in_hbm(arrays):
        return [[a] for a in arrays]

    x, cot, cot_own, own = run_kernel(
        layout_kernel,
        [shape((WROWS, D), BF16)] * 3 + [shape((WROWS, QUAD), F32)],
        [
            pltpu.VMEM((ROWS + 2 * HALO, D), F32),
            pltpu.VMEM((2, ROWS, D), BF16),
            pltpu.SemaphoreType.DMA((2,)),
        ],
        2 * WROWS * D * D,
        info,
        *in_hbm((tokens, cotangent)),
    )
    if direct:
        with_near, first, with_far, second, up_near, up_far = pl.pallas_call(
            prepare_kernel,
            out_shape=[
                jax.ShapeDtypeStruct((share, width + 2 * D), BF16),
                jax.ShapeDtypeStruct((share, width), BF16),
                jax.ShapeDtypeStruct((share, width + 2 * D), BF16),
                jax.ShapeDtypeStruct((2 * w_up.shape[0] + 5 * share, D), BF16),
                jax.ShapeDtypeStruct((2 * w_up.shape[0] + HALO, D), BF16),
                jax.ShapeDtypeStruct((2 * w_up.shape[0] + HALO, D), BF16),
            ],
            in_specs=[ANY] * 10,
            out_specs=[VMEM] * 6,
            scratch_shapes=[
                pltpu.VMEM((4, 1, share), BF16),
                pltpu.SemaphoreType.DMA((26,)),
            ],
            compiler_params=pltpu.CompilerParams(vmem_limit_bytes=LIMIT),
        )(
            *[
                far_core(a)
                for a in (tokens, cotangent, w_qkv, w_out, w_up, w_down.T)
                + tuple(v.reshape(1, -1) for v in vectors)
            ]
        )
        block = w_up.shape[0]
        own_x, own_y, near, middle, far, x, cot, cot_own, own = together(
            swap(second, "dp", 2),
            swap(second, "dp", 4),
            swap(with_near, "seq", 1),
            swap(first, "seq", 2),
            swap(with_far, "seq", 3),
            x,
            cot,
            cot_own,
            own,
        )
        column = jnp.stack([near[:, :width], middle, far[:, :width]])
        column, second = together(column, second)
        first_half = lax.all_gather(column, "dp", axis_index_groups=CHIPS)
        first_half, own_d, *rest = together(
            first_half,
            swap(second, "dp", 6),
            swap(up_near, "seq", 1),
            swap(second[: 2 * block], "seq", 2),
            swap(up_far, "seq", 3),
        )
        second_own = jnp.stack([second, own_x, own_y, own_d])
        near_cot, far_cot = rest[0], rest[2]
        rest = [rest[0][: 2 * block], rest[1], rest[2][: 2 * block]]
        rest = jnp.stack(rest)
        first_half, rest, second_own = together(first_half, rest, second_own)
        second_own = [second_own, *along_core([second_own])]
        first_all = [first_half, *along_core([first_half]), *second_own]
        second_plane = along_plane(rest)
    else:
        norms = jnp.pad(jnp.stack(vectors, axis=1), ((0, 0), (0, NORMS - 4)))
        first = jnp.concatenate([w_qkv, w_out, norms], axis=1)
        both = jnp.stack([tokens, cotangent])
        head, tail = both[:, :HALO], both[:, ROWS - HALO :]
        odd = lax.axis_index("seq") % 2 == 1
        first_all = [lax.all_gather(first, ("dp", "seq"), axis=0, tiled=True)]
        up_all = lax.all_gather(lax.all_gather(w_up, "dp", axis=0, tiled=True), "seq", axis=0)
        down_all = lax.all_gather(lax.all_gather(w_down.T, "dp", axis=0, tiled=True), "seq", axis=0)
        second_own = second_all = [up_all, down_all]
        from_left = lax.ppermute(tail, "seq", [(i, i + 1) for i in range(n_seq - 1)])
        from_right = lax.ppermute(head, "seq", [(i + 1, i) for i in range(n_seq - 1)])
        near, near_cot = jnp.where(odd, from_left, from_right)
        far, far_cot = jnp.where(odd, from_right, from_left)

    x, qkv, mixed, probs, w_all, norms_all = run_kernel(
        functools.partial(attention_kernel, direct),
        [
            shape((WROWS, D), BF16),
            shape((WROWS, 3 * D), BF16),
            shape((WROWS, D), BF16),
            shape((WROWS, D), BF16),
            shape((D, width), BF16),
            shape((8, D), F32),
        ],
        [
            pltpu.VMEM((ROWS + 2 * HALO, D), F32),
            pltpu.VMEM((3 * HALO, D), BF16),
            pltpu.VMEM((2, HALO, D), BF16),
            pltpu.SemaphoreType.DMA((6,)),
        ],
        2 * WROWS * D * 3 * D * 2,
        info,
        *in_hbm((tokens, near, far)),
        x,
        *first_all,
    )
    if direct:
        grads_shape = [shape((4, 2 * block, D), BF16)] * 2
    else:
        grads_shape = [shape((1, D, CHUNK), F32)] * 2
    *state, keep, send = run_kernel(
        functools.partial(feed_first_kernel, direct),
        [shape((WROWS, D), F32)] * 3
        + [shape((WROWS, D), BF16)] * 4
        + grads_shape,
        [
            pltpu.VMEM((1, D, CHUNK), BF16),
            pltpu.VMEM((1, D, CHUNK), BF16),
            pltpu.VMEM((ROWS + 2 * HALO, D), F32),
            pltpu.VMEM((WROWS, CHUNK), BF16),
            pltpu.VMEM((WROWS, CHUNK), BF16),
            pltpu.VMEM((3 * HALO, D), BF16),
            pltpu.VMEM((2, HALO, D), BF16),
            pltpu.SemaphoreType.DMA((4,)),
        ],
        2 * WROWS * D * (6 * CHUNK + D),
        info,
        *in_hbm((cotangent, near_cot, far_cot)),
        cot,
        cot_own,
        own,
        x,
        mixed,
        norms_all,
        w_all,
        *second_own,
    )
    if direct:
        *second_plane, total = together(*second_plane, state[1])
        state[1] = total
        second_plane = [rest, *second_plane]
        second_all = second_plane + along_core(second_plane)
        first_grads = [keep, send]
        extra = (CHUNKS - 1) * 2 * block
        grads_shape = [shape((4, extra, D), BF16)] * 2
        out_shape = [shape((4, n_seq * share, D), BF16)] * 2
    else:
        first_grads = [keep, send]
        grads_shape = [shape((CHUNKS - 1, D, CHUNK), F32)] * 2
        out_shape = [shape((D, D), F32)]
    middle, total, grad, normed, normed_own, cot, cot_own = state
    total, grad, *grads = run_kernel(
        functools.partial(feed_rest_kernel, direct),
        [shape((WROWS, D), F32)] * 2 + grads_shape,
        [
            pltpu.VMEM((CHUNKS - 1, D, CHUNK), BF16),
            pltpu.VMEM((CHUNKS - 1, D, CHUNK), BF16),
            pltpu.VMEM((D, D), F32),
            pltpu.VMEM((WROWS, CHUNK), BF16),
            pltpu.VMEM((WROWS, CHUNK), BF16),
        ],
        2 * WROWS * D * 18 * CHUNK,
        info,
        total,
        grad,
        normed,
        normed_own,
        cot,
        cot_own,
        *second_all,
    )
    if direct:
        total, *grads, from_first = together(total, *grads, *along_core([first_grads[1]]))
        from_core = [from_first, *along_core([grads[1]])]
    grad_middle, grad_norms, *out_grads = run_kernel(
        functools.partial(feed_last_kernel, direct),
        [
            shape((WROWS, D), F32),
            shape((8, D), F32),
            *out_shape,
        ],
        [pltpu.VMEM((D, D), F32), pltpu.VMEM((WROWS, D), BF16)],
        2 * WROWS * D * 2 * D,
        info,
        middle,
        grad,
        cot,
        own,
        mixed,
        norms_all,
        w_all,
    )
    (grad_mixed,) = run_kernel(
        mixed_kernel,
        [shape((WROWS, D), BF16)],
        [],
        2 * WROWS * D * D,
        info,
        grad_middle,
        w_all,
    )
    if direct:
        from_core = [*from_core, *along_core(out_grads[1:])]
        *from_core, grad_mixed = together(*from_core, grad_mixed)
        keeps, from_core = [first_grads[0], grads[0], out_grads[0]], together(*from_core)
        own_pair, to_near, pair, *low = add_chunks(keeps, from_core)
        to_near, *low, grad_mixed = together(to_near, *low, grad_mixed)
        parts = [swap(part, "dp", 2 * m + 2) for m, part in enumerate(low)]
        parts.append(swap(to_near, "seq", 1))
        grads_shape = [shape((4, n_seq, share, 3 * D + NORMS), BF16)] * 2
    else:
        grads_up, grads_down = [
            jnp.concatenate([a, b], axis=0) for a, b in zip(first_grads, grads)
        ]
        grad_up = lax.psum_scatter(grads_up, "seq", scatter_dimension=0)
        grad_up = lax.psum_scatter(grad_up, "dp", scatter_dimension=0, tiled=True)
        grad_down = lax.psum_scatter(grads_down, "seq", scatter_dimension=0)
        grad_down = lax.psum_scatter(grad_down, "dp", scatter_dimension=0, tiled=True).T
        grad_out = lax.psum_scatter(out_grads[0], ("dp", "seq"), scatter_dimension=0, tiled=True)
        grads_shape = [shape((D, 3 * D + NORMS), F32)]
    grad_tokens, *grads = run_kernel(
        functools.partial(back_kernel, direct),
        [shape((WROWS, D), F32), *grads_shape],
        [
            pltpu.VMEM((WROWS, D), BF16),
            pltpu.VMEM((WROWS, 3 * D), BF16),
            pltpu.VMEM((NORMS, D), F32),
            pltpu.VMEM((D, 3 * D + NORMS), F32),
        ],
        2 * WROWS * D * (6 * D + 3 * D),
        info,
        x,
        own,
        qkv,
        probs,
        grad_mixed,
        grad_middle,
        w_all,
        norms_all,
        grad_norms,
    )
    if direct:
        grad_tokens, *grads = together(grad_tokens, *grads)
    out, tokens_grad = [
        run_kernel(
            finish_rows_kernel,
            [jax.ShapeDtypeStruct((ROWS, D), BF16)],
            [pltpu.VMEM((ROWS + 2 * HALO, D), F32)],
            2 * WROWS * D * D,
            info,
            values,
        )[0]
        for values in (total, grad_tokens)
    ]
    if direct:
        keep, send, *parts, from_near = together(*grads, *parts)
        rows = 2 * block + share
        plan = [[(slice(None), (slice(k * rows, (k + 1) * rows),))] for k in range(2)]
        low = add(plan, [((rows, D), BF16)] * 2, pair, *parts)
        second_far, from_near_far = together(low[1], swap(low[0], "seq", 1))
        (second_far,) = add([[(slice(None), slice(None))]], [(low[1].shape, BF16)], second_far, from_near_far)
        second = [swap(second_far, "seq", 3)]
        (from_core,) = along_core([send])
        first_pair, *first_low = add_slots(keep, from_core)
        first = [swap(part, "dp", 2 * m + 2) for m, part in enumerate(first_low)]
        own_pair, *own_low = add_slots(own_pair, from_near)
        *first, second, own0, own1, own2, out, tokens_grad = together(
            *first, *second, *own_low, out, tokens_grad
        )
        everything = slice(None)
        slot = first_pair.shape[1:]
        first_own, to_near, to_far = add(
            [[(everything, 0)], [(0, 1), (1, 2)], [(everything, 3)]],
            [(slot, F32), ((2, *slot), BF16), (slot, F32)],
            first_pair,
            *first,
        )
        near_part = swap(to_near, "seq", 1)
        (far_low,) = small_call(far_kernel, [(slot, BF16)], to_far, near_part, flops=EARLY)
        far_part = swap(far_low, "seq", 3)
        own_parts = [swap(part, "dp", 2 * m + 2) for m, part in enumerate((own0, own1, own2))]
        shapes = [((block, D), F32)] * 2 + [((share, D), F32), ((share, 3 * D), F32)]
        shapes += [((1, share), F32)] * 4
        grad_up, grad_down, grad_out, w_qkv_grad, *norm_grads = small_call(
            finish_kernel,
            shapes,
            own_pair,
            first_own,
            *own_parts,
            second,
            near_part,
            far_part,
        )
        grad_down = grad_down.T
        norm_grads = [grad.reshape(share) for grad in norm_grads]
    else:
        first_sum = lax.psum_scatter(grads[0], ("dp", "seq"), scatter_dimension=0, tiled=True)
        w_qkv_grad = first_sum[:, : 3 * D]
        norm_grads = [first_sum[:, 3 * D + i] for i in range(4)]
    return (
        out,
        tokens_grad,
        w_qkv_grad,
        grad_out,
        grad_up,
        grad_down,
        *norm_grads,
    )


def solution(mesh):
    rows = P(("dp", "seq"), None)
    vector = P(("dp", "seq"))
    return jax.shard_map(
        per_device,
        mesh=mesh,
        in_specs=(
            rows,
            rows,
            rows,
            rows,
            P("dp", "seq"),
            P("seq", "dp"),
            vector,
            vector,
            vector,
            vector,
            P("dp", None),
            P("dp", None, None),
        ),
        out_specs=(
            rows,
            rows,
            rows,
            rows,
            P("dp", "seq"),
            P("seq", "dp"),
            vector,
            vector,
            vector,
            vector,
        ),
        check_vma=False,
    )
```
